32 devices in a mesh: seq: 8 (over z, x), mp: 4 (over y, core).
Axes of the slice: x: 2, y: 2, z: 4, core: 2. Of those that a mesh axis runs over, the one named last changes fastest.
Arguments:
- byte_input: bfloat16 [4096, 1024], P('seq'), may hold values from -6 to 6
- seq_lengths: int32 [6], replicated, may hold values from 1 to 450, as said below
- cotangent: float32 [4096, 1024], P('seq'), may hold values from -6 to 6
- gain_global: float32 [1024], replicated, may hold values from 0.1 to 1.9
- patch_in: bfloat16 [8192, 1024], P(('mp', 'seq')), may hold values from -0.0625 to 0.0625
- mixer_gate: bfloat16 [1024, 2048], P('seq', 'mp'), may hold values from -0.1875 to 0.1875
- mixer_input: bfloat16 [1024, 2048], P('seq', 'mp'), may hold values from -0.1875 to 0.1875
- mixer_state: bfloat16 [1024, 256], P('seq'), may hold values from -0.1875 to 0.1875
- mixer_step: bfloat16 [1024, 32], P('seq', 'mp'), may hold values from -0.1875 to 0.1875
- conv_input: float32 [4, 2048], P(None, 'mp'), may hold values from -3 to 3
- conv_state: float32 [4, 256], replicated, may hold values from -3 to 3
- step_bias: float32 [32], P('mp'), may hold values from -5 to -1
- decay_log: float32 [32], P('mp'), may hold values from -4.6 to 0.7
- skip_gain: float32 [32], P('mp'), may hold values from 0.5 to 1.5
- gain_mixer: float32 [2048], P('mp'), may hold values from 0.1 to 1.9
- mixer_out: bfloat16 [2048, 1024], P(('mp', 'seq')), may hold values from -0.125 to 0.125
- patch_out: bfloat16 [1024, 8192], P('seq', 'mp'), may hold values from -0.1875 to 0.1875
- gain_attend: float32 [1024], replicated, may hold values from 0.1 to 1.9
- attend_query: bfloat16 [1024, 1024], P('seq', 'mp'), may hold values from -0.1875 to 0.1875
- attend_key: bfloat16 [1024, 1024], P('seq', 'mp'), may hold values from -0.1875 to 0.1875
- attend_value: bfloat16 [1024, 1024], P('seq', 'mp'), may hold values from -0.1875 to 0.1875
- attend_out: bfloat16 [1024, 1024], P(('mp', 'seq')), may hold values from -0.375 to 0.375
- gain_feed: float32 [1024], replicated, may hold values from 0.1 to 1.9
- feed_gate: bfloat16 [1024, 4096], P('seq', 'mp'), may hold values from -0.1875 to 0.1875
- feed_up: bfloat16 [1024, 4096], P('seq', 'mp'), may hold values from -0.1875 to 0.1875
- feed_down: bfloat16 [4096, 1024], P(('mp', 'seq')), may hold values from -0.09375 to 0.09375
Outputs:
- byte_output: bfloat16 [4096, 1024], P('seq')
- grad_input: bfloat16 [4096, 1024], P('seq')
- grad_gain_global: float32 [1024], replicated
- grad_patch_in: float32 [8192, 1024], P(('mp', 'seq'))
- grad_mixer_gate: float32 [1024, 2048], P('seq', 'mp')
- grad_mixer_input: float32 [1024, 2048], P('seq', 'mp')
- grad_mixer_state: float32 [1024, 256], P('seq')
- grad_mixer_step: float32 [1024, 32], P('seq', 'mp')
- grad_conv_input: float32 [4, 2048], P(None, 'mp')
- grad_conv_state: float32 [4, 256], replicated
- grad_step_bias: float32 [32], P('mp')
- grad_decay_log: float32 [32], P('mp')
- grad_skip_gain: float32 [32], P('mp')
- grad_gain_mixer: float32 [2048], P('mp')
- grad_mixer_out: float32 [2048, 1024], P(('mp', 'seq'))
- grad_patch_out: float32 [1024, 8192], P('seq', 'mp')
- grad_gain_attend: float32 [1024], replicated
- grad_attend_query: float32 [1024, 1024], P('seq', 'mp')
- grad_attend_key: float32 [1024, 1024], P('seq', 'mp')
- grad_attend_value: float32 [1024, 1024], P('seq', 'mp')
- grad_attend_out: float32 [1024, 1024], P(('mp', 'seq'))
- grad_gain_feed: float32 [1024], replicated
- grad_feed_gate: float32 [1024, 4096], P('seq', 'mp')
- grad_feed_up: float32 [1024, 4096], P('seq', 'mp')
- grad_feed_down: float32 [4096, 1024], P(('mp', 'seq'))
The draws below stay inside these ranges and needn't reach their ends.
Inputs may be any that keep to these rules, and one draw needn't show every extreme that they name: `seq_lengths`: lengths in patches of 6 sequences laid end to end over all 512 patches: one is 450 long, the other 5 have 62 together, and one to three of them come before the long one.
All inputs are finite; a program needn't handle non-finite values.
Results may differ from the reference program's by a relative error of at most 0.03.
Values may be sent and summed in bfloat16 or wider, within the bound.
No kernel may reach another device: no remote copies, remote signals or barrier semaphores. Data moves between devices by JAX's collectives and lax.ppermute only.
A program may use at most 192 MiB of HBM per device.

```python
import math
from functools import partial
import jax
import jax.numpy as jnp
from jax import lax

E = 1024
HDIM = 64
FF = 4096
D = 1024
DI = 2048
HEADS = 32
NSTATE = 128
KCONV = 4
PATCH = 8
SEQS = 6
BLOCK = 64
BYTES = 4096
PATCHES = 512
SHORTS = 62


def draw_seq_lengths(key, part):
    key = jax.random.fold_in(key, 7)
    key_cuts = jax.random.fold_in(key, 1)
    key_place = jax.random.fold_in(key, 2)
    cut_points = jnp.sort(jax.random.permutation(key_cuts, SHORTS - 1)[:SEQS - 2] + 1).astype(jnp.int32)
    bounds = jnp.concatenate([jnp.zeros((1,), jnp.int32), cut_points, jnp.full((1,), SHORTS, jnp.int32)])
    shorter = bounds[1:] - bounds[:-1]
    before = jax.random.randint(key_place, (), 1, 4)
    places = jnp.arange(SEQS, dtype=jnp.int32)
    chosen = jnp.clip(jnp.where(places < before, places, places - 1), 0, SEQS - 2)
    longest = jnp.full((SEQS,), PATCHES - SHORTS, jnp.int32)
    return jnp.where(places == before, longest, shorter[chosen]).astype(jnp.int32)


def block_scale(own_key, dims, shards, smallest, high):
    gain = 1.0
    for position, blocks in shards:
        heights = jax.random.uniform(jax.random.fold_in(jax.random.fold_in(own_key, 6), position), (blocks,), jnp.float32, smallest / len(shards), high / len(shards))
        gain = gain * jnp.repeat(jnp.exp(heights), dims[position] // blocks).reshape((-1,) + (1,) * (len(dims) - 1 - position))
    return gain


def scatter_about(stream_key, shape, width, bound, split=(), held_as=jnp.bfloat16):
    gain = block_scale(stream_key, shape, split, -0.22, 0.18) if split else 1.0
    drawn = jax.random.normal(stream_key, shape, jnp.float32) * width * gain
    return jnp.minimum(jnp.maximum(drawn, -bound), bound).astype(held_as)


def setup_inputs(seed: int = 0) -> dict:
    key_list = jax.random.split(jax.random.key(seed), 27)
    return {
        "byte_input": scatter_about(key_list[0], (BYTES, E), 1.0, 6.0, ((0, 8),)),
        "seq_lengths": draw_seq_lengths(jax.random.fold_in(key_list[26], 71), 0),
        "cotangent": scatter_about(key_list[2], (BYTES, E), 1.0, 6.0, ((0, 8),), jnp.float32),
        "gain_global": jnp.clip(1.0 + 0.18 * jax.random.normal(key_list[3], (D,), jnp.float32), 0.1, 1.9),
        "patch_in": scatter_about(key_list[4], (PATCH * E, D), (PATCH * E) ** -0.5, 0.0625, ((0, 32),)),
        "mixer_gate": scatter_about(key_list[5], (D, DI), D ** -0.5, 0.1875, ((0, 8), (1, 4))),
        "mixer_input": scatter_about(key_list[6], (D, DI), D ** -0.5, 0.1875, ((0, 8), (1, 4))),
        "mixer_state": scatter_about(key_list[7], (D, 2 * NSTATE), D ** -0.5, 0.1875, ((0, 8),)),
        "mixer_step": scatter_about(key_list[8], (D, HEADS), D ** -0.5, 0.1875, ((0, 8), (1, 4))),
        "conv_input": scatter_about(key_list[9], (KCONV, DI), KCONV ** -0.5, 3.0, ((1, 4),), jnp.float32),
        "conv_state": scatter_about(key_list[10], (KCONV, 2 * NSTATE), KCONV ** -0.5, 3.0, (), jnp.float32),
        "step_bias": jnp.clip(-5.0 + 4.0 * jax.random.uniform(key_list[11], (HEADS,), jnp.float32) ** block_scale(key_list[11], (HEADS,), ((0, 4),), -0.2, 0.2), -5.0, -1.0),
        "decay_log": jnp.clip(-4.6 + 5.2999999 * jax.random.uniform(key_list[12], (HEADS,), jnp.float32) ** block_scale(key_list[12], (HEADS,), ((0, 4),), -0.2, 0.2), -4.6, 0.7),
        "skip_gain": jnp.clip(0.5 + 1.0 * jax.random.uniform(key_list[13], (HEADS,), jnp.float32) ** block_scale(key_list[13], (HEADS,), ((0, 4),), -0.2, 0.2), 0.5, 1.5),
        "gain_mixer": jnp.clip(1.0 + 0.18 * jax.random.normal(key_list[14], (DI,), jnp.float32), 0.1, 1.9),
        "mixer_out": scatter_about(key_list[15], (DI, D), DI ** -0.5, 0.125, ((0, 32),)),
        "patch_out": scatter_about(key_list[16], (D, PATCH * E), D ** -0.5, 0.1875, ((0, 8), (1, 4))),
        "gain_attend": jnp.clip(1.0 + 0.18 * jax.random.normal(key_list[17], (E,), jnp.float32), 0.1, 1.9),
        "attend_query": scatter_about(key_list[18], (E, E), E ** -0.5, 0.1875, ((0, 8), (1, 4))),
        "attend_key": scatter_about(key_list[19], (E, E), E ** -0.5, 0.1875, ((0, 8), (1, 4))),
        "attend_value": scatter_about(key_list[20], (E, E), E ** -0.5, 0.1875, ((0, 8), (1, 4))),
        "attend_out": scatter_about(key_list[21], (E, E), (E // 4) ** -0.5, 0.375, ((0, 32),)),
        "gain_feed": jnp.clip(1.0 + 0.18 * jax.random.normal(key_list[22], (E,), jnp.float32), 0.1, 1.9),
        "feed_gate": scatter_about(key_list[23], (E, FF), E ** -0.5, 0.1875, ((0, 8), (1, 4))),
        "feed_up": scatter_about(key_list[24], (E, FF), E ** -0.5, 0.1875, ((0, 8), (1, 4))),
        "feed_down": scatter_about(key_list[25], (FF, E), FF ** -0.5, 0.09375, ((0, 32),)),
    }


@jax.custom_vjp
def low(v):
    return lax.optimization_barrier(v.astype(jnp.bfloat16)).astype(jnp.float32)

@jax.custom_vjp
def low_back(v):
    return v

def low_keep(v):
    return (low(v), None)

def low_pass(kept, grad):
    return (grad,)

def back_keep(v):
    return (v, None)

def back_low(kept, grad):
    return (low(grad),)
low.defvjp(low_keep, low_pass)
low_back.defvjp(back_keep, back_low)
EPS = 1e-05
HIGH = lax.Precision.HIGHEST

def matmul(former, latter):
    return jnp.dot(former, latter, precision=HIGH, preferred_element_type=jnp.float32)

def rms_scale(values, scale_gain):
    mean_square = lax.optimization_barrier(jnp.mean(values * values, axis=-1, keepdims=True))
    return values * lax.rsqrt(mean_square + EPS) * scale_gain

def segment_of(lengths, start_row, row_count):
    bounds = jnp.cumsum(lengths).astype(jnp.int32)[:-1]
    places = start_row + jnp.arange(row_count, dtype=jnp.int32)
    return lax.optimization_barrier(jnp.sum((places[:, None] >= bounds[None, :]).astype(jnp.int32), axis=1))

def conv_silu(extended, kernel, segment_rows):
    row_count = extended.shape[0] - KCONV + 1
    segment_now = segment_rows[KCONV - 1:]
    summed = jnp.zeros((row_count, extended.shape[1]), jnp.float32)
    for offset in range(KCONV):
        same_seq = (segment_rows[offset:offset + row_count] == segment_now)[:, None]
        summed = summed + jnp.where(same_seq, extended[offset:offset + row_count], 0.0) * kernel[offset]
    return jax.nn.silu(summed)

def block_output(head_values, write_vecs, read_vecs, step_size, log_rate, skip_term, state_value, segment_rows, segment_prev):
    length = head_values.shape[0]
    running = jnp.cumsum(-step_size * jnp.exp(log_rate), axis=0)
    places = jnp.arange(length)
    allowed = (places[:, None] >= places[None, :]) & (segment_rows[:, None] == segment_rows[None, :])
    allowed = allowed[:, :, None]
    spread = jnp.where(allowed, running[:, None, :] - running[None, :, :], 0.0)
    factors = jnp.where(allowed, jnp.exp(spread), 0.0)
    affinity = jnp.dot(read_vecs, write_vecs.T, precision=HIGH, preferred_element_type=jnp.float32)
    mixing = factors * affinity[:, :, None] * step_size[None, :, :]
    inside = jnp.einsum('tsh,shp->thp', mixing, head_values, precision=HIGH)
    carried = jnp.where((segment_rows == segment_prev)[:, None], jnp.exp(running), 0.0)
    reading = jnp.einsum('tn,hpn->thp', read_vecs, state_value, precision=HIGH) * carried[:, :, None]
    result = inside + reading + skip_term[None, :, None] * head_values
    return result.reshape(length, -1)

def block_summary(head_values, write_vecs, step_size, log_rate, segment_rows, segment_prev):
    running = jnp.cumsum(-step_size * jnp.exp(log_rate), axis=0)
    latest = running[-1]
    in_tail = (segment_rows == segment_rows[-1])[:, None]
    weights = jnp.where(in_tail, jnp.exp(latest[None, :] - running), 0.0) * step_size
    scaled = weights[:, :, None] * head_values
    state_local = jnp.einsum('shp,sn->hpn', scaled, write_vecs, precision=HIGH)
    decay_total = jnp.where(segment_rows[-1] == segment_prev, jnp.exp(latest), 0.0)
    return (decay_total, state_local)

def patch_attention(queries, keys_all, values_all):
    row_count = queries.shape[0]
    head_count = queries.shape[1] // HDIM
    query_rows = queries.reshape(row_count // PATCH, PATCH, head_count, HDIM)
    key_rows = keys_all.reshape(row_count // PATCH, PATCH, head_count, HDIM)
    value_rows = values_all.reshape(row_count // PATCH, PATCH, head_count, HDIM)
    scores = jnp.einsum('bihd,bjhd->bhij', query_rows, key_rows, precision=HIGH) * HDIM ** (-0.5)
    causal = jnp.arange(PATCH)[:, None] >= jnp.arange(PATCH)[None, :]
    scores = jnp.where(causal, scores, -1e+30)
    peak = lax.optimization_barrier(jnp.max(scores, axis=-1, keepdims=True))
    probs = jnp.exp(scores - peak)
    probs = probs / lax.optimization_barrier(jnp.sum(probs, axis=-1, keepdims=True))
    context = jnp.einsum('bhij,bjhd->bihd', probs, value_rows, precision=HIGH)
    return context.reshape(row_count, head_count * HDIM)

def local_section(residual_rows, gain_attend, attend_query, attend_key, attend_value, attend_out, gain_feed, feed_gate, feed_up, feed_down):
    attend_in = low(rms_scale(residual_rows, gain_attend))
    queries = low_back(matmul(attend_in, attend_query))
    keys_all = low_back(matmul(attend_in, attend_key))
    values_all = low_back(matmul(attend_in, attend_value))
    context = low(patch_attention(queries, keys_all, values_all))
    middle = residual_rows + low_back(matmul(context, attend_out))
    feed_in = low(rms_scale(middle, gain_feed))
    gate_value = low_back(matmul(feed_in, feed_gate))
    up_value = low_back(matmul(feed_in, feed_up))
    hidden_units = low(jax.nn.silu(gate_value) * up_value)
    return middle + low_back(matmul(hidden_units, feed_down))

def forward(seq_lengths, byte_input, gain_global, patch_in, mixer_gate, mixer_input, mixer_state, mixer_step, conv_input, conv_state, step_bias, decay_log, skip_gain, gain_mixer, mixer_out, patch_out, gain_attend, attend_query, attend_key, attend_value, attend_out, gain_feed, feed_gate, feed_up, feed_down):
    patches = byte_input.reshape(PATCHES, PATCH * E)
    hidden = low_back(matmul(patches, patch_in))
    normed = low(rms_scale(hidden, gain_global))
    gate_pre = low_back(matmul(normed, mixer_gate))
    input_pre = low_back(matmul(normed, mixer_input))
    state_pre = low_back(matmul(normed, mixer_state))
    step_pre = low_back(matmul(normed, mixer_step))
    segment_ext = segment_of(seq_lengths, -(KCONV - 1), PATCHES + KCONV - 1)
    input_conv = conv_silu(jnp.concatenate([jnp.zeros((KCONV - 1, DI), jnp.float32), input_pre], axis=0), conv_input, segment_ext)
    state_conv = conv_silu(jnp.concatenate([jnp.zeros((KCONV - 1, 2 * NSTATE), jnp.float32), state_pre], axis=0), conv_state, segment_ext)
    step_size = jax.nn.softplus(step_pre + step_bias)
    blocks = PATCHES // BLOCK
    head_values = input_conv.reshape(blocks, BLOCK, HEADS, HDIM)
    write_vecs = state_conv[:, :NSTATE].reshape(blocks, BLOCK, NSTATE)
    read_vecs = state_conv[:, NSTATE:].reshape(blocks, BLOCK, NSTATE)
    step_blocks = step_size.reshape(blocks, BLOCK, HEADS)
    segment_rows = segment_ext[KCONV - 1:].reshape(blocks, BLOCK)
    bounds = jnp.cumsum(seq_lengths).astype(jnp.int32)[:-1]
    before_rows = jnp.arange(blocks, dtype=jnp.int32) * BLOCK - 1
    segment_prev = lax.optimization_barrier(jnp.sum((before_rows[:, None] >= bounds[None, :]).astype(jnp.int32), axis=1))

    def advance(state_value, pieces):
        values_in, write_rows, read_rows, step_rows, segment_block, segment_last = pieces
        output = block_output(values_in, write_rows, read_rows, step_rows, decay_log, skip_gain, state_value, segment_block, segment_last)
        decay_total, state_local = block_summary(values_in, write_rows, step_rows, decay_log, segment_block, segment_last)
        return (decay_total[:, None, None] * state_value + state_local, output)
    start_state = jnp.zeros((HEADS, HDIM, NSTATE), jnp.float32)
    _, mixed_out = lax.scan(jax.checkpoint(advance), start_state, (head_values, write_vecs, read_vecs, step_blocks, segment_rows, segment_prev))
    mixer_rows = mixed_out.reshape(PATCHES, DI)
    gated = mixer_rows * jax.nn.silu(gate_pre)
    mixed = low(rms_scale(gated, gain_mixer))
    merged = hidden + low_back(matmul(mixed, mixer_out))
    slot_values = low_back(matmul(low(merged), patch_out))
    residual = byte_input + slot_values.reshape(BYTES, E)
    block_rows = math.gcd(BYTES, 4096)
    local_step = jax.checkpoint(partial(local_section, gain_attend=gain_attend, attend_query=attend_query, attend_key=attend_key, attend_value=attend_value, attend_out=attend_out, gain_feed=gain_feed, feed_gate=feed_gate, feed_up=feed_up, feed_down=feed_down))
    out_blocks = lax.map(local_step, residual.reshape(BYTES // block_rows, block_rows, E))
    return out_blocks.reshape(BYTES, E)

def reference(byte_input, seq_lengths, cotangent, gain_global, patch_in, mixer_gate, mixer_input, mixer_state, mixer_step, conv_input, conv_state, step_bias, decay_log, skip_gain, gain_mixer, mixer_out, patch_out, gain_attend, attend_query, attend_key, attend_value, attend_out, gain_feed, feed_gate, feed_up, feed_down):
    floats = [array_in.astype(jnp.float32) for array_in in (byte_input, gain_global, patch_in, mixer_gate, mixer_input, mixer_state, mixer_step, conv_input, conv_state, step_bias, decay_log, skip_gain, gain_mixer, mixer_out, patch_out, gain_attend, attend_query, attend_key, attend_value, attend_out, gain_feed, feed_gate, feed_up, feed_down)]
    result, pullback = jax.vjp(partial(forward, seq_lengths), *floats)
    grads = pullback(cotangent.astype(jnp.float32))
    return (result.astype(jnp.bfloat16), grads[0].astype(jnp.bfloat16), grads[1], grads[2], grads[3], grads[4], grads[5], grads[6], grads[7], grads[8], grads[9], grads[10], grads[11], grads[12], grads[13], grads[14], grads[15], grads[16], grads[17], grads[18], grads[19], grads[20], grads[21], grads[22], grads[23])
```

```python
import jax
import jax.numpy as jnp
from jax import lax
from jax.sharding import PartitionSpec as P

E = 1024
HDIM = 64
DI = 2048
NSTATE = 128
KCONV = 4
PATCH = 8
TOK_DEV = 512
BLOCK = 64


EPS = 1e-05
HIGH = lax.Precision.HIGHEST


def shifted(shard, axis, by):
    length = lax.axis_size(axis)
    pairs = [(i, i + by) for i in range(length) if 0 <= i + by < length]
    return lax.ppermute(shard, axis, pairs)


def prefix(shard, axis, combine, identity):
    length, position = (lax.axis_size(axis), lax.axis_index(axis))
    everything = jax.tree.map(
        lambda part, kind: lax.all_gather(part.astype(kind), axis),
        shard,
        (jnp.bfloat16, jnp.bfloat16),
    )
    start = jax.tree.map(
        lambda part, zero: jnp.broadcast_to(jnp.asarray(zero, part.dtype), part.shape),
        shard,
        identity,
    )

    def prefix_turn(k, before):
        reached = k < position
        new = combine(
            before, jax.tree.map(lambda part, own: part[k].astype(own.dtype), everything, shard)
        )
        return jax.tree.map(lambda a, b: jnp.where(reached, a, b), new, before)

    return lax.fori_loop(0, length, prefix_turn, start)


def carried_in(shard, axis, combine, identity):
    length, position = (lax.axis_size(axis), lax.axis_index(axis))
    everything = jax.tree.map(
        lambda part, kind: lax.all_gather(part.astype(kind), axis),
        shard,
        jax.tree.map(lambda a: jnp.bfloat16 if a.dtype == jnp.float32 else a.dtype, shard),
    )
    start = jax.tree.map(
        lambda part, zero: jnp.broadcast_to(jnp.asarray(zero, part.dtype), part.shape),
        shard,
        identity,
    )

    def carried_turn(k, before):
        at = length - 1 - k
        reached = at > position
        new = combine(
            before, jax.tree.map(lambda part, own: part[at].astype(own.dtype), everything, shard)
        )
        return jax.tree.map(lambda a, b: jnp.where(reached, a, b), new, before)

    return lax.fori_loop(0, length, carried_turn, start)


def product(former, latter):
    return jnp.dot(former, latter, preferred_element_type=jnp.float32)


def product_left(former, latter):
    return lax.dot_general(
        former, latter, (((0,), (0,)), ((), ())), preferred_element_type=jnp.float32
    )


def product_right(former, latter):
    return lax.dot_general(
        former, latter, (((1,), (1,)), ((), ())), preferred_element_type=jnp.float32
    )


def over_heads(partial_sum):
    return lax.psum(partial_sum, "mp")


def gather_slots(pieces):
    return lax.all_gather(pieces.astype(jnp.bfloat16), "mp", axis=1, tiled=True).astype(
        pieces.dtype
    )


def rms_scale(values, scale_gain):
    mean_square = jnp.mean(values * values, axis=-1, keepdims=True)
    return values * lax.rsqrt(mean_square + EPS) * scale_gain


def rms_back(values, scale_gain, upstream):
    pullback = jax.vjp(rms_scale, values, scale_gain)[1]
    return pullback(upstream)


def running_bounds(lengths):
    places = jnp.arange(lengths.shape[0])
    upto = places[None, :] <= places[:-1, None]
    return jnp.sum(jnp.where(upto, lengths[None, :], 0), axis=1)


def running_sum(values):
    places = jnp.arange(values.shape[0])
    lower = (places[:, None] >= places[None, :]).astype(jnp.float32)
    return jnp.dot(lower, values, precision=HIGH, preferred_element_type=jnp.float32)


def segment_of(lengths, start_row, row_count):
    bounds = running_bounds(lengths)
    places = start_row + jnp.arange(row_count, dtype=jnp.int32)
    return jnp.sum((places[:, None] >= bounds[None, :]).astype(jnp.int32), axis=1)


def conv_silu(extended, kernel, segment_rows):
    row_count = extended.shape[0] - KCONV + 1
    segment_now = segment_rows[KCONV - 1 :]
    summed = jnp.zeros((row_count, extended.shape[1]), jnp.float32)
    for offset in range(KCONV):
        same_seq = (segment_rows[offset : offset + row_count] == segment_now)[:, None]
        summed = (
            summed
            + jnp.where(same_seq, extended[offset : offset + row_count], 0.0) * kernel[offset]
        )
    return jax.nn.silu(summed)


def block_output(
    head_values,
    write_vecs,
    read_vecs,
    step_size,
    log_rate,
    skip_term,
    state_value,
    segment_rows,
    segment_prev,
):
    length = head_values.shape[0]
    running = running_sum(-step_size * jnp.exp(log_rate))
    places = jnp.arange(length)
    allowed = (places[:, None] >= places[None, :]) & (
        segment_rows[:, None] == segment_rows[None, :]
    )
    allowed = allowed[:, :, None]
    spread = jnp.where(allowed, running[:, None, :] - running[None, :, :], 0.0)
    factors = jnp.where(allowed, jnp.exp(spread), 0.0)
    affinity = jnp.dot(read_vecs, write_vecs.T, precision=HIGH, preferred_element_type=jnp.float32)
    mixing = factors * affinity[:, :, None] * step_size[None, :, :]
    inside = jnp.einsum("tsh,shp->thp", mixing, head_values, precision=HIGH)
    carried = jnp.where((segment_rows == segment_prev)[:, None], jnp.exp(running), 0.0)
    reading = (
        jnp.einsum("tn,hpn->thp", read_vecs, state_value, precision=HIGH) * carried[:, :, None]
    )
    result = inside + reading + skip_term[None, :, None] * head_values
    return result.reshape(length, -1)


def block_summary(head_values, write_vecs, step_size, log_rate, segment_rows, segment_prev):
    running = running_sum(-step_size * jnp.exp(log_rate))
    latest = running[-1]
    in_tail = (segment_rows == segment_rows[-1])[:, None]
    weights = jnp.where(in_tail, jnp.exp(latest[None, :] - running), 0.0) * step_size
    scaled = weights[:, :, None] * head_values
    state_local = jnp.einsum("shp,sn->hpn", scaled, write_vecs, precision=HIGH)
    decay_total = jnp.where(segment_rows[-1] == segment_prev, jnp.exp(latest), 0.0)
    return (decay_total, state_local)


def combine_state(earlier, later):
    return (earlier[0] * later[0], later[0][:, None, None] * earlier[1] + later[1])


def patch_attention(queries, keys_all, values_all):
    row_count = queries.shape[0]
    head_count = queries.shape[1] // HDIM
    query_rows = queries.reshape(row_count // PATCH, PATCH, head_count, HDIM)
    key_rows = keys_all.reshape(row_count // PATCH, PATCH, head_count, HDIM)
    value_rows = values_all.reshape(row_count // PATCH, PATCH, head_count, HDIM)
    scores = jnp.einsum("bihd,bjhd->bhij", query_rows, key_rows, precision=HIGH) * HDIM ** (-0.5)
    causal = jnp.arange(PATCH)[:, None] >= jnp.arange(PATCH)[None, :]
    scores = jnp.where(causal, scores, -1e30)
    peak = jnp.max(scores, axis=-1, keepdims=True)
    probs = jnp.exp(scores - peak)
    probs = probs / jnp.sum(probs, axis=-1, keepdims=True)
    context = jnp.einsum("bhij,bjhd->bihd", probs, value_rows, precision=HIGH)
    return context.reshape(row_count, head_count * HDIM)


def add_tail(main_rows, tail_rows):
    keep_count = main_rows.shape[0] - tail_rows.shape[0]
    return jnp.concatenate([main_rows[:keep_count], main_rows[keep_count:] + tail_rows], axis=0)


def gathered_plan(
    byte_input,
    seq_lengths,
    cotangent,
    gain_global,
    patch_in,
    mixer_gate,
    mixer_input,
    mixer_state,
    mixer_step,
    conv_input,
    conv_state,
    step_bias,
    decay_log,
    skip_gain,
    gain_mixer,
    mixer_out,
    patch_out,
    gain_attend,
    attend_query,
    attend_key,
    attend_value,
    attend_out,
    gain_feed,
    feed_gate,
    feed_up,
    feed_down,
):
    group_size = lax.axis_size("mp")
    slot_width = PATCH * E // group_size
    slot_start = lax.axis_index("mp") * slot_width
    first_row = lax.axis_index("seq") * BLOCK
    segment_ext = segment_of(seq_lengths, first_row - (KCONV - 1), BLOCK + KCONV - 1)
    segment_rows = segment_ext[KCONV - 1 :]
    segment_prev = segment_of(seq_lengths, first_row - 1, 1)[0]

    def fetch_global():
        return (
            lax.all_gather(patch_in, "seq", axis=0, tiled=True),
            lax.all_gather(mixer_gate, "seq", axis=0, tiled=True),
            lax.all_gather(mixer_input, "seq", axis=0, tiled=True),
            lax.all_gather(mixer_state, "seq", axis=0, tiled=True),
            lax.all_gather(mixer_step, "seq", axis=0, tiled=True),
            lax.all_gather(mixer_out, "seq", axis=0, tiled=True),
            lax.all_gather(patch_out, "seq", axis=0, tiled=True),
        )

    def fetch_local():
        return (
            lax.all_gather(attend_query, "seq", axis=0, tiled=True),
            lax.all_gather(attend_key, "seq", axis=0, tiled=True),
            lax.all_gather(attend_value, "seq", axis=0, tiled=True),
            lax.all_gather(attend_out, "seq", axis=0, tiled=True),
            lax.all_gather(feed_gate, "seq", axis=0, tiled=True),
            lax.all_gather(feed_up, "seq", axis=0, tiled=True),
            lax.all_gather(feed_down, "seq", axis=0, tiled=True),
        )

    def conv_of(extended, kernel):
        return conv_silu(extended, kernel, segment_ext)

    def summary_of(values_in, writes_in, steps_in, rates_in):
        return block_summary(values_in, writes_in, steps_in, rates_in, segment_rows, segment_prev)

    def output_of(values_in, writes_in, reads_in, steps_in, rates_in, skips_in, state_value):
        return block_output(
            values_in,
            writes_in,
            reads_in,
            steps_in,
            rates_in,
            skips_in,
            state_value,
            segment_rows,
            segment_prev,
        )

    full_patch_in, full_gate, full_input, full_state, full_step, full_mixout, full_patchout = (
        fetch_global()
    )
    patches = byte_input.reshape(BLOCK, PATCH * E)
    local_bytes = lax.dynamic_slice_in_dim(patches, slot_start, slot_width, 1)
    hidden = over_heads(product(local_bytes, full_patch_in))
    normed = rms_scale(hidden, gain_global).astype(jnp.bfloat16)
    gate_pre = product(normed, full_gate)
    input_pre = product(normed, full_input)
    state_pre = product(normed, full_state)
    step_pre = product(normed, full_step)
    rim_rows = shifted((input_pre[BLOCK - KCONV + 1 :], state_pre[BLOCK - KCONV + 1 :]), "seq", 1)
    input_ext = jnp.concatenate([rim_rows[0], input_pre], axis=0)
    state_ext = jnp.concatenate([rim_rows[1], state_pre], axis=0)
    input_conv = conv_of(input_ext, conv_input)
    state_conv = conv_of(state_ext, conv_state)
    step_size = jax.nn.softplus(step_pre + step_bias)
    head_count = step_size.shape[1]
    head_values = input_conv.reshape(BLOCK, head_count, HDIM)
    write_vecs = state_conv[:, :NSTATE]
    read_vecs = state_conv[:, NSTATE:]
    decay_total, state_local = summary_of(head_values, write_vecs, step_size, decay_log)
    identity = (jnp.ones_like(decay_total), jnp.zeros_like(state_local))
    state_in = prefix((decay_total, state_local), "seq", combine_state, identity)[1]
    mixer_rows = output_of(
        head_values, write_vecs, read_vecs, step_size, decay_log, skip_gain, state_in
    )
    gate_sigm = jax.nn.sigmoid(gate_pre)
    gate_silu = gate_pre * gate_sigm
    gated = mixer_rows * gate_silu
    mean_square = over_heads(jnp.sum(gated * gated, axis=-1, keepdims=True)) / DI
    root_inverse = lax.rsqrt(mean_square + EPS)
    mixed = (gated * root_inverse * gain_mixer).astype(jnp.bfloat16)
    merged = hidden + over_heads(product(mixed, full_mixout))
    merged_low = merged.astype(jnp.bfloat16)
    slot_values = gather_slots(product(merged_low, full_patchout)).reshape(TOK_DEV, E)
    residual = byte_input.astype(jnp.float32) + slot_values
    full_query, full_key, full_value, full_attout, full_feedgate, full_up, full_down = fetch_local()
    attend_in = rms_scale(residual, gain_attend).astype(jnp.bfloat16)
    queries = product(attend_in, full_query)
    keys_all = product(attend_in, full_key)
    values_all = product(attend_in, full_value)
    context = patch_attention(queries, keys_all, values_all).astype(jnp.bfloat16)
    middle = residual + over_heads(product(context, full_attout))
    feed_in = rms_scale(middle, gain_feed).astype(jnp.bfloat16)
    gate_value = product(feed_in, full_feedgate)
    up_value = product(feed_in, full_up)
    gate_sig = jax.nn.sigmoid(gate_value)
    hidden_units = (gate_value * gate_sig * up_value).astype(jnp.bfloat16)
    byte_output = middle + over_heads(product(hidden_units, full_down))
    full_query, full_key, full_value, full_attout, full_feedgate, full_up, full_down = fetch_local()
    out_low = cotangent.astype(jnp.bfloat16)
    grad_feed_down = product_left(hidden_units, out_low)
    grad_units = product_right(out_low, full_down)
    grad_gate_value = (
        grad_units * up_value * gate_sig * (1.0 + gate_value * (1.0 - gate_sig))
    ).astype(jnp.bfloat16)
    grad_up_value = (grad_units * gate_value * gate_sig).astype(jnp.bfloat16)
    grad_feed_gate = product_left(feed_in, grad_gate_value)
    grad_feed_up = product_left(feed_in, grad_up_value)
    grad_feed_in = over_heads(
        product_right(grad_gate_value, full_feedgate) + product_right(grad_up_value, full_up)
    )
    grad_middle_part, grad_gain_feed = rms_back(middle, gain_feed, grad_feed_in)
    grad_middle = cotangent + grad_middle_part
    middle_low = grad_middle.astype(jnp.bfloat16)
    grad_attend_out = product_left(context, middle_low)
    grad_context = product_right(middle_low, full_attout)
    attention_pull = jax.vjp(patch_attention, queries, keys_all, values_all)[1]
    grad_query_raw, grad_key_raw, grad_value_raw = attention_pull(grad_context)
    grad_query_rows = grad_query_raw.astype(jnp.bfloat16)
    grad_key_rows = grad_key_raw.astype(jnp.bfloat16)
    grad_value_rows = grad_value_raw.astype(jnp.bfloat16)
    grad_attend_query = product_left(attend_in, grad_query_rows)
    grad_attend_key = product_left(attend_in, grad_key_rows)
    grad_attend_value = product_left(attend_in, grad_value_rows)
    grad_attend_in = over_heads(
        product_right(grad_query_rows, full_query)
        + product_right(grad_key_rows, full_key)
        + product_right(grad_value_rows, full_value)
    )
    grad_residual_part, grad_gain_attend = rms_back(residual, gain_attend, grad_attend_in)
    grad_residual = grad_middle + grad_residual_part
    local_sums = (
        lax.psum_scatter(grad_attend_query, "seq", scatter_dimension=0, tiled=True),
        lax.psum_scatter(grad_attend_key, "seq", scatter_dimension=0, tiled=True),
        lax.psum_scatter(grad_attend_value, "seq", scatter_dimension=0, tiled=True),
        lax.psum_scatter(grad_attend_out, "seq", scatter_dimension=0, tiled=True),
        lax.psum_scatter(grad_feed_gate, "seq", scatter_dimension=0, tiled=True),
        lax.psum_scatter(grad_feed_up, "seq", scatter_dimension=0, tiled=True),
        lax.psum_scatter(grad_feed_down, "seq", scatter_dimension=0, tiled=True),
    )
    full_patch_in, full_gate, full_input, full_state, full_step, full_mixout, full_patchout = (
        fetch_global()
    )
    residual_patches = grad_residual.reshape(BLOCK, PATCH * E)
    slot_grad = lax.dynamic_slice_in_dim(residual_patches, slot_start, slot_width, 1).astype(
        jnp.bfloat16
    )
    grad_patch_out = product_left(merged_low, slot_grad)
    grad_merged = over_heads(product_right(slot_grad, full_patchout))
    merged_grad_low = grad_merged.astype(jnp.bfloat16)
    grad_mixer_out = product_left(mixed, merged_grad_low)
    grad_mixed = product_right(merged_grad_low, full_mixout)
    grad_gain_mixer = jnp.sum(grad_mixed * gated * root_inverse, axis=0)
    scaled_grad = grad_mixed * gain_mixer
    inner_dot = over_heads(jnp.sum(scaled_grad * gated, axis=-1, keepdims=True))
    grad_gated = scaled_grad * root_inverse - gated * inner_dot * root_inverse**3 / DI
    grad_mixer_rows = grad_gated * gate_silu
    grad_gate_pre = grad_gated * mixer_rows * gate_sigm * (1.0 + gate_pre * (1.0 - gate_sigm))
    output_pull = jax.vjp(
        output_of, head_values, write_vecs, read_vecs, step_size, decay_log, skip_gain, state_in
    )[1]
    (
        grad_values_a,
        grad_writes_a,
        grad_reads,
        grad_steps_a,
        grad_rates_a,
        grad_skip_gain,
        grad_state_in,
    ) = output_pull(grad_mixer_rows)
    state_end = carried_in((decay_total, grad_state_in), "seq", combine_state, identity)[1]
    summary_pull = jax.vjp(summary_of, head_values, write_vecs, step_size, decay_log)[1]
    grad_values_b, grad_writes_b, grad_steps_b, grad_rates_b = summary_pull(
        (jnp.sum(state_end * state_in, axis=(1, 2)), state_end)
    )
    grad_input_conv = (grad_values_a + grad_values_b).reshape(BLOCK, -1)
    grad_state_conv = over_heads(
        jnp.concatenate([grad_writes_a + grad_writes_b, grad_reads], axis=1)
    )
    grad_step_pre = (grad_steps_a + grad_steps_b) * jax.nn.sigmoid(step_pre + step_bias)
    grad_step_bias = jnp.sum(grad_step_pre, axis=0)
    grad_decay_log = grad_rates_a + grad_rates_b
    grad_input_ext, grad_conv_input = jax.vjp(conv_of, input_ext, conv_input)[1](grad_input_conv)
    grad_state_ext, grad_conv_state = jax.vjp(conv_of, state_ext, conv_state)[1](grad_state_conv)
    rim_back = shifted((grad_input_ext[: KCONV - 1], grad_state_ext[: KCONV - 1]), "seq", -1)
    grad_input_low = add_tail(grad_input_ext[KCONV - 1 :], rim_back[0]).astype(jnp.bfloat16)
    grad_state_low = add_tail(grad_state_ext[KCONV - 1 :], rim_back[1]).astype(jnp.bfloat16)
    grad_gate_low = grad_gate_pre.astype(jnp.bfloat16)
    grad_step_low = grad_step_pre.astype(jnp.bfloat16)
    grad_mixer_gate = product_left(normed, grad_gate_low)
    grad_mixer_input = product_left(normed, grad_input_low)
    grad_mixer_state = product_left(normed, grad_state_low)
    grad_mixer_step = product_left(normed, grad_step_low)
    head_part = over_heads(
        product_right(grad_gate_low, full_gate)
        + product_right(grad_input_low, full_input)
        + product_right(grad_step_low, full_step)
    )
    grad_normed = head_part + product_right(grad_state_low, full_state)
    grad_hidden_part, grad_gain_global = rms_back(hidden, gain_global, grad_normed)
    hidden_grad_low = (grad_merged + grad_hidden_part).astype(jnp.bfloat16)
    grad_patch_in = product_left(local_bytes, hidden_grad_low)
    grad_byte_part = gather_slots(product_right(hidden_grad_low, full_patch_in)).reshape(TOK_DEV, E)
    grad_input = (grad_residual + grad_byte_part).astype(jnp.bfloat16)
    global_sums = (
        lax.psum_scatter(grad_patch_in, "seq", scatter_dimension=0, tiled=True),
        lax.psum_scatter(grad_mixer_gate, "seq", scatter_dimension=0, tiled=True),
        lax.psum_scatter(grad_mixer_input, "seq", scatter_dimension=0, tiled=True),
        lax.psum_scatter(grad_mixer_state, "seq", scatter_dimension=0, tiled=True),
        lax.psum_scatter(grad_mixer_step, "seq", scatter_dimension=0, tiled=True),
        lax.psum_scatter(grad_mixer_out, "seq", scatter_dimension=0, tiled=True),
        lax.psum_scatter(grad_patch_out, "seq", scatter_dimension=0, tiled=True),
    )
    small_sums = lax.psum(
        (
            grad_gain_global,
            grad_conv_input,
            grad_conv_state,
            grad_step_bias,
            grad_decay_log,
            grad_skip_gain,
            grad_gain_mixer,
            grad_gain_attend,
            grad_gain_feed,
        ),
        "seq",
    )
    return (
        byte_output.astype(jnp.bfloat16),
        grad_input,
        small_sums[0],
        global_sums[0],
        global_sums[1],
        global_sums[2],
        global_sums[3],
        global_sums[4],
        small_sums[1],
        small_sums[2],
        small_sums[3],
        small_sums[4],
        small_sums[5],
        small_sums[6],
        global_sums[5],
        global_sums[6],
        small_sums[7],
        local_sums[0],
        local_sums[1],
        local_sums[2],
        local_sums[3],
        small_sums[8],
        local_sums[4],
        local_sums[5],
        local_sums[6],
    )


PAIR_X = [(i, i ^ 1) for i in range(8)]
PAIR_C = [(i, i ^ 1) for i in range(4)]
PAIR_Y = [(i, i ^ 2) for i in range(4)]


def bf(values):
    return values.astype(jnp.bfloat16)


def swap_x(shard):
    return lax.ppermute(shard, "seq", PAIR_X)


def swap_c(shard):
    return lax.ppermute(shard, "mp", PAIR_C)


def swap_y(shard):
    return lax.ppermute(shard, "mp", PAIR_Y)


def swap_seq(shard, by):
    return lax.ppermute(shard, "seq", [(i, i ^ by) for i in range(8)])


def pick(stacked, index):
    return lax.dynamic_index_in_dim(stacked, index, 0, keepdims=False)


def in_order(mine, other, bit):
    first = jnp.where(bit == 0, mine, other)
    second = jnp.where(bit == 0, other, mine)
    return jnp.concatenate([first, second], axis=0)


def select_blocks(blocks, own, count):
    placed = []
    for j in range(count):
        value = blocks[0]
        for k in range(1, count):
            value = jnp.where((own ^ k) == j, blocks[k], value)
        placed.append(value)
    return placed


def scatter_rows(partial, place):
    z, x, c = place
    width = partial.shape[1]
    halves = partial.reshape(2, -1, width)
    rows = pick(halves, c) + swap_c(bf(pick(halves, 1 - c))).astype(jnp.float32)
    halves = rows.reshape(2, -1, width)
    rows = pick(halves, x) + swap_x(bf(pick(halves, 1 - x))).astype(jnp.float32)
    parts = rows.reshape(4, -1, width)
    low = bf(parts)
    rows = pick(parts, z)
    got = [swap_seq(pick(low, z ^ k), 2 * k) for k in range(1, 4)]
    for part in got:
        rows = rows + part.astype(jnp.float32)
    return rows


def gather_rows(rows, place):
    z, x, c = place
    parts = [rows] + [swap_seq(rows, 2 * k) for k in range(1, 4)]
    rows = jnp.concatenate(select_blocks(parts, z, 4), axis=0)
    rows = in_order(rows, swap_x(rows), x)
    return in_order(rows, swap_c(rows), c)


def both_y(rows):
    low = bf(rows)
    return low.astype(jnp.float32) + swap_y(low).astype(jnp.float32)


def gather_bytes(rows):
    far = swap_y(rows)
    return [rows, swap_c(rows), far, swap_c(far)]


def scatter_bytes(partial):
    width = partial.shape[1]
    blocks = partial.reshape(4, -1, width)
    sent = swap_c(bf(jnp.stack([blocks[1], blocks[3]])))
    near = blocks[0] + sent[0].astype(jnp.float32)
    far = blocks[2] + sent[1].astype(jnp.float32)
    return near + swap_y(bf(far)).astype(jnp.float32)


def exchange_seq(stacked, s):
    got = [pick(stacked, s)] + [swap_seq(pick(stacked, s ^ k), k) for k in range(1, 8)]
    return jnp.stack(select_blocks(got, s, 8))


def mixer_core(input_pre, state_pre, step_pre, taps, state_taps, bias, log_rate, skip, segment):
    length = input_pre.shape[0]
    seg_ext = jnp.concatenate([jnp.full((KCONV - 1,), -1, jnp.int32), segment])

    def conv(values, kernel):
        return conv_silu(jnp.pad(values, ((KCONV - 1, 0), (0, 0))), kernel, seg_ext)

    heads = conv(input_pre, taps)
    state = conv(state_pre, state_taps)
    writes, reads = (state[:, :NSTATE], state[:, NSTATE:])
    step_size = jax.nn.softplus(step_pre + bias)
    running = running_sum(-step_size * jnp.exp(log_rate))
    places = jnp.arange(length)
    allowed = (places[:, None] >= places[None, :]) & (segment[:, None] == segment[None, :])
    affinity = product_right(bf(reads), bf(writes))
    outs = []
    for h in range(input_pre.shape[1] // HDIM):
        values = heads[:, h * HDIM : (h + 1) * HDIM]
        spread = jnp.where(allowed, running[:, h : h + 1] - running[:, h][None, :], 0.0)
        factors = jnp.where(allowed, jnp.exp(spread), 0.0)
        mixing = bf(factors * affinity)
        outs.append(
            product(mixing, bf(values * step_size[:, h : h + 1])) + skip[h] * values
        )
    return jnp.concatenate(outs, axis=1)


def block_attention(queries, keys, values):
    rows, width = queries.shape
    heads = width // HDIM
    q, k, v = (a.reshape(rows // 128, 128, heads, HDIM) for a in (queries, keys, values))
    scores = jnp.einsum(
        "bihd,bjhd->bhij", bf(q), bf(k), preferred_element_type=jnp.float32
    ) * HDIM ** (-0.5)
    i, j = (jnp.arange(128)[:, None], jnp.arange(128)[None, :])
    mask = (i >= j) & (i // PATCH == j // PATCH)
    scores = jnp.where(mask, scores, -1e30)
    peak = jnp.max(scores, axis=-1, keepdims=True)
    probs = jnp.exp(scores - peak)
    probs = probs / jnp.sum(probs, axis=-1, keepdims=True)
    out = jnp.einsum("bhij,bjhd->bihd", bf(probs), bf(v), preferred_element_type=jnp.float32)
    return out.reshape(rows, width)


def split_plan(
    byte_input,
    seq_lengths,
    cotangent,
    gain_global,
    patch_in,
    mixer_gate,
    mixer_input,
    mixer_state,
    mixer_step,
    conv_input,
    conv_state,
    step_bias,
    decay_log,
    skip_gain,
    gain_mixer,
    mixer_out,
    patch_out,
    gain_attend,
    attend_query,
    attend_key,
    attend_value,
    attend_out,
    gain_feed,
    feed_gate,
    feed_up,
    feed_down,
):
    s, m = (lax.axis_index("seq"), lax.axis_index("mp"))
    z, x, y, c = (s // 2, s % 2, m // 2, m % 2)
    place = (z, x, c)
    patches = 512
    f32 = jnp.float32

    step_far = swap_y(mixer_step)
    gathered_a = lax.all_gather(
        jnp.concatenate(
            [
                mixer_state,
                mixer_step,
                step_far,
                jnp.zeros((128, 112), jnp.bfloat16),
                attend_query,
                attend_key,
                attend_value,
            ],
            axis=1,
        ),
        "seq",
        axis=0,
        tiled=True,
    )
    gathered_b = lax.all_gather(
        jnp.concatenate([feed_gate, feed_up, attend_out.reshape(128, 256)], axis=1),
        "seq",
        axis=0,
        tiled=True,
    )
    down = lax.all_gather(feed_down, "seq", axis=0, tiled=True)
    w_state = gathered_a[:, :256]
    w_step = jnp.concatenate(
        [
            lax.dynamic_slice_in_dim(gathered_a, 256 + jnp.where(y == 0, s, 8 + s), 1, 1),
            lax.dynamic_slice_in_dim(gathered_a, 256 + jnp.where(y == 0, 8 + s, s), 1, 1),
        ],
        axis=1,
    )
    w_qkv = gathered_a[:, 384:]
    w_gate, w_up = (gathered_b[:, :1024], gathered_b[:, 1024:2048])
    w_out = gathered_b[:, 2048:].reshape(256, 1024)

    own_slots = lax.dynamic_slice_in_dim(byte_input.reshape(64, PATCH, E), 2 * m, 2, 1)
    sent = own_slots.reshape(64, 8, 256).transpose(1, 0, 2)
    columns_in = lax.all_to_all(sent, "seq", 0, 0, tiled=True).reshape(patches, 256)
    hidden = both_y(scatter_rows(product(columns_in, patch_in), place))
    normed = gather_rows(bf(rms_scale(hidden, gain_global)), place)

    moved = jnp.concatenate(
        [
            mixer_gate.reshape(128, 8, HDIM),
            mixer_input.reshape(128, 8, HDIM),
            patch_out.reshape(128, 8, 256),
        ],
        axis=2,
    ).transpose(1, 0, 2)
    moved = exchange_seq(moved, s).reshape(1024, 384)
    heads_own = moved[:, : 2 * HDIM]
    w_patch = moved[:, 2 * HDIM :]
    heads_far = swap_y(heads_own)
    w_first = jnp.where(y == 0, heads_own, heads_far)
    w_second = jnp.where(y == 0, heads_far, heads_own)
    w_heads = jnp.concatenate(
        [w_first[:, :HDIM], w_second[:, :HDIM], w_first[:, HDIM:], w_second[:, HDIM:]], axis=1
    )
    w_mixout = in_order(mixer_out, swap_y(mixer_out), y)
    table = jnp.concatenate(
        [
            lax.dynamic_slice_in_dim(conv_input, s * HDIM, HDIM, 1),
            lax.dynamic_slice_in_dim(gain_mixer, s * HDIM, HDIM, 0)[None],
            jnp.broadcast_to(lax.dynamic_slice_in_dim(step_bias, s, 1, 0)[:, None], (1, HDIM)),
            jnp.broadcast_to(lax.dynamic_slice_in_dim(decay_log, s, 1, 0)[:, None], (1, HDIM)),
            jnp.broadcast_to(lax.dynamic_slice_in_dim(skip_gain, s, 1, 0)[:, None], (1, HDIM)),
        ],
        axis=0,
    )
    table = in_order(table[None], swap_y(table)[None], y)
    taps = jnp.concatenate([table[0, :4], table[1, :4]], axis=1)
    gain_heads = jnp.concatenate([table[0, 4], table[1, 4]])
    bias, log_rate, skip = (table[:, 5, 0], table[:, 6, 0], table[:, 7, 0])

    heads_pre = product(normed, w_heads)
    gate_pre, input_pre = (heads_pre[:, :128], heads_pre[:, 128:])
    state_pre = product(normed, w_state)
    step_pre = product(normed, w_step)
    segment = segment_of(seq_lengths, 0, patches)
    mixer_rows, core_pull = jax.vjp(
        lambda *a: mixer_core(*a, segment),
        input_pre,
        state_pre,
        step_pre,
        taps,
        conv_state,
        bias,
        log_rate,
        skip,
    )
    gate_sigm = jax.nn.sigmoid(gate_pre)
    gate_silu = gate_pre * gate_sigm
    gated = mixer_rows * gate_silu
    scaled = bf(gated * gain_heads)
    squares = jnp.broadcast_to(jnp.sum(gated * gated, axis=1, keepdims=True), (patches, 128))
    sums = scatter_rows(jnp.concatenate([product(scaled, w_mixout), squares], axis=1), place)
    unscaled, root = (sums[:, :1024], lax.rsqrt(sums[:, 1024:1025] / DI + EPS))
    merged_low = gather_rows(bf(hidden + root * unscaled), place)
    slots = bf(product(merged_low, w_patch)).reshape(32, 16, 256)
    slots = lax.all_to_all(slots, ("seq", "mp"), 0, 0, tiled=True)
    slots = slots.reshape(8, 4, 16, 256).transpose(2, 1, 0, 3).reshape(128, E)
    residual = lax.dynamic_slice_in_dim(byte_input, m * 128, 128, 0).astype(f32) + slots

    attend_in = jnp.concatenate(gather_bytes(bf(rms_scale(residual, gain_attend))), axis=0)
    qkv = product(attend_in, w_qkv)
    context_raw, attention_pull = jax.vjp(
        block_attention, qkv[:, :256], qkv[:, 256:512], qkv[:, 512:]
    )
    context = bf(context_raw)
    middle = residual + scatter_bytes(product(context, w_out))
    feed_in = jnp.concatenate(gather_bytes(bf(rms_scale(middle, gain_feed))), axis=0)
    gate_value = product(feed_in, w_gate)
    up_value = product(feed_in, w_up)
    gate_sig = jax.nn.sigmoid(gate_value)
    hidden_units = bf(gate_value * gate_sig * up_value)

    cot_blocks = cotangent.reshape(4, 128, E)
    cot_rows = pick(cot_blocks, m)
    out_low = jnp.concatenate([bf(pick(cot_blocks, m ^ k)) for k in range(4)], axis=0)
    grad_units = product_right(out_low, down)
    grad_gate_value = bf(grad_units * up_value * gate_sig * (1.0 + gate_value * (1.0 - gate_sig)))
    grad_up_value = bf(grad_units * gate_value * gate_sig)
    grad_feed_in = scatter_bytes(
        product_right(grad_gate_value, w_gate) + product_right(grad_up_value, w_up)
    )
    sum_gate = lax.psum_scatter(
        bf(product_left(feed_in, grad_gate_value)), "seq", scatter_dimension=0, tiled=True
    )
    sum_up = lax.psum_scatter(
        bf(product_left(feed_in, grad_up_value)), "seq", scatter_dimension=0, tiled=True
    )
    grad_middle_part, gain_feed_part = rms_back(middle, gain_feed, grad_feed_in)
    grad_middle = cot_rows + grad_middle_part
    middle_low = jnp.concatenate(gather_bytes(bf(grad_middle)), axis=0)
    grad_context = product_right(middle_low, w_out)
    grad_qkv = bf(jnp.concatenate(attention_pull(grad_context), axis=1))
    grad_attend_in = scatter_bytes(product_right(grad_qkv, w_qkv))
    sum_rest = lax.psum_scatter(
        jnp.concatenate(
            [
                bf(product_left(context, middle_low)).reshape(8, 32, 1024),
                bf(product_left(hidden_units, out_low)).reshape(8, 128, 1024),
            ],
            axis=1,
        ).reshape(1280, 1024),
        "seq",
        scatter_dimension=0,
        tiled=True,
    )
    sum_qkv = lax.psum_scatter(
        bf(product_left(attend_in, grad_qkv)), "seq", scatter_dimension=0, tiled=True
    )
    grad_residual_part, gain_attend_part = rms_back(residual, gain_attend, grad_attend_in)
    grad_residual = grad_middle + grad_residual_part

    out_rows = bf(middle + scatter_bytes(product(hidden_units, down)))
    byte_output = jnp.concatenate(select_blocks(gather_bytes(out_rows), m, 4), axis=0)

    slot_rows = bf(grad_residual).reshape(16, 4, 8, 256).transpose(2, 1, 0, 3).reshape(32, 16, 256)
    slot_grad = lax.all_to_all(slot_rows, ("seq", "mp"), 0, 0, tiled=True).reshape(patches, 256)
    grad_patch_cols = bf(product_left(merged_low, slot_grad))
    grad_patch_out = (
        exchange_seq(grad_patch_cols.reshape(8, 128, 256), s)
        .transpose(1, 0, 2)
        .reshape(128, 2048)
        .astype(f32)
    )
    merged_rows = scatter_rows(product_right(slot_grad, w_patch), place)
    gains = jnp.stack([gain_feed_part, gain_attend_part])
    merged_rows = both_y(jnp.concatenate([merged_rows, gains, jnp.zeros((6, 1024), f32)], axis=0))
    grad_merged, gain_rows = (merged_rows[:32], merged_rows[32:])
    merged_grad_low = bf(grad_merged).astype(f32)
    kappa = jnp.sum(merged_grad_low * unscaled, axis=1, keepdims=True) * root**3 / DI
    sent = jnp.concatenate(
        [
            jnp.concatenate([merged_grad_low * root, jnp.broadcast_to(kappa, (32, 128))], axis=1),
            jnp.concatenate([gain_rows, jnp.zeros((8, 128), f32)], axis=1),
        ],
        axis=0,
    )
    got = gather_rows(bf(sent), place).reshape(16, 40, 1152)
    merged_grad = got[:, :32, :1024].reshape(patches, 1024)
    kappa = got[:, :32, 1024:1025].reshape(patches, 1).astype(f32)
    grad_gain_feed = jnp.sum(got[:, 32, :1024].astype(f32), axis=0)
    grad_gain_attend = jnp.sum(got[:, 33, :1024].astype(f32), axis=0)

    grad_mixed = product_right(merged_grad, w_mixout)
    scaled_own = jnp.where(y == 0, scaled[:, :HDIM], scaled[:, HDIM:])
    grad_mixer_out = product_left(scaled_own, merged_grad)
    grad_gain_heads = jnp.sum(grad_mixed * gated, axis=0)
    grad_gated = grad_mixed * gain_heads - gated * kappa
    grad_gate_low = bf(grad_gated * mixer_rows * gate_sigm * (1.0 + gate_pre * (1.0 - gate_sigm)))
    (
        grad_input_pre,
        grad_state_pre,
        grad_step_pre,
        grad_taps,
        grad_state_taps,
        grad_bias,
        grad_log_rate,
        grad_skip,
    ) = core_pull(grad_gated * gate_silu)
    grad_input_low = bf(grad_input_pre)
    grad_state_low = bf(grad_state_pre)
    grad_step_low = bf(grad_step_pre)
    grad_normed = (
        product_right(jnp.concatenate([grad_gate_low, grad_input_low], axis=1), w_heads)
        + product_right(grad_state_low, w_state)
        + product_right(grad_step_low, w_step)
    )
    sums = scatter_rows(jnp.concatenate([grad_normed, grad_state_pre], axis=1), place)
    grad_hidden_part, gain_global_part = rms_back(hidden, gain_global, sums[:, :1024])
    hidden_rows = grad_merged + grad_hidden_part

    def own(pair):
        return jnp.where(y == 0, pair[0], pair[1])

    head_row = jnp.concatenate(
        [
            jnp.where(y == 0, grad_taps[:, :HDIM], grad_taps[:, HDIM:]).reshape(4 * HDIM),
            jnp.where(y == 0, grad_gain_heads[:HDIM], grad_gain_heads[HDIM:]),
            own(grad_bias)[None],
            own(grad_log_rate)[None],
            own(grad_skip)[None],
            jnp.zeros((1024 - 5 * HDIM - 3,), f32),
        ]
    )
    step_own = jnp.where(y == 0, grad_step_pre[:, 0], grad_step_pre[:, 1])
    small = jnp.stack(
        [
            gain_global_part,
            grad_state_taps.reshape(1024),
            head_row,
            jnp.concatenate([step_own, jnp.zeros((512,), f32)]),
        ]
    )
    sent = jnp.concatenate(
        [
            jnp.concatenate([hidden_rows, sums[:, 1024:]], axis=1),
            jnp.pad(small, ((0, 4), (0, 256))),
        ],
        axis=0,
    )
    got = gather_rows(bf(sent), place).reshape(16, 40, 1280)
    hidden_grad = got[:, :32, :1024].reshape(patches, 1024)
    state_grad = got[:, :32, 1024:].reshape(patches, 256)
    small = got[:, 32:36, :1024].astype(f32)
    grad_gain_global = jnp.sum(small[:, 0], axis=0)
    grad_conv_state = jnp.sum(small[:, 1], axis=0).reshape(4, 256)
    mine = pick(small.reshape(2, 2, 4, 4, 1024), c).transpose(1, 0, 2, 3).reshape(8, 4, 1024)
    grad_conv_input = mine[:, 2, : 4 * HDIM].reshape(8, 4, HDIM).transpose(1, 0, 2).reshape(4, 512)
    grad_gain_mixer = mine[:, 2, 4 * HDIM : 5 * HDIM].reshape(512)
    grad_step_bias = mine[:, 2, 5 * HDIM]
    grad_decay_log = mine[:, 2, 5 * HDIM + 1]
    grad_skip_gain = mine[:, 2, 5 * HDIM + 2]
    normed_cols = lax.dynamic_slice_in_dim(normed, s * 128, 128, 1)
    grad_mixer_step = product_right(normed_cols.T, bf(mine[:, 3, :512]))
    grad_mixer_state = product_left(normed_cols, state_grad)
    grad_patch_in = product_left(columns_in, hidden_grad)

    head_cols = jnp.concatenate(
        [
            jnp.where(y == 0, grad_gate_low[:, :HDIM], grad_gate_low[:, HDIM:]),
            jnp.where(y == 0, grad_input_low[:, :HDIM], grad_input_low[:, HDIM:]),
        ],
        axis=1,
    )
    grad_head_cols = bf(product_left(normed, head_cols)).reshape(8, 128, 128)
    grad_head_cols = exchange_seq(grad_head_cols, s).transpose(1, 0, 2).astype(f32)
    grad_mixer_gate = grad_head_cols[:, :, :HDIM].reshape(128, 512)
    grad_mixer_input = grad_head_cols[:, :, HDIM:].reshape(128, 512)

    back = bf(product_right(hidden_grad, patch_in)).reshape(32, 16, 256)
    back = lax.all_to_all(back, ("seq", "mp"), 0, 0, tiled=True)
    back = back.reshape(8, 4, 16, 256).transpose(2, 1, 0, 3).reshape(128, E)
    grad_rows = bf(grad_residual + back)
    grad_input = jnp.concatenate(select_blocks(gather_bytes(grad_rows), m, 4), axis=0)

    sum_qkv, sum_rest = (sum_qkv.astype(f32), sum_rest.astype(f32))
    return (
        byte_output,
        grad_input,
        grad_gain_global,
        grad_patch_in,
        grad_mixer_gate,
        grad_mixer_input,
        grad_mixer_state,
        grad_mixer_step,
        grad_conv_input,
        grad_conv_state,
        grad_step_bias,
        grad_decay_log,
        grad_skip_gain,
        grad_gain_mixer,
        grad_mixer_out,
        grad_patch_out,
        grad_gain_attend,
        sum_qkv[:, :256],
        sum_qkv[:, 256:512],
        sum_qkv[:, 512:],
        sum_rest[:32],
        grad_gain_feed,
        sum_gate.astype(f32),
        sum_up.astype(f32),
        sum_rest[32:],
    )


def solution(mesh):
    in_specs = (
        P("seq", None),
        P(),
        P("seq", None),
        P(),
        P(("mp", "seq"), None),
        P("seq", "mp"),
        P("seq", "mp"),
        P("seq", None),
        P("seq", "mp"),
        P(None, "mp"),
        P(),
        P("mp"),
        P("mp"),
        P("mp"),
        P("mp"),
        P(("mp", "seq"), None),
        P("seq", "mp"),
        P(),
        P("seq", "mp"),
        P("seq", "mp"),
        P("seq", "mp"),
        P(("mp", "seq"), None),
        P(),
        P("seq", "mp"),
        P("seq", "mp"),
        P(("mp", "seq"), None),
    )
    out_specs = (
        P("seq", None),
        P("seq", None),
        P(),
        P(("mp", "seq"), None),
        P("seq", "mp"),
        P("seq", "mp"),
        P("seq", None),
        P("seq", "mp"),
        P(None, "mp"),
        P(),
        P("mp"),
        P("mp"),
        P("mp"),
        P("mp"),
        P(("mp", "seq"), None),
        P("seq", "mp"),
        P(),
        P("seq", "mp"),
        P("seq", "mp"),
        P("seq", "mp"),
        P(("mp", "seq"), None),
        P(),
        P("seq", "mp"),
        P("seq", "mp"),
        P(("mp", "seq"), None),
    )
    plan = split_plan if (mesh.shape["seq"], mesh.shape["mp"]) == (8, 4) else gathered_plan
    return jax.shard_map(plan, mesh=mesh, in_specs=in_specs, out_specs=out_specs, check_vma=False)
```

```python
from functools import partial

import jax
import jax.numpy as jnp
from jax import lax
from jax.experimental import pallas as pl
from jax.experimental.pallas import tpu as pltpu
from jax.sharding import PartitionSpec as P

E = 1024
HDIM = 64
DI = 2048
NSTATE = 128
KCONV = 4
PATCH = 8
TOK_DEV = 512
BLOCK = 64


EPS = 1e-05
HIGH = lax.Precision.HIGHEST


def shifted(shard, axis, by):
    length = lax.axis_size(axis)
    pairs = [(i, i + by) for i in range(length) if 0 <= i + by < length]
    return lax.ppermute(shard, axis, pairs)


def prefix(shard, axis, combine, identity):
    length, position = (lax.axis_size(axis), lax.axis_index(axis))
    everything = jax.tree.map(
        lambda part, kind: lax.all_gather(part.astype(kind), axis),
        shard,
        (jnp.bfloat16, jnp.bfloat16),
    )
    start = jax.tree.map(
        lambda part, zero: jnp.broadcast_to(jnp.asarray(zero, part.dtype), part.shape),
        shard,
        identity,
    )

    def prefix_turn(k, before):
        reached = k < position
        new = combine(
            before, jax.tree.map(lambda part, own: part[k].astype(own.dtype), everything, shard)
        )
        return jax.tree.map(lambda a, b: jnp.where(reached, a, b), new, before)

    return lax.fori_loop(0, length, prefix_turn, start)


def carried_in(shard, axis, combine, identity):
    length, position = (lax.axis_size(axis), lax.axis_index(axis))
    everything = jax.tree.map(
        lambda part, kind: lax.all_gather(part.astype(kind), axis),
        shard,
        jax.tree.map(lambda a: jnp.bfloat16 if a.dtype == jnp.float32 else a.dtype, shard),
    )
    start = jax.tree.map(
        lambda part, zero: jnp.broadcast_to(jnp.asarray(zero, part.dtype), part.shape),
        shard,
        identity,
    )

    def carried_turn(k, before):
        at = length - 1 - k
        reached = at > position
        new = combine(
            before, jax.tree.map(lambda part, own: part[at].astype(own.dtype), everything, shard)
        )
        return jax.tree.map(lambda a, b: jnp.where(reached, a, b), new, before)

    return lax.fori_loop(0, length, carried_turn, start)


def product(former, latter):
    return jnp.dot(former, latter, preferred_element_type=jnp.float32)


def product_left(former, latter):
    return lax.dot_general(
        former, latter, (((0,), (0,)), ((), ())), preferred_element_type=jnp.float32
    )


def product_right(former, latter):
    return lax.dot_general(
        former, latter, (((1,), (1,)), ((), ())), preferred_element_type=jnp.float32
    )


def over_heads(partial_sum):
    return lax.psum(partial_sum, "mp")


def gather_slots(pieces):
    return lax.all_gather(pieces.astype(jnp.bfloat16), "mp", axis=1, tiled=True).astype(
        pieces.dtype
    )


def rms_scale(values, scale_gain):
    mean_square = jnp.mean(values * values, axis=-1, keepdims=True)
    return values * lax.rsqrt(mean_square + EPS) * scale_gain


def rms_back(values, scale_gain, upstream):
    pullback = jax.vjp(rms_scale, values, scale_gain)[1]
    return pullback(upstream)


def running_bounds(lengths):
    places = jnp.arange(lengths.shape[0])
    upto = places[None, :] <= places[:-1, None]
    return jnp.sum(jnp.where(upto, lengths[None, :], 0), axis=1)


def running_sum(values):
    places = jnp.arange(values.shape[0])
    lower_part = (places[:, None] >= places[None, :]).astype(jnp.float32)
    return jnp.dot(lower_part, values, precision=HIGH, preferred_element_type=jnp.float32)


def segment_of(lengths, start_row, row_count):
    bounds = running_bounds(lengths)
    places = start_row + jnp.arange(row_count, dtype=jnp.int32)
    return jnp.sum((places[:, None] >= bounds[None, :]).astype(jnp.int32), axis=1)


def conv_silu(extended, kernel, segment_rows):
    row_count = extended.shape[0] - KCONV + 1
    segment_now = segment_rows[KCONV - 1 :]
    summed = jnp.zeros((row_count, extended.shape[1]), jnp.float32)
    for offset in range(KCONV):
        same_seq = (segment_rows[offset : offset + row_count] == segment_now)[:, None]
        summed = (
            summed
            + jnp.where(same_seq, extended[offset : offset + row_count], 0.0) * kernel[offset]
        )
    return jax.nn.silu(summed)


def block_output(
    head_values,
    write_vecs,
    read_vecs,
    step_size,
    log_rate,
    skip_term,
    state_value,
    segment_rows,
    segment_prev,
):
    length = head_values.shape[0]
    running = running_sum(-step_size * jnp.exp(log_rate))
    places = jnp.arange(length)
    allowed = (places[:, None] >= places[None, :]) & (
        segment_rows[:, None] == segment_rows[None, :]
    )
    allowed = allowed[:, :, None]
    spread = jnp.where(allowed, running[:, None, :] - running[None, :, :], 0.0)
    factors = jnp.where(allowed, jnp.exp(spread), 0.0)
    affinity = jnp.dot(read_vecs, write_vecs.T, precision=HIGH, preferred_element_type=jnp.float32)
    mixing = factors * affinity[:, :, None] * step_size[None, :, :]
    inside = jnp.einsum("tsh,shp->thp", mixing, head_values, precision=HIGH)
    carried = jnp.where((segment_rows == segment_prev)[:, None], jnp.exp(running), 0.0)
    reading = (
        jnp.einsum("tn,hpn->thp", read_vecs, state_value, precision=HIGH) * carried[:, :, None]
    )
    result = inside + reading + skip_term[None, :, None] * head_values
    return result.reshape(length, -1)


def block_summary(head_values, write_vecs, step_size, log_rate, segment_rows, segment_prev):
    running = running_sum(-step_size * jnp.exp(log_rate))
    latest = running[-1]
    in_tail = (segment_rows == segment_rows[-1])[:, None]
    weights = jnp.where(in_tail, jnp.exp(latest[None, :] - running), 0.0) * step_size
    scaled = weights[:, :, None] * head_values
    state_local = jnp.einsum("shp,sn->hpn", scaled, write_vecs, precision=HIGH)
    decay_total = jnp.where(segment_rows[-1] == segment_prev, jnp.exp(latest), 0.0)
    return (decay_total, state_local)


def combine_state(earlier, later):
    return (earlier[0] * later[0], later[0][:, None, None] * earlier[1] + later[1])


def patch_attention(queries, keys_all, values_all):
    row_count = queries.shape[0]
    head_count = queries.shape[1] // HDIM
    query_rows = queries.reshape(row_count // PATCH, PATCH, head_count, HDIM)
    key_rows = keys_all.reshape(row_count // PATCH, PATCH, head_count, HDIM)
    value_rows = values_all.reshape(row_count // PATCH, PATCH, head_count, HDIM)
    scores = jnp.einsum("bihd,bjhd->bhij", query_rows, key_rows, precision=HIGH) * HDIM ** (-0.5)
    causal = jnp.arange(PATCH)[:, None] >= jnp.arange(PATCH)[None, :]
    scores = jnp.where(causal, scores, -1e30)
    peak = jnp.max(scores, axis=-1, keepdims=True)
    probs = jnp.exp(scores - peak)
    probs = probs / jnp.sum(probs, axis=-1, keepdims=True)
    context = jnp.einsum("bhij,bjhd->bihd", probs, value_rows, precision=HIGH)
    return context.reshape(row_count, head_count * HDIM)


def add_tail(main_rows, tail_rows):
    keep_count = main_rows.shape[0] - tail_rows.shape[0]
    return jnp.concatenate([main_rows[:keep_count], main_rows[keep_count:] + tail_rows], axis=0)


def gathered_plan(
    byte_input,
    seq_lengths,
    cotangent,
    gain_global,
    patch_in,
    mixer_gate,
    mixer_input,
    mixer_state,
    mixer_step,
    conv_input,
    conv_state,
    step_bias,
    decay_log,
    skip_gain,
    gain_mixer,
    mixer_out,
    patch_out,
    gain_attend,
    attend_query,
    attend_key,
    attend_value,
    attend_out,
    gain_feed,
    feed_gate,
    feed_up,
    feed_down,
):
    group_size = lax.axis_size("mp")
    slot_width = PATCH * E // group_size
    slot_start = lax.axis_index("mp") * slot_width
    first_row = lax.axis_index("seq") * BLOCK
    segment_ext = segment_of(seq_lengths, first_row - (KCONV - 1), BLOCK + KCONV - 1)
    segment_rows = segment_ext[KCONV - 1 :]
    segment_prev = segment_of(seq_lengths, first_row - 1, 1)[0]

    def fetch_global():
        return (
            lax.all_gather(patch_in, "seq", axis=0, tiled=True),
            lax.all_gather(mixer_gate, "seq", axis=0, tiled=True),
            lax.all_gather(mixer_input, "seq", axis=0, tiled=True),
            lax.all_gather(mixer_state, "seq", axis=0, tiled=True),
            lax.all_gather(mixer_step, "seq", axis=0, tiled=True),
            lax.all_gather(mixer_out, "seq", axis=0, tiled=True),
            lax.all_gather(patch_out, "seq", axis=0, tiled=True),
        )

    def fetch_local():
        return (
            lax.all_gather(attend_query, "seq", axis=0, tiled=True),
            lax.all_gather(attend_key, "seq", axis=0, tiled=True),
            lax.all_gather(attend_value, "seq", axis=0, tiled=True),
            lax.all_gather(attend_out, "seq", axis=0, tiled=True),
            lax.all_gather(feed_gate, "seq", axis=0, tiled=True),
            lax.all_gather(feed_up, "seq", axis=0, tiled=True),
            lax.all_gather(feed_down, "seq", axis=0, tiled=True),
        )

    def conv_of(extended, kernel):
        return conv_silu(extended, kernel, segment_ext)

    def summary_of(values_in, writes_in, steps_in, rates_in):
        return block_summary(values_in, writes_in, steps_in, rates_in, segment_rows, segment_prev)

    def output_of(values_in, writes_in, reads_in, steps_in, rates_in, skips_in, state_value):
        return block_output(
            values_in,
            writes_in,
            reads_in,
            steps_in,
            rates_in,
            skips_in,
            state_value,
            segment_rows,
            segment_prev,
        )

    full_patch_in, full_gate, full_input, full_state, full_step, full_mixout, full_patchout = (
        fetch_global()
    )
    patches = byte_input.reshape(BLOCK, PATCH * E)
    local_bytes = lax.dynamic_slice_in_dim(patches, slot_start, slot_width, 1)
    hidden = over_heads(product(local_bytes, full_patch_in))
    normed = rms_scale(hidden, gain_global).astype(jnp.bfloat16)
    gate_pre = product(normed, full_gate)
    input_pre = product(normed, full_input)
    state_pre = product(normed, full_state)
    step_pre = product(normed, full_step)
    rim_rows = shifted((input_pre[BLOCK - KCONV + 1 :], state_pre[BLOCK - KCONV + 1 :]), "seq", 1)
    input_ext = jnp.concatenate([rim_rows[0], input_pre], axis=0)
    state_ext = jnp.concatenate([rim_rows[1], state_pre], axis=0)
    input_conv = conv_of(input_ext, conv_input)
    state_conv = conv_of(state_ext, conv_state)
    step_size = jax.nn.softplus(step_pre + step_bias)
    head_count = step_size.shape[1]
    head_values = input_conv.reshape(BLOCK, head_count, HDIM)
    write_vecs = state_conv[:, :NSTATE]
    read_vecs = state_conv[:, NSTATE:]
    decay_total, state_local = summary_of(head_values, write_vecs, step_size, decay_log)
    identity = (jnp.ones_like(decay_total), jnp.zeros_like(state_local))
    state_in = prefix((decay_total, state_local), "seq", combine_state, identity)[1]
    mixer_rows = output_of(
        head_values, write_vecs, read_vecs, step_size, decay_log, skip_gain, state_in
    )
    gate_sigm = jax.nn.sigmoid(gate_pre)
    gate_silu = gate_pre * gate_sigm
    gated = mixer_rows * gate_silu
    mean_square = over_heads(jnp.sum(gated * gated, axis=-1, keepdims=True)) / DI
    root_inverse = lax.rsqrt(mean_square + EPS)
    mixed = (gated * root_inverse * gain_mixer).astype(jnp.bfloat16)
    merged = hidden + over_heads(product(mixed, full_mixout))
    merged_low = merged.astype(jnp.bfloat16)
    slot_values = gather_slots(product(merged_low, full_patchout)).reshape(TOK_DEV, E)
    residual = byte_input.astype(jnp.float32) + slot_values
    full_query, full_key, full_value, full_attout, full_feedgate, full_up, full_down = fetch_local()
    attend_in = rms_scale(residual, gain_attend).astype(jnp.bfloat16)
    queries = product(attend_in, full_query)
    keys_all = product(attend_in, full_key)
    values_all = product(attend_in, full_value)
    context = patch_attention(queries, keys_all, values_all).astype(jnp.bfloat16)
    middle = residual + over_heads(product(context, full_attout))
    feed_in = rms_scale(middle, gain_feed).astype(jnp.bfloat16)
    gate_value = product(feed_in, full_feedgate)
    up_value = product(feed_in, full_up)
    gate_sig = jax.nn.sigmoid(gate_value)
    hidden_units = (gate_value * gate_sig * up_value).astype(jnp.bfloat16)
    byte_output = middle + over_heads(product(hidden_units, full_down))
    full_query, full_key, full_value, full_attout, full_feedgate, full_up, full_down = fetch_local()
    out_low = cotangent.astype(jnp.bfloat16)
    grad_feed_down = product_left(hidden_units, out_low)
    grad_units = product_right(out_low, full_down)
    grad_gate_value = (
        grad_units * up_value * gate_sig * (1.0 + gate_value * (1.0 - gate_sig))
    ).astype(jnp.bfloat16)
    grad_up_value = (grad_units * gate_value * gate_sig).astype(jnp.bfloat16)
    grad_feed_gate = product_left(feed_in, grad_gate_value)
    grad_feed_up = product_left(feed_in, grad_up_value)
    grad_feed_in = over_heads(
        product_right(grad_gate_value, full_feedgate) + product_right(grad_up_value, full_up)
    )
    grad_middle_part, grad_gain_feed = rms_back(middle, gain_feed, grad_feed_in)
    grad_middle = cotangent + grad_middle_part
    middle_low = grad_middle.astype(jnp.bfloat16)
    grad_attend_out = product_left(context, middle_low)
    grad_context = product_right(middle_low, full_attout)
    attention_pull = jax.vjp(patch_attention, queries, keys_all, values_all)[1]
    grad_query_raw, grad_key_raw, grad_value_raw = attention_pull(grad_context)
    grad_query_rows = grad_query_raw.astype(jnp.bfloat16)
    grad_key_rows = grad_key_raw.astype(jnp.bfloat16)
    grad_value_rows = grad_value_raw.astype(jnp.bfloat16)
    grad_attend_query = product_left(attend_in, grad_query_rows)
    grad_attend_key = product_left(attend_in, grad_key_rows)
    grad_attend_value = product_left(attend_in, grad_value_rows)
    grad_attend_in = over_heads(
        product_right(grad_query_rows, full_query)
        + product_right(grad_key_rows, full_key)
        + product_right(grad_value_rows, full_value)
    )
    grad_residual_part, grad_gain_attend = rms_back(residual, gain_attend, grad_attend_in)
    grad_residual = grad_middle + grad_residual_part
    local_sums = (
        lax.psum_scatter(grad_attend_query, "seq", scatter_dimension=0, tiled=True),
        lax.psum_scatter(grad_attend_key, "seq", scatter_dimension=0, tiled=True),
        lax.psum_scatter(grad_attend_value, "seq", scatter_dimension=0, tiled=True),
        lax.psum_scatter(grad_attend_out, "seq", scatter_dimension=0, tiled=True),
        lax.psum_scatter(grad_feed_gate, "seq", scatter_dimension=0, tiled=True),
        lax.psum_scatter(grad_feed_up, "seq", scatter_dimension=0, tiled=True),
        lax.psum_scatter(grad_feed_down, "seq", scatter_dimension=0, tiled=True),
    )
    full_patch_in, full_gate, full_input, full_state, full_step, full_mixout, full_patchout = (
        fetch_global()
    )
    residual_patches = grad_residual.reshape(BLOCK, PATCH * E)
    slot_grad = lax.dynamic_slice_in_dim(residual_patches, slot_start, slot_width, 1).astype(
        jnp.bfloat16
    )
    grad_patch_out = product_left(merged_low, slot_grad)
    grad_merged = over_heads(product_right(slot_grad, full_patchout))
    merged_grad_low = grad_merged.astype(jnp.bfloat16)
    grad_mixer_out = product_left(mixed, merged_grad_low)
    grad_mixed = product_right(merged_grad_low, full_mixout)
    grad_gain_mixer = jnp.sum(grad_mixed * gated * root_inverse, axis=0)
    scaled_grad = grad_mixed * gain_mixer
    inner_dot = over_heads(jnp.sum(scaled_grad * gated, axis=-1, keepdims=True))
    grad_gated = scaled_grad * root_inverse - gated * inner_dot * root_inverse**3 / DI
    grad_mixer_rows = grad_gated * gate_silu
    grad_gate_pre = grad_gated * mixer_rows * gate_sigm * (1.0 + gate_pre * (1.0 - gate_sigm))
    output_pull = jax.vjp(
        output_of, head_values, write_vecs, read_vecs, step_size, decay_log, skip_gain, state_in
    )[1]
    (
        grad_values_a,
        grad_writes_a,
        grad_reads,
        grad_steps_a,
        grad_rates_a,
        grad_skip_gain,
        grad_state_in,
    ) = output_pull(grad_mixer_rows)
    state_end = carried_in((decay_total, grad_state_in), "seq", combine_state, identity)[1]
    summary_pull = jax.vjp(summary_of, head_values, write_vecs, step_size, decay_log)[1]
    grad_values_b, grad_writes_b, grad_steps_b, grad_rates_b = summary_pull(
        (jnp.sum(state_end * state_in, axis=(1, 2)), state_end)
    )
    grad_input_conv = (grad_values_a + grad_values_b).reshape(BLOCK, -1)
    grad_state_conv = over_heads(
        jnp.concatenate([grad_writes_a + grad_writes_b, grad_reads], axis=1)
    )
    grad_step_pre = (grad_steps_a + grad_steps_b) * jax.nn.sigmoid(step_pre + step_bias)
    grad_step_bias = jnp.sum(grad_step_pre, axis=0)
    grad_decay_log = grad_rates_a + grad_rates_b
    grad_input_ext, grad_conv_input = jax.vjp(conv_of, input_ext, conv_input)[1](grad_input_conv)
    grad_state_ext, grad_conv_state = jax.vjp(conv_of, state_ext, conv_state)[1](grad_state_conv)
    rim_back = shifted((grad_input_ext[: KCONV - 1], grad_state_ext[: KCONV - 1]), "seq", -1)
    grad_input_low = add_tail(grad_input_ext[KCONV - 1 :], rim_back[0]).astype(jnp.bfloat16)
    grad_state_low = add_tail(grad_state_ext[KCONV - 1 :], rim_back[1]).astype(jnp.bfloat16)
    grad_gate_low = grad_gate_pre.astype(jnp.bfloat16)
    grad_step_low = grad_step_pre.astype(jnp.bfloat16)
    grad_mixer_gate = product_left(normed, grad_gate_low)
    grad_mixer_input = product_left(normed, grad_input_low)
    grad_mixer_state = product_left(normed, grad_state_low)
    grad_mixer_step = product_left(normed, grad_step_low)
    head_part = over_heads(
        product_right(grad_gate_low, full_gate)
        + product_right(grad_input_low, full_input)
        + product_right(grad_step_low, full_step)
    )
    grad_normed = head_part + product_right(grad_state_low, full_state)
    grad_hidden_part, grad_gain_global = rms_back(hidden, gain_global, grad_normed)
    hidden_grad_low = (grad_merged + grad_hidden_part).astype(jnp.bfloat16)
    grad_patch_in = product_left(local_bytes, hidden_grad_low)
    grad_byte_part = gather_slots(product_right(hidden_grad_low, full_patch_in)).reshape(TOK_DEV, E)
    grad_input = (grad_residual + grad_byte_part).astype(jnp.bfloat16)
    global_sums = (
        lax.psum_scatter(grad_patch_in, "seq", scatter_dimension=0, tiled=True),
        lax.psum_scatter(grad_mixer_gate, "seq", scatter_dimension=0, tiled=True),
        lax.psum_scatter(grad_mixer_input, "seq", scatter_dimension=0, tiled=True),
        lax.psum_scatter(grad_mixer_state, "seq", scatter_dimension=0, tiled=True),
        lax.psum_scatter(grad_mixer_step, "seq", scatter_dimension=0, tiled=True),
        lax.psum_scatter(grad_mixer_out, "seq", scatter_dimension=0, tiled=True),
        lax.psum_scatter(grad_patch_out, "seq", scatter_dimension=0, tiled=True),
    )
    small_sums = lax.psum(
        (
            grad_gain_global,
            grad_conv_input,
            grad_conv_state,
            grad_step_bias,
            grad_decay_log,
            grad_skip_gain,
            grad_gain_mixer,
            grad_gain_attend,
            grad_gain_feed,
        ),
        "seq",
    )
    return (
        byte_output.astype(jnp.bfloat16),
        grad_input,
        small_sums[0],
        global_sums[0],
        global_sums[1],
        global_sums[2],
        global_sums[3],
        global_sums[4],
        small_sums[1],
        small_sums[2],
        small_sums[3],
        small_sums[4],
        small_sums[5],
        small_sums[6],
        global_sums[5],
        global_sums[6],
        small_sums[7],
        local_sums[0],
        local_sums[1],
        local_sums[2],
        local_sums[3],
        small_sums[8],
        local_sums[4],
        local_sums[5],
        local_sums[6],
    )


ROWS = 512
HALF = 256
VMEM_BYTES = 56 * 1024 * 1024


def bf(values):
    return values.astype(jnp.bfloat16)


def up(values):
    return values.astype(jnp.float32)


def whole(shape):
    return pl.BlockSpec(shape, lambda *_: (0,) * len(shape))


def scalars():
    return pl.BlockSpec(memory_space=pltpu.SMEM)


def kernel_params(count=1):
    return pltpu.CompilerParams(
        vmem_limit_bytes=VMEM_BYTES, dimension_semantics=("arbitrary",) * count
    )


def cost(flops, size):
    return pl.CostEstimate(flops=flops, bytes_accessed=size, transcendentals=0)


def block_index(place, k):
    c, y = (place[0], place[1])
    c = 1 - c if k >= 2 else c
    y = 1 - y if k % 2 else y
    return c * 2 + y


def put_pieces(place, pieces, out_ref, rows=128):
    for k, piece in enumerate(pieces):
        at = pl.multiple_of(block_index(place, k) * rows, rows)
        out_ref[pl.ds(at, rows), :] = piece[:rows, :]


def lane_of(values, lane):
    lanes = lax.broadcasted_iota(jnp.int32, values.shape, 1)
    return jnp.sum(jnp.where(lanes == lane, values, 0.0), axis=1, keepdims=True)


def segments(lengths, shift, shape, axis):
    rows = lax.broadcasted_iota(jnp.int32, shape, axis) - shift
    total = jnp.zeros(shape, jnp.int32)
    bound = 0
    for k in range(lengths.shape[0] - 1):
        bound = bound + lengths[k]
        total = total + (rows >= bound).astype(jnp.int32)
    return total


def tap_masks(lengths):
    here = segments(lengths, 0, (ROWS, 1), 0)
    rows = lax.broadcasted_iota(jnp.int32, (ROWS, 1), 0)
    return [
        up((rows >= j) & (segments(lengths, j, (ROWS, 1), 0) == here))
        for j in range(1, KCONV)
    ]


def conv_rows(values, taps, masks):
    total = values * taps[KCONV - 1 : KCONV, :]
    for j in range(1, KCONV):
        earlier = pltpu.roll(values, j, 0) * masks[j - 1]
        total = total + earlier * taps[KCONV - 1 - j : KCONV - j, :]
    return total


def conv_back(values, taps, masks, grads):
    rows_grad = grads * taps[KCONV - 1 : KCONV, :]
    taps_grad = [None] * KCONV
    taps_grad[KCONV - 1] = jnp.sum(grads * values, axis=0, keepdims=True)
    for j in range(1, KCONV):
        masked = grads * masks[j - 1]
        rows_grad = rows_grad + pltpu.roll(masked, ROWS - j, 0) * taps[
            KCONV - 1 - j : KCONV - j, :
        ]
        taps_grad[KCONV - 1 - j] = jnp.sum(
            masked * pltpu.roll(values, j, 0), axis=0, keepdims=True
        )
    return rows_grad, taps_grad


def silu_parts(values):
    gate = 1.0 / (1.0 + jnp.exp(-values))
    return values * gate, gate * (1.0 + values * (1.0 - gate))


def softplus(values):
    return jnp.maximum(values, 0.0) + jnp.log1p(jnp.exp(-jnp.abs(values)))


def lower(shape, flip=False):
    rows = lax.broadcasted_iota(jnp.int32, shape, 0)
    columns = lax.broadcasted_iota(jnp.int32, shape, 1)
    return up(rows <= columns) if flip else up(rows >= columns)


def allowed_pairs(lengths):
    rows = lax.broadcasted_iota(jnp.int32, (ROWS, ROWS), 0)
    columns = lax.broadcasted_iota(jnp.int32, (ROWS, ROWS), 1)
    same = segments(lengths, 0, (ROWS, 1), 0) == segments(lengths, 0, (1, ROWS), 1)
    return (rows >= columns) & same


def decay_block(run, run_row, r):
    spread = run[r * HALF : (r + 1) * HALF, :] - run_row[:, : (r + 1) * HALF]
    return jnp.exp(jnp.minimum(spread, 0.0))


def head_columns(j, i, table):
    return lane_of(table, 2 * j + i)


def by_head(first, second):
    lanes = lax.broadcasted_iota(jnp.int32, (1, 2 * HDIM), 1)
    return jnp.where(lanes < HDIM, first, second)


def shared_setup(
    j, lengths, pre_ref, state_taps, params, affinity, step_ref, run_ref, run_t, wr_ref, mask_ref
):
    @pl.when(j == 0)
    def _():
        step = softplus(pre_ref[:, 1280:] + params[0:1, :])
        step_ref[...] = step
        running = jnp.dot(
            lower((ROWS, ROWS)), -step * jnp.exp(params[1:2, :]), precision=HIGH,
            preferred_element_type=jnp.float32,
        )
        run_ref[...] = running
        run_t[...] = running.T
        masks = [jnp.broadcast_to(mask, (ROWS, 128)) for mask in tap_masks(lengths)]
        for k in range(KCONV - 1):
            mask_ref[k] = masks[k]
        masks = [jnp.concatenate([mask, mask], axis=1) for mask in masks]
        state = silu_parts(conv_rows(pre_ref[:, 1024:1280], state_taps[...], masks))[0]
        wr_ref[...] = bf(state)
        pairs = product_right(bf(state[:, NSTATE:]), bf(state[:, :NSTATE]))
        affinity[...] = jnp.where(allowed_pairs(lengths), pairs, 0.0)


def start_weights(place, pieces, weights, arrived):
    copies = []
    for v, piece in enumerate(pieces):
        at = pl.multiple_of(place[2 + v] * 128 + (64 if v == 8 else 0), 64)
        target = weights.at[pl.ds(at, piece.shape[0]), :]
        copies.append(pltpu.make_async_copy(piece, target, arrived.at[v]))
    for copy in copies:
        copy.start()
    return copies


def put_mix_out(weights, mix_out):
    for s in range(8):
        rows = slice(s * HDIM, (s + 1) * HDIM)
        mix_out[rows, :512] = weights[s * 128 : s * 128 + 64, 1408:]
        mix_out[rows, 512:] = weights[s * 128 + 64 : (s + 1) * 128, 1408:]


def mixer_forward_kernel(
    place, lengths, p0, p1, p2, p3, table, state_taps, params, w0, w1, w2, w3, w4, w5, w6, w7, w8,
    send, keep, normed, pre, inside, scaled,
    affinity, step_ref, run_ref, run_t, wr_ref, mask_ref, squares, mix_out,
    weights, arrived,
):
    j = pl.program_id(0)

    @pl.when(j == 0)
    def _():
        copies = start_weights(place, (w0, w1, w2, w3, w4, w5, w6, w7, w8), weights, arrived)
        put_pieces(place, (p0, p1, p2, p3), normed)
        for copy in copies:
            copy.wait()
        pre[...] = product(normed[...], weights[:, :1408])
        put_mix_out(weights, mix_out)
        squares[...] = jnp.zeros_like(squares)

    shared_setup(j, lengths, pre, state_taps, params, affinity, step_ref, run_ref, run_t, wr_ref, mask_ref)
    columns = pl.ds(pl.multiple_of(j * 128, 128), 128)
    masks = [mask_ref[k] for k in range(KCONV - 1)]
    values = silu_parts(
        conv_rows(pre[:, pl.ds(pl.multiple_of(512 + j * 128, 128), 128)], table[:, columns], masks)
    )[0]
    step = by_head(*[head_columns(j, i, step_ref[...]) for i in range(2)])
    steps = bf(values * step)
    for i in range(2):
        run = head_columns(j, i, run_ref[...])
        run_row = run_t[pl.ds(2 * j + i, 1), :]
        for r in range(2):
            seen = (r + 1) * HALF
            mixing = bf(
                affinity[r * HALF : seen, :seen] * decay_block(run, run_row, r)
            )
            inner = product(mixing, steps[:seen, i * HDIM : (i + 1) * HDIM])
            if i == 0:
                inside[r * HALF : seen, columns] = jnp.concatenate([inner, inner], axis=1)
            else:
                kept = inside[r * HALF : seen, columns]
                inside[r * HALF : seen, columns] = by_head(
                    kept, jnp.concatenate([inner, inner], axis=1)
                )
    skip = by_head(*[head_columns(j, i, params[2:3, :]) for i in range(2)])
    rows = inside[:, columns] + skip * values
    gated = rows * silu_parts(pre[:, columns])[0]
    scaled[:, columns] = bf(gated * table[4:5, columns])
    squares[...] += jnp.broadcast_to(jnp.sum(gated * gated, axis=1, keepdims=True), (ROWS, 128))

    @pl.when(j == 3)
    def _():
        for out, half in ((send, 1 - place[0]), (keep, place[0])):
            at = pl.ds(pl.multiple_of(half * HALF, HALF), HALF)
            out[:, :1024] = bf(product(scaled[at, :], mix_out[...]))
            out[:, 1024:] = bf(squares[at, :])


def mixer_forward(place, lengths, pieces, weights, table, state_taps, params):
    f32, low = (jnp.float32, jnp.bfloat16)
    shapes = [
        ((HALF, 1152), low),
        ((HALF, 1152), low),
        ((ROWS, 1024), low),
        ((ROWS, 1408), f32),
        ((ROWS, 512), f32),
        ((ROWS, 512), low),
    ]
    return pl.pallas_call(
        mixer_forward_kernel,
        grid=(4,),
        in_specs=[scalars(), scalars()]
        + [whole(a.shape) for a in (*pieces, table, state_taps, params)]
        + [pl.BlockSpec(memory_space=pl.ANY)] * 9,
        out_specs=[whole(s) for s, _ in shapes],
        out_shape=[jax.ShapeDtypeStruct(s, t) for s, t in shapes],
        scratch_shapes=[
            pltpu.VMEM((ROWS, ROWS), f32),
            pltpu.VMEM((ROWS, 128), f32),
            pltpu.VMEM((ROWS, 128), f32),
            pltpu.VMEM((128, ROWS), f32),
            pltpu.VMEM((ROWS, 256), low),
            pltpu.VMEM((KCONV - 1, ROWS, 128), f32),
            pltpu.VMEM((ROWS, 128), f32),
            pltpu.VMEM((512, 1024), low),
            pltpu.VMEM((1024, 1920), low),
            pltpu.SemaphoreType.DMA((9,)),
        ],
        compiler_params=kernel_params(),
        cost_estimate=cost(14_000_000_000, 10_000_000),
        name="mixer_forward",
    )(place, lengths, *pieces, table, state_taps, params, *weights)


def mixer_backward_kernel(
    place, lengths, g0, g1, g2, g3, table, state_taps, params, pre, inside,
    w0, w1, w2, w3, w4, w5, w6, w7, w8,
    send, keep, grads, merged, table_grad, state_taps_grad, params_grad,
    grad_mixed, kappa, affinity, step_ref, run_ref, run_t, wr_ref, mask_ref, pair_grad, run_grad, step_grad,
    mix_out, weights, arrived,
):
    j = pl.program_id(0)
    pieces = (w0, w1, w2, w3, w4, w5, w6, w7, w8)

    @pl.when(j == 0)
    def _():
        for copy in start_weights(place, pieces, weights, arrived):
            copy.wait()

    shared_setup(j, lengths, pre, state_taps, params, affinity, step_ref, run_ref, run_t, wr_ref, mask_ref)

    @pl.when(j == 0)
    def _():
        for k, piece in enumerate((g0, g1, g2, g3)):
            at = pl.ds(pl.multiple_of(block_index(place, k) * 128, 128), 128)
            merged[at, :] = piece[:128, :1024]
            kappa[at, :] = up(piece[:128, 1024:])
        put_mix_out(weights, mix_out)
        grad_mixed[...] = product_right(merged[...], mix_out[...])
        pair_grad[...] = jnp.zeros_like(pair_grad)
        run_grad[...] = jnp.zeros_like(run_grad)
        step_grad[...] = jnp.zeros_like(step_grad)
        params_grad[...] = jnp.zeros_like(params_grad)
        table_grad[...] = jnp.zeros_like(table_grad)
        state_taps_grad[...] = jnp.zeros_like(state_taps_grad)

    columns = pl.ds(pl.multiple_of(j * 128, 128), 128)
    columns_in = pl.ds(pl.multiple_of(512 + j * 128, 128), 128)
    masks = [mask_ref[k] for k in range(KCONV - 1)]
    taps = table[:, columns]
    before = pre[:, columns_in]
    values, values_slope = silu_parts(conv_rows(before, taps, masks))
    step = by_head(*[head_columns(j, i, step_ref[...]) for i in range(2)])
    skip = by_head(*[head_columns(j, i, params[2:3, :]) for i in range(2)])
    steps = bf(values * step)
    gate, gate_slope = silu_parts(pre[:, columns])
    within = inside[:, columns]
    rows = within + skip * values
    gated = rows * gate
    mixed_grad = grad_mixed[:, columns]
    gain_grad = jnp.sum(mixed_grad * gated, axis=0, keepdims=True)
    gated_grad = mixed_grad * table[4:5, columns] - gated * kappa[...]
    grads[:, columns] = bf(gated_grad * rows * gate_slope)
    rows_grad = gated_grad * gate
    rows_low = bf(rows_grad)
    rows_turned = rows_low.T
    steps_grads = []
    for i in range(2):
        run = head_columns(j, i, run_ref[...])
        run_row = run_t[pl.ds(2 * j + i, 1), :]
        lanes = slice(i * HDIM, (i + 1) * HDIM)
        turned = jnp.zeros((HDIM, ROWS), jnp.float32)
        for r in range(2):
            seen = (r + 1) * HALF
            block = slice(r * HALF, seen)
            decay = decay_block(run, run_row, r)
            mixing = bf(affinity[block, :seen] * decay)
            mixing_grad = product_right(rows_low[block, lanes], steps[:seen, lanes])
            pair_grad[block, :seen] += mixing_grad * decay
            part = product(rows_turned[lanes, block], mixing)
            if seen < ROWS:
                part = jnp.concatenate(
                    [part, jnp.zeros((HDIM, ROWS - seen), jnp.float32)], axis=1
                )
            turned = turned + part
        steps_grads.append(turned)
    steps_grad = jnp.concatenate(steps_grads, axis=0).T
    lanes_in = lax.broadcasted_iota(jnp.int32, (128, 128), 0)
    lanes_out = lax.broadcasted_iota(jnp.int32, (128, 128), 1)
    to_head = up(lanes_out == 2 * j + lanes_in // HDIM)

    def head_sums(columns_of):
        return jnp.dot(columns_of, to_head, precision=HIGH, preferred_element_type=jnp.float32)

    run_grad[...] += head_sums(up(rows_low) * within - up(steps) * steps_grad)
    step_grad[...] += head_sums(steps_grad * values)
    params_grad[2:3, :] += jnp.sum(head_sums(rows_grad * values), axis=0, keepdims=True)
    conv_grad = (steps_grad * step + skip * rows_grad) * values_slope
    before_grad, taps_grad = conv_back(before, taps, masks, conv_grad)
    grads[:, columns_in] = bf(before_grad)
    for k in range(KCONV):
        table_grad[k : k + 1, columns] = taps_grad[k]
    table_grad[4:5, columns] = gain_grad

    @pl.when(j == 3)
    def _():
        decay_grad = jnp.dot(
            lower((ROWS, ROWS), True), run_grad[...], precision=HIGH,
            preferred_element_type=jnp.float32,
        )
        rate = jnp.exp(params[1:2, :])
        step_total = step_grad[...] - decay_grad * rate
        slope = 1.0 / (1.0 + jnp.exp(-(pre[:, 1280:] + params[0:1, :])))
        lanes = lax.broadcasted_iota(jnp.int32, (1, 128), 1)
        step_total = jnp.where(lanes < 8, step_total * slope, 0.0)
        grads[:, 1280:] = bf(step_total)
        params_grad[0:1, :] = jnp.sum(step_total, axis=0, keepdims=True)
        params_grad[1:2, :] = jnp.sum(
            -decay_grad * step_ref[...] * rate, axis=0, keepdims=True
        )
        pairs = jnp.where(allowed_pairs(lengths), pair_grad[...], 0.0)
        read_grad = product(bf(pairs), wr_ref[:, :NSTATE])
        write_grad = product(bf(pairs.T), wr_ref[:, NSTATE:])
        wide = [jnp.concatenate([mask, mask], axis=1) for mask in masks]
        state_before = pre[:, 1024:1280]
        state_slope = silu_parts(conv_rows(state_before, state_taps[...], wide))[1]
        state_grad, state_taps_parts = conv_back(
            state_before,
            state_taps[...],
            wide,
            jnp.concatenate([write_grad, read_grad], axis=1) * state_slope,
        )
        grads[:, 1024:1280] = bf(state_grad)
        for k in range(KCONV):
            state_taps_grad[k : k + 1, :] = state_taps_parts[k]
        for out, half in ((send, 1 - place[0]), (keep, place[0])):
            at = pl.ds(pl.multiple_of(half * HALF, HALF), HALF)
            out[:, :1024] = bf(product_right(grads[at, :], weights[:, :1408]))
            out[:, 1024:] = grads[at, 1024:1280]


def mixer_backward(place, lengths, pieces, weights, table, state_taps, params, pre, inside):
    f32, low = (jnp.float32, jnp.bfloat16)
    shapes = [
        ((HALF, 1280), low),
        ((HALF, 1280), low),
        ((ROWS, 1408), low),
        ((ROWS, 1024), low),
        ((8, 512), f32),
        ((8, 256), f32),
        ((8, 128), f32),
    ]
    operands = (*pieces, table, state_taps, params, pre, inside)
    return pl.pallas_call(
        mixer_backward_kernel,
        grid=(4,),
        in_specs=[scalars(), scalars()]
        + [whole(a.shape) for a in operands]
        + [pl.BlockSpec(memory_space=pl.ANY)] * 9,
        out_specs=[whole(s) for s, _ in shapes],
        out_shape=[jax.ShapeDtypeStruct(s, t) for s, t in shapes],
        scratch_shapes=[
            pltpu.VMEM((ROWS, 512), f32),
            pltpu.VMEM((ROWS, 128), f32),
            pltpu.VMEM((ROWS, ROWS), f32),
            pltpu.VMEM((ROWS, 128), f32),
            pltpu.VMEM((ROWS, 128), f32),
            pltpu.VMEM((128, ROWS), f32),
            pltpu.VMEM((ROWS, 256), low),
            pltpu.VMEM((KCONV - 1, ROWS, 128), f32),
            pltpu.VMEM((ROWS, ROWS), f32),
            pltpu.VMEM((ROWS, 128), f32),
            pltpu.VMEM((ROWS, 128), f32),
            pltpu.VMEM((512, 1024), low),
            pltpu.VMEM((1024, 1920), low),
            pltpu.SemaphoreType.DMA((9,)),
        ],
        compiler_params=kernel_params(),
        cost_estimate=cost(22_000_000_000, 14_000_000),
        name="mixer_backward",
    )(place, lengths, *operands, *weights)


def patch_mask():
    rows = lax.broadcasted_iota(jnp.int32, (128, 128), 0)
    columns = lax.broadcasted_iota(jnp.int32, (128, 128), 1)
    return (rows >= columns) & (rows // PATCH == columns // PATCH)


def patch_probs(queries, keys, mask):
    scores = product_right(queries, keys) * HDIM ** (-0.5)
    scores = jnp.where(mask, scores, -1e30)
    weights = jnp.exp(scores - jnp.max(scores, axis=1, keepdims=True))
    return weights / jnp.sum(weights, axis=1, keepdims=True)


def split_blocks(values, keep, send):
    for k, out in ((0, keep), (1, send), (2, keep), (3, send)):
        out[k // 2] = bf(values[k * 128 : (k + 1) * 128, :])


def put_w_out(weights, w_out):
    for s in range(8):
        for q in range(4):
            at = s * 128 + q * 32
            w_out[s * 32 : (s + 1) * 32, q * 256 : (q + 1) * 256] = weights[at : at + 32, 768:]


def attend_forward_kernel(
    place, x0, x1, x2, x3, w0, w1, w2, w3, w4, w5, w6, w7, w8,
    keep, send, rows, qkv, context, w_out, weights, arrived,
):
    for copy in start_weights(place, (w0, w1, w2, w3, w4, w5, w6, w7, w8), weights, arrived):
        copy.wait()
    put_w_out(weights, w_out)
    for k, piece in enumerate((x0, x1, x2, x3)):
        rows[k * 128 : (k + 1) * 128, :] = piece[...]
    qkv[...] = bf(product(rows[...], weights[:, :768]))
    mask = patch_mask()
    for b in range(4):
        at = slice(b * 128, (b + 1) * 128)
        outs = []
        for h in range(4):
            q, k, v = (qkv[at, n * 256 + h * HDIM : n * 256 + (h + 1) * HDIM] for n in range(3))
            outs.append(product(bf(patch_probs(q, k, mask)), v))
        context[at, :] = bf(jnp.concatenate(outs, axis=1))
    split_blocks(product(context[...], w_out[...]), keep, send)


def attend_forward(place, pieces, weights):
    low = jnp.bfloat16
    shapes = [(2, 128, 1024), (2, 128, 1024), (ROWS, 1024), (ROWS, 768), (ROWS, 256)]
    return pl.pallas_call(
        attend_forward_kernel,
        grid=(1,),
        in_specs=[scalars()]
        + [whole(a.shape) for a in pieces]
        + [pl.BlockSpec(memory_space=pl.ANY)] * 9,
        out_specs=[whole(s) for s in shapes],
        out_shape=[jax.ShapeDtypeStruct(s, low) for s in shapes],
        compiler_params=pltpu.CompilerParams(vmem_limit_bytes=VMEM_BYTES),
        scratch_shapes=[
            pltpu.VMEM((256, 1024), low),
            pltpu.VMEM((1024, 1024), low),
            pltpu.SemaphoreType.DMA((9,)),
        ],
        cost_estimate=cost(8_000_000_000, 7_000_000),
        name="attend_forward",
    )(place, *pieces, *weights)


def attend_backward_kernel(
    place, g0, g1, g2, g3, qkv, w0, w1, w2, w3, w4, w5, w6, w7, w8,
    keep, send, rows, qkv_grad, w_out, weights, arrived,
):
    for copy in start_weights(place, (w0, w1, w2, w3, w4, w5, w6, w7, w8), weights, arrived):
        copy.wait()
    put_w_out(weights, w_out)
    for k, piece in enumerate((g0, g1, g2, g3)):
        rows[k * 128 : (k + 1) * 128, :] = piece[...]
    context_grad = product_right(rows[...], w_out[...])
    mask = patch_mask()
    for b in range(4):
        at = slice(b * 128, (b + 1) * 128)
        outs = [[], [], []]
        for h in range(4):
            q, k, v = (qkv[at, n * 256 + h * HDIM : n * 256 + (h + 1) * HDIM] for n in range(3))
            probs = patch_probs(q, k, mask)
            grad = bf(context_grad[at, h * HDIM : (h + 1) * HDIM])
            probs_grad = product_right(grad, v)
            mean = jnp.sum(probs * probs_grad, axis=1, keepdims=True)
            scores_grad = probs * (probs_grad - mean) * HDIM ** (-0.5)
            outs[0].append(product(bf(scores_grad), k))
            outs[1].append(product(bf(scores_grad.T), q))
            outs[2].append(product(bf(probs.T), grad))
        qkv_grad[at, :] = bf(jnp.concatenate(outs[0] + outs[1] + outs[2], axis=1))
    split_blocks(product_right(qkv_grad[...], weights[:, :768]), keep, send)


def attend_backward(place, pieces, qkv, weights):
    low = jnp.bfloat16
    shapes = [(2, 128, 1024), (2, 128, 1024), (ROWS, 1024), (ROWS, 768)]
    return pl.pallas_call(
        attend_backward_kernel,
        grid=(1,),
        in_specs=[scalars()]
        + [whole(a.shape) for a in (*pieces, qkv)]
        + [pl.BlockSpec(memory_space=pl.ANY)] * 9,
        out_specs=[whole(s) for s in shapes],
        out_shape=[jax.ShapeDtypeStruct(s, low) for s in shapes],
        compiler_params=pltpu.CompilerParams(vmem_limit_bytes=VMEM_BYTES),
        scratch_shapes=[
            pltpu.VMEM((256, 1024), low),
            pltpu.VMEM((1024, 1024), low),
            pltpu.SemaphoreType.DMA((9,)),
        ],
        cost_estimate=cost(11_000_000_000, 7_000_000),
        name="attend_backward",
    )(place, *pieces, qkv, *weights)


def feed_kernel(
    place, x0, x1, x2, x3, out_grad, w0, w1, w2, w3, w4, w5, w6, w7, w8,
    keep, send, out_keep, out_send, rows, hidden, gate_grad, up_grad,
    weights, total, total_out, arrived,
):
    j = pl.program_id(0)

    @pl.when(j == 0)
    def _():
        pieces = (w0, w1, w2, w3, w4, w5, w6, w7, w8)
        copies = start_weights(place, pieces, weights, arrived)
        for k, piece in enumerate((x0, x1, x2, x3)):
            rows[k * 128 : (k + 1) * 128, :] = piece[...]
        total[...] = jnp.zeros_like(total)
        total_out[...] = jnp.zeros_like(total_out)
        for copy in copies:
            copy.wait()

    chunk = pl.multiple_of(j * 256, 256)
    w_gate = weights[:, pl.ds(chunk, 256)]
    w_up = weights[:, pl.ds(pl.multiple_of(1024 + chunk, 256), 256)]
    w_down = weights[pl.ds(chunk, 256), 2048:]
    gate, slope = silu_parts(product(rows[...], w_gate))
    lift = product(rows[...], w_up)
    units = bf(gate * lift)
    hidden[...] = units
    units_grad = product_right(out_grad[...], w_down)
    gate_low = bf(units_grad * lift * slope)
    up_low = bf(units_grad * gate)
    gate_grad[...] = gate_low
    up_grad[...] = up_low
    total[...] += product_right(gate_low, w_gate) + product_right(up_low, w_up)
    total_out[...] += product(units, w_down)

    @pl.when(j == pl.num_programs(0) - 1)
    def _():
        split_blocks(total, keep, send)
        split_blocks(total_out, out_keep, out_send)


def feed(place, pieces, out_grad, weights):
    low = jnp.bfloat16
    pair = (2, 128, 1024)
    column = pl.BlockSpec((ROWS, 256), lambda j: (0, j))
    return pl.pallas_call(
        feed_kernel,
        grid=(4,),
        in_specs=[scalars()]
        + [whole(a.shape) for a in (*pieces, out_grad)]
        + [pl.BlockSpec(memory_space=pl.ANY)] * 9,
        out_specs=[whole(pair)] * 4 + [whole((ROWS, 1024)), column, column, column],
        out_shape=[jax.ShapeDtypeStruct(pair, low)] * 4
        + [jax.ShapeDtypeStruct((ROWS, 1024), low)] * 4,
        scratch_shapes=[
            pltpu.VMEM((1024, 3072), low),
            pltpu.VMEM((ROWS, 1024), jnp.float32),
            pltpu.VMEM((ROWS, 1024), jnp.float32),
            pltpu.SemaphoreType.DMA((9,)),
        ],
        compiler_params=kernel_params(),
        cost_estimate=cost(14_000_000_000, 12_000_000),
        name="feed",
    )(place, *pieces, out_grad, *weights)


def put_by_target(place, values, out):
    for s in range(8):
        out[place[11 + s], :, : values.shape[1]] = values[s * 128 : (s + 1) * 128, :]


def feed_grads_kernel(place, rows, gate_grad, up_grad, hidden, out_grad, grads, turned):
    j = pl.program_id(0)

    @pl.when(j == 0)
    def _():
        turned[...] = rows[...].T

    @pl.when(j == 4)
    def _():
        turned[...] = hidden[...].T

    columns = pl.ds(pl.multiple_of((j % 2) * 512, 512), 512)
    for first, right in ((0, gate_grad), (2, up_grad), (4, out_grad)):

        @pl.when((j >= first) & (j < first + 2))
        def _():
            put_by_target(place, bf(product(turned[...], right[:, columns])), grads)


def feed_grads(place, rows, gate_grad, up_grad, hidden, out_grad):
    low = jnp.bfloat16
    return pl.pallas_call(
        feed_grads_kernel,
        grid=(6,),
        in_specs=[scalars()] + [whole((ROWS, 1024))] * 5,
        out_specs=pl.BlockSpec((8, 128, 512), lambda j: (0, 0, j)),
        out_shape=jax.ShapeDtypeStruct((8, 128, 3072), low),
        scratch_shapes=[pltpu.VMEM((1024, ROWS), low)],
        compiler_params=kernel_params(),
        cost_estimate=cost(7_000_000_000, 11_000_000),
        name="feed_grads",
    )(place, rows, gate_grad, up_grad, hidden, out_grad)


def attend_grads_kernel(place, rows, qkv_grad, context, middle_grad, grads):
    put_by_target(place, bf(product(rows[...].T, qkv_grad[...])), grads)
    out_grad = bf(product(context[...].T, middle_grad[...]))
    for s in range(8):
        for q in range(4):
            grads[place[11 + s], q * 32 : (q + 1) * 32, 768:] = out_grad[
                s * 32 : (s + 1) * 32, q * 256 : (q + 1) * 256
            ]


def attend_grads(place, rows, qkv_grad, context, middle_grad):
    operands = (rows, qkv_grad, context, middle_grad)
    return pl.pallas_call(
        attend_grads_kernel,
        grid=(1,),
        in_specs=[scalars()] + [whole(a.shape) for a in operands],
        out_specs=whole((8, 128, 1024)),
        out_shape=jax.ShapeDtypeStruct((8, 128, 1024), jnp.bfloat16),
        compiler_params=kernel_params(),
        cost_estimate=cost(4_000_000_000, 6_000_000),
        name="attend_grads",
    )(place, *operands)


def placed_kernel(turned, place, p0, p1, p2, p3, weights, rows, result):
    put_pieces(place, (p0, p1, p2, p3), rows)
    left = rows[:, :1024]
    result[...] = bf(product_right(left, weights[...]) if turned else product(left, weights[...]))


def placed_product(place, pieces, weights, turned):
    width = pieces[0].shape[1]
    low = jnp.bfloat16
    return pl.pallas_call(
        partial(placed_kernel, turned),
        in_specs=[scalars()] + [whole(a.shape) for a in (*pieces, weights)],
        out_specs=[whole((ROWS, width)), whole((ROWS, 256))],
        grid=(1,),
        out_shape=[
            jax.ShapeDtypeStruct((ROWS, width), low),
            jax.ShapeDtypeStruct((ROWS, 256), low),
        ],
        compiler_params=kernel_params(),
        cost_estimate=cost(300_000_000, 3_000_000),
        name="placed_product",
    )(place, *pieces, weights)


PAIR_C = [(i, i ^ 1) for i in range(4)]
PAIR_Y = [(i, i ^ 2) for i in range(4)]


def swap_c(shard):
    return lax.ppermute(shard, "mp", PAIR_C)


def swap_y(shard):
    return lax.ppermute(shard, "mp", PAIR_Y)


def swap_seq(shard, by):
    return lax.ppermute(shard, "seq", [(i, i ^ by) for i in range(8)])


RING = (0, 2, 4, 6, 7, 5, 3, 1)
UP = [(RING[i], RING[(i + 1) % 8]) for i in range(8)]
DOWN = [(b, a) for a, b in UP]
REACH = (0, -1, 1, -2, 2, -3, 3, 4, 4)


def swap_up(shard):
    return lax.ppermute(shard, "seq", UP)


def swap_down(shard):
    return lax.ppermute(shard, "seq", DOWN)


def chosen(index, values):
    places = jnp.arange(len(values), dtype=jnp.int32)
    return jnp.sum(jnp.where(index[..., None] == places, jnp.array(values, jnp.int32), 0), axis=-1)


def places_of(c, y, s):
    at = [RING.index(k) for k in range(8)]
    own = chosen(s, at)
    owners = chosen((own + jnp.array(REACH, jnp.int32) + 8) % 8, RING)
    ahead = (jnp.array(at, jnp.int32) - own + 8) % 8
    return jnp.concatenate([jnp.stack([c, y]), owners, ahead]).astype(jnp.int32)


class RingGather:
    def __init__(self, shard):
        self.pieces = [shard]
        self.flying = [shard, shard]

    def step(self):
        ahead, behind = self.flying
        if len(self.pieces) == 7:
            ahead, behind = (ahead[:64], behind[64:])
        self.flying = [swap_up(ahead), swap_down(behind)]

    def landed(self, value):
        value, self.flying = lax.optimization_barrier((value, self.flying))
        self.pieces = self.pieces + self.flying
        return value


class RingSum:
    def __init__(self, blocks):
        self.blocks = blocks
        self.flying = None
        self.count = 0

    def step(self):
        if self.count == 0:
            far = self.blocks[4]
            sent = [far[:64], far[64:]]
        elif self.count == 1:
            ahead, behind = (self.blocks[3], self.blocks[5])
            sent = [
                jnp.concatenate([bf(up(ahead[:64]) + up(self.flying[0])), ahead[64:]]),
                jnp.concatenate([behind[:64], bf(up(behind[64:]) + up(self.flying[1]))]),
            ]
        else:
            sent = [
                bf(up(self.blocks[k]) + up(part))
                for k, part in zip((4 - self.count, 4 + self.count), self.flying, strict=True)
            ]
        self.flying = [swap_up(sent[0]), swap_down(sent[1])]
        self.count += 1

    def landed(self, value):
        value, self.flying = lax.optimization_barrier((value, self.flying))
        return value

    def result(self):
        return up(self.blocks[0]) + up(self.flying[0]) + up(self.flying[1])


def pick(stacked, index):
    return lax.dynamic_index_in_dim(stacked, index, 0, keepdims=False)


def over_seq(rows):
    return lax.all_to_all(rows, "seq", 0, 0, tiled=True)


def over_all(blocks):
    return lax.all_to_all(blocks, ("seq", "mp"), 0, 0, tiled=True)


def from_all_seq(rows):
    return over_seq(jnp.broadcast_to(rows[None], (8, *rows.shape)))


def sum_rows(send, keep, y):
    total = up(keep) + up(swap_c(send))
    parts = total.reshape(2, 128, -1)
    return pick(parts, y) + up(swap_y(bf(pick(parts, 1 - y))))


def gather_rows(rows):
    far = swap_y(rows)
    return [rows, far, swap_c(rows), swap_c(far)]


def alike(parts):
    return (parts[0] + parts[2]) + (parts[1] + parts[3])


def sum_group(partial, c, y):
    halves = bf(partial).reshape(2, HALF, -1)
    return bf(sum_rows(pick(halves, 1 - c), pick(halves, c), y))


def sum_seq(rows):
    return jnp.sum(up(over_seq(rows.reshape(8, 16, -1))), axis=0)


def gather_bytes(rows):
    far = swap_y(rows)
    return [rows, swap_c(rows), far, swap_c(far)]


def sum_bytes(keep, send):
    got = up(keep) + up(swap_c(send))
    return got[0] + up(swap_y(bf(got[1])))


def placed(parts, m):
    blocks = jnp.stack(parts)
    return jnp.concatenate([pick(blocks, m ^ k) for k in range(4)], axis=0)


def to_bytes(columns):
    got = over_all(columns.reshape(32, 16, 256))
    return got.reshape(8, 4, 16, 256).transpose(2, 1, 0, 3).reshape(128, E)


def to_columns(rows):
    sent = rows.reshape(16, 4, 8, 256).transpose(2, 1, 0, 3).reshape(32, 16, 256)
    return over_all(sent).reshape(ROWS, 256)


def split_plan(
    byte_input,
    seq_lengths,
    cotangent,
    gain_global,
    patch_in,
    mixer_gate,
    mixer_input,
    mixer_state,
    mixer_step,
    conv_input,
    conv_state,
    step_bias,
    decay_log,
    skip_gain,
    gain_mixer,
    mixer_out,
    patch_out,
    gain_attend,
    attend_query,
    attend_key,
    attend_value,
    attend_out,
    gain_feed,
    feed_gate,
    feed_up,
    feed_down,
):
    s, m = (lax.axis_index("seq"), lax.axis_index("mp"))
    y, c = (m // 2, m % 2)
    place = places_of(c, y, s)
    f32 = jnp.float32

    out_halves = mixer_out.reshape(64, 2, 512).transpose(1, 0, 2).reshape(128, 512)
    w_mixer = RingGather(jnp.concatenate(
        [
            mixer_gate,
            mixer_input,
            mixer_state,
            mixer_step,
            jnp.zeros((128, 120), jnp.bfloat16),
            out_halves,
        ],
        axis=1,
    ))
    w_mixer.step()
    out_quarters = attend_out.reshape(32, 4, 256).transpose(1, 0, 2).reshape(128, 256)
    w_attend = RingGather(
        jnp.concatenate([attend_query, attend_key, attend_value, out_quarters], axis=1)
    )
    w_feed = RingGather(jnp.concatenate([feed_gate, feed_up, feed_down], axis=1))
    table = jnp.concatenate([conv_input, gain_mixer[None], jnp.zeros((3, 512), f32)], axis=0)
    state_taps = jnp.concatenate([conv_state, jnp.zeros((4, 256), f32)], axis=0)
    params = jnp.pad(jnp.stack([step_bias, decay_log, skip_gain]), ((0, 5), (0, 120)))

    own_slots = lax.dynamic_slice_in_dim(byte_input.reshape(64, PATCH, E), 2 * m, 2, 1)
    columns_in = over_seq(own_slots.reshape(64, 8, 256).transpose(1, 0, 2)).reshape(ROWS, 256)
    columns_in = w_mixer.landed(columns_in)
    w_mixer.step()
    rows = sum_group(product(columns_in, patch_in), c, y)
    hidden = w_mixer.landed(bf(sum_seq(rows)))
    w_mixer.step()
    hidden = w_mixer.landed(from_all_seq(hidden).reshape(128, 1024))
    w_mixer.step()
    hidden = up(hidden)
    normed_parts = w_mixer.landed(gather_rows(bf(rms_scale(hidden, gain_global))))

    w_attend.step()
    w_feed.step()
    send, keep, normed, pre, inside, scaled = mixer_forward(
        place, seq_lengths, normed_parts, w_mixer.pieces, table, state_taps, params
    )
    w_patch = over_seq(patch_out.reshape(128, 8, 256).transpose(1, 0, 2))
    send, w_patch = w_attend.landed((send, w_patch))
    w_attend.step()
    w_patch = w_patch.reshape(1024, 256)
    sums = w_attend.landed(w_feed.landed(sum_rows(send, keep, y)))
    w_attend.step()
    w_feed.step()
    unscaled, root = (sums[:, :1024], lax.rsqrt(sums[:, 1024:1025] / DI + EPS))
    merged_parts = w_attend.landed(gather_rows(bf(hidden + root * unscaled)))
    w_attend.step()
    merged_low, slots = placed_product(place, merged_parts, w_patch, False)
    slots = w_attend.landed(w_feed.landed(to_bytes(slots)))
    w_feed.step()
    residual = up(lax.dynamic_slice_in_dim(byte_input, m * 128, 128, 0)) + slots

    attend_parts = gather_bytes(bf(rms_scale(residual, gain_attend)))
    keep, send, attend_in, qkv, context = attend_forward(place, attend_parts, w_attend.pieces)
    send = w_feed.landed(send)
    w_feed.step()
    middle = residual + sum_bytes(keep, send)
    feed_parts = w_feed.landed(gather_bytes(bf(rms_scale(middle, gain_feed))))
    cot_blocks = cotangent.reshape(4, 128, E)
    cot_rows = pick(cot_blocks, m)
    out_low = jnp.concatenate([bf(pick(cot_blocks, m ^ k)) for k in range(4)], axis=0)
    keep, send, out_keep, out_send, feed_in, hidden_units, grad_gate, grad_up = feed(
        place, feed_parts, out_low, w_feed.pieces
    )
    feed_sums = feed_grads(place, feed_in, grad_gate, grad_up, hidden_units, out_low)
    grad_middle_part, gain_feed_part = rms_back(middle, gain_feed, sum_bytes(keep, send))
    grad_middle = cot_rows + grad_middle_part
    middle_parts, feed_sums = lax.optimization_barrier((gather_bytes(bf(grad_middle)), feed_sums))
    feed_sums = RingSum(feed_sums)
    feed_sums.step()
    keep, send, middle_low, grad_qkv = attend_backward(place, middle_parts, qkv, w_attend.pieces)
    send = feed_sums.landed(send)
    feed_sums.step()
    attend_sums = attend_grads(place, attend_in, grad_qkv, context, middle_low)
    grad_attend_in, attend_sums = lax.optimization_barrier((sum_bytes(keep, send), attend_sums))
    attend_sums = RingSum(attend_sums)
    grad_attend_in = feed_sums.landed(grad_attend_in)
    feed_sums.step()
    grad_residual_part, gain_attend_part = rms_back(residual, gain_attend, grad_attend_in)
    grad_residual = grad_middle + grad_residual_part

    slot_grad, out_send = lax.optimization_barrier(
        (to_columns(bf(grad_residual)), swap_c(out_send))
    )
    slot_grad = feed_sums.landed(slot_grad)
    feed_sums.step()
    grad_patch_out = bf(product_left(merged_low, slot_grad)).reshape(8, 128, 256)
    rows = sum_group(product_right(slot_grad, w_patch), c, y)
    out_parts = up(out_keep) + up(out_send)
    rows, out_far = lax.optimization_barrier((rows, bf(out_parts[1])))
    merged_rows, out_far = lax.optimization_barrier((sum_seq(rows), swap_y(out_far)))
    out_rows = bf(middle + out_parts[0] + up(out_far))
    merged_rows = feed_sums.landed(merged_rows)
    attend_sums.step()
    gains = jnp.stack([gain_feed_part, gain_attend_part])
    got = from_all_seq(
        bf(jnp.concatenate([merged_rows, gains, jnp.zeros((6, 1024), f32)], axis=0))
    )
    got, out_far, out_near = lax.optimization_barrier((got, swap_y(out_rows), swap_c(out_rows)))
    got = attend_sums.landed(got)
    attend_sums.step()
    grad_merged = up(got[:, :16].reshape(128, 1024))
    gains = jnp.sum(up(got[:, 16:18]), axis=0)
    kappa = jnp.sum(grad_merged * unscaled, axis=1, keepdims=True) * root**3 / DI
    rows = jnp.concatenate([grad_merged * root, jnp.broadcast_to(kappa, (128, 128))], axis=1)
    merged_parts = gather_rows(
        bf(jnp.concatenate([rows, jnp.pad(gains, ((0, 6), (0, 128)))], axis=0))
    )
    merged_parts = attend_sums.landed(merged_parts)
    attend_sums.step()
    out_both = swap_c(out_far)
    grad_patch_out = over_seq(grad_patch_out)
    gains = alike([up(part[128:130, :1024]) for part in merged_parts])
    send, keep, grads, merged_grad, table_grad, state_taps_grad, params_grad = mixer_backward(
        place,
        seq_lengths,
        merged_parts,
        w_mixer.pieces,
        table,
        state_taps,
        params,
        pre,
        inside,
    )
    send, grad_patch_out, out_both = attend_sums.landed((send, grad_patch_out, out_both))
    attend_sums.step()
    byte_output = placed([out_rows, out_near, out_far, out_both], m)
    sums = attend_sums.landed(sum_rows(send, keep, y))
    feed_sums, attend_sums = (feed_sums.result(), attend_sums.result())
    grad_hidden_part, gain_global_part = rms_back(hidden, gain_global, sums[:, :1024])
    rows = jnp.concatenate([grad_merged + grad_hidden_part, sums[:, 1024:]], axis=1)
    small = jnp.stack([gain_global_part, state_taps_grad[:4].reshape(1024)])
    hidden_parts = gather_rows(
        bf(jnp.concatenate([rows, jnp.pad(small, ((0, 6), (0, 256)))], axis=0))
    )
    small = alike([up(part[128:130, :1024]) for part in hidden_parts])
    hidden_rows, back = placed_product(place, hidden_parts, patch_in, True)
    grad_input = placed(gather_bytes(bf(grad_residual + to_bytes(back))), m)

    hidden_grad = hidden_rows[:, :1024]
    normed_columns = lax.dynamic_slice_in_dim(normed, s * 128, 128, 1)
    first_grad = product_left(normed_columns, grads)
    own_scaled = lax.dynamic_slice_in_dim(scaled, s * HDIM, HDIM, 1)
    return (
        byte_output,
        grad_input,
        small[0],
        product_left(columns_in, hidden_grad),
        first_grad[:, :512],
        first_grad[:, 512:1024],
        product_left(normed_columns, hidden_rows[:, 1024:]),
        first_grad[:, 1280:1288],
        table_grad[:4],
        small[1].reshape(4, 256),
        params_grad[0, :8],
        params_grad[1, :8],
        params_grad[2, :8],
        table_grad[4],
        product_left(own_scaled, merged_grad),
        grad_patch_out.transpose(1, 0, 2).reshape(128, 2048).astype(f32),
        gains[1],
        attend_sums[:, :256],
        attend_sums[:, 256:512],
        attend_sums[:, 512:768],
        attend_sums[:, 768:].reshape(4, 32, 256).transpose(1, 0, 2).reshape(32, 1024),
        gains[0],
        feed_sums[:, :1024],
        feed_sums[:, 1024:2048],
        feed_sums[:, 2048:],
    )


def solution(mesh):
    in_specs = (
        P("seq", None),
        P(),
        P("seq", None),
        P(),
        P(("mp", "seq"), None),
        P("seq", "mp"),
        P("seq", "mp"),
        P("seq", None),
        P("seq", "mp"),
        P(None, "mp"),
        P(),
        P("mp"),
        P("mp"),
        P("mp"),
        P("mp"),
        P(("mp", "seq"), None),
        P("seq", "mp"),
        P(),
        P("seq", "mp"),
        P("seq", "mp"),
        P("seq", "mp"),
        P(("mp", "seq"), None),
        P(),
        P("seq", "mp"),
        P("seq", "mp"),
        P(("mp", "seq"), None),
    )
    out_specs = (
        P("seq", None),
        P("seq", None),
        P(),
        P(("mp", "seq"), None),
        P("seq", "mp"),
        P("seq", "mp"),
        P("seq", None),
        P("seq", "mp"),
        P(None, "mp"),
        P(),
        P("mp"),
        P("mp"),
        P("mp"),
        P("mp"),
        P(("mp", "seq"), None),
        P("seq", "mp"),
        P(),
        P("seq", "mp"),
        P("seq", "mp"),
        P("seq", "mp"),
        P(("mp", "seq"), None),
        P(),
        P("seq", "mp"),
        P("seq", "mp"),
        P(("mp", "seq"), None),
    )
    plan = split_plan if (mesh.shape["seq"], mesh.shape["mp"]) == (8, 4) else gathered_plan
    return jax.shard_map(plan, mesh=mesh, in_specs=in_specs, out_specs=out_specs, check_vma=False)
```

```python
from functools import partial

import jax
import jax.numpy as jnp
from jax import lax
from jax.experimental import pallas as pl
from jax.experimental.pallas import tpu as pltpu
from jax.sharding import PartitionSpec as P

E = 1024
HDIM = 64
DI = 2048
NSTATE = 128
KCONV = 4
PATCH = 8
TOK_DEV = 512
BLOCK = 64


EPS = 1e-05
HIGH = lax.Precision.HIGHEST


def shifted(shard, axis, by):
    length = lax.axis_size(axis)
    pairs = [(i, i + by) for i in range(length) if 0 <= i + by < length]
    return lax.ppermute(shard, axis, pairs)


def prefix(shard, axis, combine, identity):
    length, position = (lax.axis_size(axis), lax.axis_index(axis))
    everything = jax.tree.map(
        lambda part, kind: lax.all_gather(part.astype(kind), axis),
        shard,
        (jnp.bfloat16, jnp.bfloat16),
    )
    start = jax.tree.map(
        lambda part, zero: jnp.broadcast_to(jnp.asarray(zero, part.dtype), part.shape),
        shard,
        identity,
    )

    def prefix_turn(k, before):
        reached = k < position
        new = combine(
            before, jax.tree.map(lambda part, own: part[k].astype(own.dtype), everything, shard)
        )
        return jax.tree.map(lambda a, b: jnp.where(reached, a, b), new, before)

    return lax.fori_loop(0, length, prefix_turn, start)


def carried_in(shard, axis, combine, identity):
    length, position = (lax.axis_size(axis), lax.axis_index(axis))
    everything = jax.tree.map(
        lambda part, kind: lax.all_gather(part.astype(kind), axis),
        shard,
        jax.tree.map(lambda a: jnp.bfloat16 if a.dtype == jnp.float32 else a.dtype, shard),
    )
    start = jax.tree.map(
        lambda part, zero: jnp.broadcast_to(jnp.asarray(zero, part.dtype), part.shape),
        shard,
        identity,
    )

    def carried_turn(k, before):
        at = length - 1 - k
        reached = at > position
        new = combine(
            before, jax.tree.map(lambda part, own: part[at].astype(own.dtype), everything, shard)
        )
        return jax.tree.map(lambda a, b: jnp.where(reached, a, b), new, before)

    return lax.fori_loop(0, length, carried_turn, start)


def product(former, latter):
    return jnp.dot(former, latter, preferred_element_type=jnp.float32)


def product_left(former, latter):
    return lax.dot_general(
        former, latter, (((0,), (0,)), ((), ())), preferred_element_type=jnp.float32
    )


def product_right(former, latter):
    return lax.dot_general(
        former, latter, (((1,), (1,)), ((), ())), preferred_element_type=jnp.float32
    )


def over_heads(partial_sum):
    return lax.psum(partial_sum, "mp")


def gather_slots(pieces):
    return lax.all_gather(pieces.astype(jnp.bfloat16), "mp", axis=1, tiled=True).astype(
        pieces.dtype
    )


def rms_scale(values, scale_gain):
    mean_square = jnp.mean(values * values, axis=-1, keepdims=True)
    return values * lax.rsqrt(mean_square + EPS) * scale_gain


def rms_back(values, scale_gain, upstream):
    pullback = jax.vjp(rms_scale, values, scale_gain)[1]
    return pullback(upstream)


def running_bounds(lengths):
    places = jnp.arange(lengths.shape[0])
    upto = places[None, :] <= places[:-1, None]
    return jnp.sum(jnp.where(upto, lengths[None, :], 0), axis=1)


def running_sum(values):
    places = jnp.arange(values.shape[0])
    lower_part = (places[:, None] >= places[None, :]).astype(jnp.float32)
    return jnp.dot(lower_part, values, precision=HIGH, preferred_element_type=jnp.float32)


def segment_of(lengths, start_row, row_count):
    bounds = running_bounds(lengths)
    places = start_row + jnp.arange(row_count, dtype=jnp.int32)
    return jnp.sum((places[:, None] >= bounds[None, :]).astype(jnp.int32), axis=1)


def conv_silu(extended, kernel, segment_rows):
    row_count = extended.shape[0] - KCONV + 1
    segment_now = segment_rows[KCONV - 1 :]
    summed = jnp.zeros((row_count, extended.shape[1]), jnp.float32)
    for offset in range(KCONV):
        same_seq = (segment_rows[offset : offset + row_count] == segment_now)[:, None]
        summed = (
            summed
            + jnp.where(same_seq, extended[offset : offset + row_count], 0.0) * kernel[offset]
        )
    return jax.nn.silu(summed)


def block_output(
    head_values,
    write_vecs,
    read_vecs,
    step_size,
    log_rate,
    skip_term,
    state_value,
    segment_rows,
    segment_prev,
):
    length = head_values.shape[0]
    running = running_sum(-step_size * jnp.exp(log_rate))
    places = jnp.arange(length)
    allowed = (places[:, None] >= places[None, :]) & (
        segment_rows[:, None] == segment_rows[None, :]
    )
    allowed = allowed[:, :, None]
    spread = jnp.where(allowed, running[:, None, :] - running[None, :, :], 0.0)
    factors = jnp.where(allowed, jnp.exp(spread), 0.0)
    affinity = jnp.dot(read_vecs, write_vecs.T, precision=HIGH, preferred_element_type=jnp.float32)
    mixing = factors * affinity[:, :, None] * step_size[None, :, :]
    inside = jnp.einsum("tsh,shp->thp", mixing, head_values, precision=HIGH)
    carried = jnp.where((segment_rows == segment_prev)[:, None], jnp.exp(running), 0.0)
    reading = (
        jnp.einsum("tn,hpn->thp", read_vecs, state_value, precision=HIGH) * carried[:, :, None]
    )
    result = inside + reading + skip_term[None, :, None] * head_values
    return result.reshape(length, -1)


def block_summary(head_values, write_vecs, step_size, log_rate, segment_rows, segment_prev):
    running = running_sum(-step_size * jnp.exp(log_rate))
    latest = running[-1]
    in_tail = (segment_rows == segment_rows[-1])[:, None]
    weights = jnp.where(in_tail, jnp.exp(latest[None, :] - running), 0.0) * step_size
    scaled = weights[:, :, None] * head_values
    state_local = jnp.einsum("shp,sn->hpn", scaled, write_vecs, precision=HIGH)
    decay_total = jnp.where(segment_rows[-1] == segment_prev, jnp.exp(latest), 0.0)
    return (decay_total, state_local)


def combine_state(earlier, later):
    return (earlier[0] * later[0], later[0][:, None, None] * earlier[1] + later[1])


def patch_attention(queries, keys_all, values_all):
    row_count = queries.shape[0]
    head_count = queries.shape[1] // HDIM
    query_rows = queries.reshape(row_count // PATCH, PATCH, head_count, HDIM)
    key_rows = keys_all.reshape(row_count // PATCH, PATCH, head_count, HDIM)
    value_rows = values_all.reshape(row_count // PATCH, PATCH, head_count, HDIM)
    scores = jnp.einsum("bihd,bjhd->bhij", query_rows, key_rows, precision=HIGH) * HDIM ** (-0.5)
    causal = jnp.arange(PATCH)[:, None] >= jnp.arange(PATCH)[None, :]
    scores = jnp.where(causal, scores, -1e30)
    peak = jnp.max(scores, axis=-1, keepdims=True)
    probs = jnp.exp(scores - peak)
    probs = probs / jnp.sum(probs, axis=-1, keepdims=True)
    context = jnp.einsum("bhij,bjhd->bihd", probs, value_rows, precision=HIGH)
    return context.reshape(row_count, head_count * HDIM)


def add_tail(main_rows, tail_rows):
    keep_count = main_rows.shape[0] - tail_rows.shape[0]
    return jnp.concatenate([main_rows[:keep_count], main_rows[keep_count:] + tail_rows], axis=0)


def gathered_plan(
    byte_input,
    seq_lengths,
    cotangent,
    gain_global,
    patch_in,
    mixer_gate,
    mixer_input,
    mixer_state,
    mixer_step,
    conv_input,
    conv_state,
    step_bias,
    decay_log,
    skip_gain,
    gain_mixer,
    mixer_out,
    patch_out,
    gain_attend,
    attend_query,
    attend_key,
    attend_value,
    attend_out,
    gain_feed,
    feed_gate,
    feed_up,
    feed_down,
):
    group_size = lax.axis_size("mp")
    slot_width = PATCH * E // group_size
    slot_start = lax.axis_index("mp") * slot_width
    first_row = lax.axis_index("seq") * BLOCK
    segment_ext = segment_of(seq_lengths, first_row - (KCONV - 1), BLOCK + KCONV - 1)
    segment_rows = segment_ext[KCONV - 1 :]
    segment_prev = segment_of(seq_lengths, first_row - 1, 1)[0]

    def fetch_global():
        return (
            lax.all_gather(patch_in, "seq", axis=0, tiled=True),
            lax.all_gather(mixer_gate, "seq", axis=0, tiled=True),
            lax.all_gather(mixer_input, "seq", axis=0, tiled=True),
            lax.all_gather(mixer_state, "seq", axis=0, tiled=True),
            lax.all_gather(mixer_step, "seq", axis=0, tiled=True),
            lax.all_gather(mixer_out, "seq", axis=0, tiled=True),
            lax.all_gather(patch_out, "seq", axis=0, tiled=True),
        )

    def fetch_local():
        return (
            lax.all_gather(attend_query, "seq", axis=0, tiled=True),
            lax.all_gather(attend_key, "seq", axis=0, tiled=True),
            lax.all_gather(attend_value, "seq", axis=0, tiled=True),
            lax.all_gather(attend_out, "seq", axis=0, tiled=True),
            lax.all_gather(feed_gate, "seq", axis=0, tiled=True),
            lax.all_gather(feed_up, "seq", axis=0, tiled=True),
            lax.all_gather(feed_down, "seq", axis=0, tiled=True),
        )

    def conv_of(extended, kernel):
        return conv_silu(extended, kernel, segment_ext)

    def summary_of(values_in, writes_in, steps_in, rates_in):
        return block_summary(values_in, writes_in, steps_in, rates_in, segment_rows, segment_prev)

    def output_of(values_in, writes_in, reads_in, steps_in, rates_in, skips_in, state_value):
        return block_output(
            values_in,
            writes_in,
            reads_in,
            steps_in,
            rates_in,
            skips_in,
            state_value,
            segment_rows,
            segment_prev,
        )

    full_patch_in, full_gate, full_input, full_state, full_step, full_mixout, full_patchout = (
        fetch_global()
    )
    patches = byte_input.reshape(BLOCK, PATCH * E)
    local_bytes = lax.dynamic_slice_in_dim(patches, slot_start, slot_width, 1)
    hidden = over_heads(product(local_bytes, full_patch_in))
    normed = rms_scale(hidden, gain_global).astype(jnp.bfloat16)
    gate_pre = product(normed, full_gate)
    input_pre = product(normed, full_input)
    state_pre = product(normed, full_state)
    step_pre = product(normed, full_step)
    rim_rows = shifted((input_pre[BLOCK - KCONV + 1 :], state_pre[BLOCK - KCONV + 1 :]), "seq", 1)
    input_ext = jnp.concatenate([rim_rows[0], input_pre], axis=0)
    state_ext = jnp.concatenate([rim_rows[1], state_pre], axis=0)
    input_conv = conv_of(input_ext, conv_input)
    state_conv = conv_of(state_ext, conv_state)
    step_size = jax.nn.softplus(step_pre + step_bias)
    head_count = step_size.shape[1]
    head_values = input_conv.reshape(BLOCK, head_count, HDIM)
    write_vecs = state_conv[:, :NSTATE]
    read_vecs = state_conv[:, NSTATE:]
    decay_total, state_local = summary_of(head_values, write_vecs, step_size, decay_log)
    identity = (jnp.ones_like(decay_total), jnp.zeros_like(state_local))
    state_in = prefix((decay_total, state_local), "seq", combine_state, identity)[1]
    mixer_rows = output_of(
        head_values, write_vecs, read_vecs, step_size, decay_log, skip_gain, state_in
    )
    gate_sigm = jax.nn.sigmoid(gate_pre)
    gate_silu = gate_pre * gate_sigm
    gated = mixer_rows * gate_silu
    mean_square = over_heads(jnp.sum(gated * gated, axis=-1, keepdims=True)) / DI
    root_inverse = lax.rsqrt(mean_square + EPS)
    mixed = (gated * root_inverse * gain_mixer).astype(jnp.bfloat16)
    merged = hidden + over_heads(product(mixed, full_mixout))
    merged_low = merged.astype(jnp.bfloat16)
    slot_values = gather_slots(product(merged_low, full_patchout)).reshape(TOK_DEV, E)
    residual = byte_input.astype(jnp.float32) + slot_values
    full_query, full_key, full_value, full_attout, full_feedgate, full_up, full_down = fetch_local()
    attend_in = rms_scale(residual, gain_attend).astype(jnp.bfloat16)
    queries = product(attend_in, full_query)
    keys_all = product(attend_in, full_key)
    values_all = product(attend_in, full_value)
    context = patch_attention(queries, keys_all, values_all).astype(jnp.bfloat16)
    middle = residual + over_heads(product(context, full_attout))
    feed_in = rms_scale(middle, gain_feed).astype(jnp.bfloat16)
    gate_value = product(feed_in, full_feedgate)
    up_value = product(feed_in, full_up)
    gate_sig = jax.nn.sigmoid(gate_value)
    hidden_units = (gate_value * gate_sig * up_value).astype(jnp.bfloat16)
    byte_output = middle + over_heads(product(hidden_units, full_down))
    full_query, full_key, full_value, full_attout, full_feedgate, full_up, full_down = fetch_local()
    out_low = cotangent.astype(jnp.bfloat16)
    grad_feed_down = product_left(hidden_units, out_low)
    grad_units = product_right(out_low, full_down)
    grad_gate_value = (
        grad_units * up_value * gate_sig * (1.0 + gate_value * (1.0 - gate_sig))
    ).astype(jnp.bfloat16)
    grad_up_value = (grad_units * gate_value * gate_sig).astype(jnp.bfloat16)
    grad_feed_gate = product_left(feed_in, grad_gate_value)
    grad_feed_up = product_left(feed_in, grad_up_value)
    grad_feed_in = over_heads(
        product_right(grad_gate_value, full_feedgate) + product_right(grad_up_value, full_up)
    )
    grad_middle_part, grad_gain_feed = rms_back(middle, gain_feed, grad_feed_in)
    grad_middle = cotangent + grad_middle_part
    middle_low = grad_middle.astype(jnp.bfloat16)
    grad_attend_out = product_left(context, middle_low)
    grad_context = product_right(middle_low, full_attout)
    attention_pull = jax.vjp(patch_attention, queries, keys_all, values_all)[1]
    grad_query_raw, grad_key_raw, grad_value_raw = attention_pull(grad_context)
    grad_query_rows = grad_query_raw.astype(jnp.bfloat16)
    grad_key_rows = grad_key_raw.astype(jnp.bfloat16)
    grad_value_rows = grad_value_raw.astype(jnp.bfloat16)
    grad_attend_query = product_left(attend_in, grad_query_rows)
    grad_attend_key = product_left(attend_in, grad_key_rows)
    grad_attend_value = product_left(attend_in, grad_value_rows)
    grad_attend_in = over_heads(
        product_right(grad_query_rows, full_query)
        + product_right(grad_key_rows, full_key)
        + product_right(grad_value_rows, full_value)
    )
    grad_residual_part, grad_gain_attend = rms_back(residual, gain_attend, grad_attend_in)
    grad_residual = grad_middle + grad_residual_part
    local_sums = (
        lax.psum_scatter(grad_attend_query, "seq", scatter_dimension=0, tiled=True),
        lax.psum_scatter(grad_attend_key, "seq", scatter_dimension=0, tiled=True),
        lax.psum_scatter(grad_attend_value, "seq", scatter_dimension=0, tiled=True),
        lax.psum_scatter(grad_attend_out, "seq", scatter_dimension=0, tiled=True),
        lax.psum_scatter(grad_feed_gate, "seq", scatter_dimension=0, tiled=True),
        lax.psum_scatter(grad_feed_up, "seq", scatter_dimension=0, tiled=True),
        lax.psum_scatter(grad_feed_down, "seq", scatter_dimension=0, tiled=True),
    )
    full_patch_in, full_gate, full_input, full_state, full_step, full_mixout, full_patchout = (
        fetch_global()
    )
    residual_patches = grad_residual.reshape(BLOCK, PATCH * E)
    slot_grad = lax.dynamic_slice_in_dim(residual_patches, slot_start, slot_width, 1).astype(
        jnp.bfloat16
    )
    grad_patch_out = product_left(merged_low, slot_grad)
    grad_merged = over_heads(product_right(slot_grad, full_patchout))
    merged_grad_low = grad_merged.astype(jnp.bfloat16)
    grad_mixer_out = product_left(mixed, merged_grad_low)
    grad_mixed = product_right(merged_grad_low, full_mixout)
    grad_gain_mixer = jnp.sum(grad_mixed * gated * root_inverse, axis=0)
    scaled_grad = grad_mixed * gain_mixer
    inner_dot = over_heads(jnp.sum(scaled_grad * gated, axis=-1, keepdims=True))
    grad_gated = scaled_grad * root_inverse - gated * inner_dot * root_inverse**3 / DI
    grad_mixer_rows = grad_gated * gate_silu
    grad_gate_pre = grad_gated * mixer_rows * gate_sigm * (1.0 + gate_pre * (1.0 - gate_sigm))
    output_pull = jax.vjp(
        output_of, head_values, write_vecs, read_vecs, step_size, decay_log, skip_gain, state_in
    )[1]
    (
        grad_values_a,
        grad_writes_a,
        grad_reads,
        grad_steps_a,
        grad_rates_a,
        grad_skip_gain,
        grad_state_in,
    ) = output_pull(grad_mixer_rows)
    state_end = carried_in((decay_total, grad_state_in), "seq", combine_state, identity)[1]
    summary_pull = jax.vjp(summary_of, head_values, write_vecs, step_size, decay_log)[1]
    grad_values_b, grad_writes_b, grad_steps_b, grad_rates_b = summary_pull(
        (jnp.sum(state_end * state_in, axis=(1, 2)), state_end)
    )
    grad_input_conv = (grad_values_a + grad_values_b).reshape(BLOCK, -1)
    grad_state_conv = over_heads(
        jnp.concatenate([grad_writes_a + grad_writes_b, grad_reads], axis=1)
    )
    grad_step_pre = (grad_steps_a + grad_steps_b) * jax.nn.sigmoid(step_pre + step_bias)
    grad_step_bias = jnp.sum(grad_step_pre, axis=0)
    grad_decay_log = grad_rates_a + grad_rates_b
    grad_input_ext, grad_conv_input = jax.vjp(conv_of, input_ext, conv_input)[1](grad_input_conv)
    grad_state_ext, grad_conv_state = jax.vjp(conv_of, state_ext, conv_state)[1](grad_state_conv)
    rim_back = shifted((grad_input_ext[: KCONV - 1], grad_state_ext[: KCONV - 1]), "seq", -1)
    grad_input_low = add_tail(grad_input_ext[KCONV - 1 :], rim_back[0]).astype(jnp.bfloat16)
    grad_state_low = add_tail(grad_state_ext[KCONV - 1 :], rim_back[1]).astype(jnp.bfloat16)
    grad_gate_low = grad_gate_pre.astype(jnp.bfloat16)
    grad_step_low = grad_step_pre.astype(jnp.bfloat16)
    grad_mixer_gate = product_left(normed, grad_gate_low)
    grad_mixer_input = product_left(normed, grad_input_low)
    grad_mixer_state = product_left(normed, grad_state_low)
    grad_mixer_step = product_left(normed, grad_step_low)
    head_part = over_heads(
        product_right(grad_gate_low, full_gate)
        + product_right(grad_input_low, full_input)
        + product_right(grad_step_low, full_step)
    )
    grad_normed = head_part + product_right(grad_state_low, full_state)
    grad_hidden_part, grad_gain_global = rms_back(hidden, gain_global, grad_normed)
    hidden_grad_low = (grad_merged + grad_hidden_part).astype(jnp.bfloat16)
    grad_patch_in = product_left(local_bytes, hidden_grad_low)
    grad_byte_part = gather_slots(product_right(hidden_grad_low, full_patch_in)).reshape(TOK_DEV, E)
    grad_input = (grad_residual + grad_byte_part).astype(jnp.bfloat16)
    global_sums = (
        lax.psum_scatter(grad_patch_in, "seq", scatter_dimension=0, tiled=True),
        lax.psum_scatter(grad_mixer_gate, "seq", scatter_dimension=0, tiled=True),
        lax.psum_scatter(grad_mixer_input, "seq", scatter_dimension=0, tiled=True),
        lax.psum_scatter(grad_mixer_state, "seq", scatter_dimension=0, tiled=True),
        lax.psum_scatter(grad_mixer_step, "seq", scatter_dimension=0, tiled=True),
        lax.psum_scatter(grad_mixer_out, "seq", scatter_dimension=0, tiled=True),
        lax.psum_scatter(grad_patch_out, "seq", scatter_dimension=0, tiled=True),
    )
    small_sums = lax.psum(
        (
            grad_gain_global,
            grad_conv_input,
            grad_conv_state,
            grad_step_bias,
            grad_decay_log,
            grad_skip_gain,
            grad_gain_mixer,
            grad_gain_attend,
            grad_gain_feed,
        ),
        "seq",
    )
    return (
        byte_output.astype(jnp.bfloat16),
        grad_input,
        small_sums[0],
        global_sums[0],
        global_sums[1],
        global_sums[2],
        global_sums[3],
        global_sums[4],
        small_sums[1],
        small_sums[2],
        small_sums[3],
        small_sums[4],
        small_sums[5],
        small_sums[6],
        global_sums[5],
        global_sums[6],
        small_sums[7],
        local_sums[0],
        local_sums[1],
        local_sums[2],
        local_sums[3],
        small_sums[8],
        local_sums[4],
        local_sums[5],
        local_sums[6],
    )


ROWS = 512
HALF = 256
VMEM_BYTES = 56 * 1024 * 1024


def bf(values):
    return values.astype(jnp.bfloat16)


def up(values):
    return values.astype(jnp.float32)


def whole(shape):
    return pl.BlockSpec(shape, lambda *_: (0,) * len(shape))


def scalars():
    return pl.BlockSpec(memory_space=pltpu.SMEM)


def kernel_params(limit=VMEM_BYTES):
    return pltpu.CompilerParams(vmem_limit_bytes=limit, dimension_semantics=("arbitrary",))


def cost(flops, size):
    return pl.CostEstimate(flops=flops, bytes_accessed=size, transcendentals=0)


def block_index(place, k):
    c, y = (place[0], place[1])
    c = 1 - c if k >= 2 else c
    y = 1 - y if k % 2 else y
    return c * 2 + y


def put_pieces(place, pieces, out_ref, rows=128):
    for k, piece in enumerate(pieces):
        at = pl.multiple_of(block_index(place, k) * rows, rows)
        out_ref[pl.ds(at, rows), :] = piece[:rows, :]


def lane_of(values, lane):
    lanes = lax.broadcasted_iota(jnp.int32, values.shape, 1)
    return jnp.sum(jnp.where(lanes == lane, values, 0.0), axis=1, keepdims=True)


def segments(lengths, shift, shape, axis):
    rows = lax.broadcasted_iota(jnp.int32, shape, axis) - shift
    total = jnp.zeros(shape, jnp.int32)
    bound = 0
    for k in range(lengths.shape[0] - 1):
        bound = bound + lengths[k]
        total = total + (rows >= bound).astype(jnp.int32)
    return total


def tap_masks(lengths):
    here = segments(lengths, 0, (ROWS, 1), 0)
    rows = lax.broadcasted_iota(jnp.int32, (ROWS, 1), 0)
    return [
        up((rows >= j) & (segments(lengths, j, (ROWS, 1), 0) == here))
        for j in range(1, KCONV)
    ]


def conv_rows(values, taps, masks):
    total = values * taps[KCONV - 1 : KCONV, :]
    for j in range(1, KCONV):
        earlier = pltpu.roll(values, j, 0) * masks[j - 1]
        total = total + earlier * taps[KCONV - 1 - j : KCONV - j, :]
    return total


def conv_back(values, taps, masks, grads):
    rows_grad = grads * taps[KCONV - 1 : KCONV, :]
    taps_grad = [None] * KCONV
    taps_grad[KCONV - 1] = jnp.sum(grads * values, axis=0, keepdims=True)
    for j in range(1, KCONV):
        masked = grads * masks[j - 1]
        rows_grad = rows_grad + pltpu.roll(masked, ROWS - j, 0) * taps[
            KCONV - 1 - j : KCONV - j, :
        ]
        taps_grad[KCONV - 1 - j] = jnp.sum(
            masked * pltpu.roll(values, j, 0), axis=0, keepdims=True
        )
    return rows_grad, taps_grad


def silu_parts(values):
    gate = 1.0 / (1.0 + jnp.exp(-values))
    return values * gate, gate * (1.0 + values * (1.0 - gate))


def softplus(values):
    return jnp.maximum(values, 0.0) + jnp.log1p(jnp.exp(-jnp.abs(values)))


def lower(shape, flip=False):
    rows = lax.broadcasted_iota(jnp.int32, shape, 0)
    columns = lax.broadcasted_iota(jnp.int32, shape, 1)
    return up(rows <= columns) if flip else up(rows >= columns)


def allowed_pairs(lengths):
    rows = lax.broadcasted_iota(jnp.int32, (ROWS, ROWS), 0)
    columns = lax.broadcasted_iota(jnp.int32, (ROWS, ROWS), 1)
    same = segments(lengths, 0, (ROWS, 1), 0) == segments(lengths, 0, (1, ROWS), 1)
    return (rows >= columns) & same


def decay_block(run, run_row):
    return jnp.exp(jnp.minimum(run - run_row, 0.0))


def head_columns(j, i, table):
    return lane_of(table, 2 * j + i)


def by_head(first, second):
    lanes = lax.broadcasted_iota(jnp.int32, (1, 2 * HDIM), 1)
    return jnp.where(lanes < HDIM, first, second)


def shared_setup(
    j, lengths, pre_ref, state_taps, params, affinity, step_ref, run_ref, run_t, wr_ref, mask_ref
):
    @pl.when(j == 0)
    def _():
        step = softplus(pre_ref[:, 256:] + params[0:1, :])
        step_ref[...] = step
        running = jnp.dot(
            lower((ROWS, ROWS)), -step * jnp.exp(params[1:2, :]), precision=HIGH,
            preferred_element_type=jnp.float32,
        )
        run_ref[...] = running
        run_t[...] = running.T
        masks = [jnp.broadcast_to(mask, (ROWS, 128)) for mask in tap_masks(lengths)]
        for k in range(KCONV - 1):
            mask_ref[k] = masks[k]
        masks = [jnp.concatenate([mask, mask], axis=1) for mask in masks]
        state = silu_parts(conv_rows(pre_ref[:, :256], state_taps[...], masks))[0]
        wr_ref[...] = bf(state)
        pairs = product_right(bf(state[:, NSTATE:]), bf(state[:, :NSTATE]))
        affinity[...] = jnp.where(allowed_pairs(lengths), pairs, 0.0)


def weight_copies(place, pieces, weights, arrived):
    copies = []
    for v, piece in enumerate(pieces):
        at = pl.multiple_of(place[3 + v] * 128 + (64 if v == 8 else 0), 64)
        target = weights.at[pl.ds(at, piece.shape[0]), :]
        copies.append(pltpu.make_async_copy(piece, target, arrived.at[v]))
    return copies


def start_weights(place, pieces, weights, arrived):
    copies = weight_copies(place, pieces, weights, arrived)
    for copy in copies:
        copy.start()
    return copies


def put_mix_out(parts, mix_out):
    for s in range(8):
        rows = slice(s * HDIM, (s + 1) * HDIM)
        mix_out[rows, :512] = parts[s * 128 : s * 128 + 64, :]
        mix_out[rows, 512:] = parts[s * 128 + 64 : (s + 1) * 128, :]


def mixer_forward_kernel(
    place, lengths, p0, p1, p2, p3, table, state_taps, params, w0, w1, w2, w3, w4, w5, w6, w7, w8,
    send, keep, own_normed, gate_pre, input_pre, rest_pre, inside, scaled,
    normed, pre, all_scaled, affinity, step_ref, run_ref, run_t, wr_ref, mask_ref, squares,
    mix_out, weights, arrived, rest_sent,
):
    j = pl.program_id(0)
    rest_copy = pltpu.make_async_copy(pre.at[:, 1024:], rest_pre, rest_sent)

    @pl.when(j == 0)
    def _():
        pieces = (w0, w1, w2, w3, w4, w5, w6, w7, w8)
        copies = start_weights(place, [p.at[:, :1920] for p in pieces], weights, arrived)
        put_pieces(place, (p0, p1, p2, p3), normed)
        own = pl.ds(pl.multiple_of(place[2] * 128, 128), 128)
        own_normed[...] = normed[:, own]
        squares[...] = jnp.zeros_like(squares)
        for copy in copies:
            copy.wait()
        pre[...] = product(normed[...], weights[:, :1408])
        put_mix_out(weights.at[:, 1408:], mix_out)
        rest_copy.start()

    shared_setup(
        j, lengths, pre.at[:, 1024:], state_taps, params, affinity, step_ref, run_ref, run_t,
        wr_ref, mask_ref,
    )
    columns = pl.ds(pl.multiple_of(j * 128, 128), 128)
    masks = [mask_ref[k] for k in range(KCONV - 1)]
    before = pre[:, pl.ds(pl.multiple_of(512 + j * 128, 128), 128)]
    input_pre[...] = before
    values = silu_parts(conv_rows(before, table[:, columns], masks))[0]
    step = by_head(*[head_columns(j, i, step_ref[...]) for i in range(2)])
    steps = bf(values * step)
    inner = []
    for r in range(2):
        seen = (r + 1) * HALF
        pairs = affinity[r * HALF : seen, :seen]
        parts = []
        for i in range(2):
            run = head_columns(j, i, run_ref[r * HALF : seen, :])
            run_row = run_t[pl.ds(2 * j + i, 1), :seen]
            mixing = bf(pairs * decay_block(run, run_row))
            parts.append(product(mixing, steps[:seen, i * HDIM : (i + 1) * HDIM]))
        inner.append(jnp.concatenate(parts, axis=1))
    inner = jnp.concatenate(inner, axis=0)
    inside[...] = inner
    skip = by_head(*[head_columns(j, i, params[2:3, :]) for i in range(2)])
    gate = pre[:, columns]
    gate_pre[...] = gate
    gated = (inner + skip * values) * silu_parts(gate)[0]
    low = bf(gated * table[4:5, columns])
    all_scaled[:, columns] = low
    scaled[...] = low
    squares[...] += jnp.broadcast_to(jnp.sum(gated * gated, axis=1, keepdims=True), (ROWS, 128))

    @pl.when(j == 3)
    def _():
        for out, half in ((send, 1 - place[0]), (keep, place[0])):
            at = pl.ds(pl.multiple_of(half * HALF, HALF), HALF)
            out[:, :1024] = bf(product(all_scaled[at, :], mix_out[...]))
            out[:, 1024:] = bf(squares[at, :])
        rest_copy.wait()


def by_columns():
    return pl.BlockSpec((ROWS, 128), lambda j: (0, j))


def mixer_forward(place, lengths, pieces, weights, table, state_taps, params):
    f32, low = (jnp.float32, jnp.bfloat16)
    shapes = [
        ((HALF, 1152), low, whole((HALF, 1152))),
        ((HALF, 1152), low, whole((HALF, 1152))),
        ((ROWS, 128), low, whole((ROWS, 128))),
        ((ROWS, 512), f32, by_columns()),
        ((ROWS, 512), f32, by_columns()),
        ((ROWS, 384), f32, pl.BlockSpec(memory_space=pl.ANY)),
        ((ROWS, 512), f32, by_columns()),
        ((ROWS, 512), low, by_columns()),
    ]
    return pl.pallas_call(
        mixer_forward_kernel,
        grid=(4,),
        in_specs=[scalars(), scalars()]
        + [whole(a.shape) for a in (*pieces, table, state_taps, params)]
        + [pl.BlockSpec(memory_space=pl.ANY)] * 9,
        out_specs=[spec for _, _, spec in shapes],
        out_shape=[jax.ShapeDtypeStruct(s, t) for s, t, _ in shapes],
        scratch_shapes=[
            pltpu.VMEM((ROWS, 1024), low),
            pltpu.VMEM((ROWS, 1408), f32),
            pltpu.VMEM((ROWS, 512), low),
            pltpu.VMEM((ROWS, ROWS), f32),
            pltpu.VMEM((ROWS, 128), f32),
            pltpu.VMEM((ROWS, 128), f32),
            pltpu.VMEM((128, ROWS), f32),
            pltpu.VMEM((ROWS, 256), low),
            pltpu.VMEM((KCONV - 1, ROWS, 128), f32),
            pltpu.VMEM((ROWS, 128), f32),
            pltpu.VMEM((512, 1024), low),
            pltpu.VMEM((1024, 1920), low),
            pltpu.SemaphoreType.DMA((9,)),
            pltpu.SemaphoreType.DMA,
        ],
        compiler_params=kernel_params(),
        cost_estimate=cost(1_000_000, 10_000),
        name="mixer_forward",
    )(place, lengths, *pieces, table, state_taps, params, *weights)


def mixer_backward_kernel(
    place, lengths, g0, g1, g2, g3, table, state_taps, params, gate_pre, input_pre, rest_pre, inside,
    w0, w1, w2, w3, w4, w5, w6, w7, w8,
    send, keep, grads, merged, table_grad, state_taps_grad, params_grad,
    grad_mixed, kappa, affinity, step_ref, run_ref, run_t, wr_ref, mask_ref, pair_grad, run_grad,
    step_grad, out_parts, mix_out, weights, out_arrived, arrived,
):
    j = pl.program_id(0)
    pieces = (w0, w1, w2, w3, w4, w5, w6, w7, w8)
    first_copies = weight_copies(place, [p.at[:, :1408] for p in pieces], weights, arrived)

    @pl.when(j == 0)
    def _():
        copies = weight_copies(place, [p.at[:, 1408:1920] for p in pieces], out_parts, out_arrived)
        for copy in copies + first_copies:
            copy.start()
        for copy in copies:
            copy.wait()

    shared_setup(
        j, lengths, rest_pre, state_taps, params, affinity, step_ref, run_ref, run_t, wr_ref, mask_ref
    )

    @pl.when(j == 0)
    def _():
        for k, piece in enumerate((g0, g1, g2, g3)):
            at = pl.ds(pl.multiple_of(block_index(place, k) * 128, 128), 128)
            merged[at, :] = piece[:128, :1024]
            kappa[at, :] = up(piece[:128, 1024:])
        put_mix_out(out_parts, mix_out)
        grad_mixed[...] = product_right(merged[...], mix_out[...])
        pair_grad[...] = jnp.zeros_like(pair_grad)
        run_grad[...] = jnp.zeros_like(run_grad)
        step_grad[...] = jnp.zeros_like(step_grad)
        params_grad[...] = jnp.zeros_like(params_grad)
        table_grad[...] = jnp.zeros_like(table_grad)
        state_taps_grad[...] = jnp.zeros_like(state_taps_grad)

    columns = pl.ds(pl.multiple_of(j * 128, 128), 128)
    columns_in = pl.ds(pl.multiple_of(512 + j * 128, 128), 128)
    masks = [mask_ref[k] for k in range(KCONV - 1)]
    taps = table[:, columns]
    before = input_pre[...]
    values, values_slope = silu_parts(conv_rows(before, taps, masks))
    step = by_head(*[head_columns(j, i, step_ref[...]) for i in range(2)])
    skip = by_head(*[head_columns(j, i, params[2:3, :]) for i in range(2)])
    steps = bf(values * step)
    gate, gate_slope = silu_parts(gate_pre[...])
    within = inside[...]
    rows = within + skip * values
    gated = rows * gate
    mixed_grad = grad_mixed[:, columns]
    gain_grad = jnp.sum(mixed_grad * gated, axis=0, keepdims=True)
    gated_grad = mixed_grad * table[4:5, columns] - gated * kappa[...]
    grads[:, columns] = bf(gated_grad * rows * gate_slope)
    rows_grad = gated_grad * gate
    rows_low = bf(rows_grad)
    rows_turned = rows_low.T
    steps_grads = []
    for i in range(2):
        run = head_columns(j, i, run_ref[...])
        run_row = run_t[pl.ds(2 * j + i, 1), :]
        lanes = slice(i * HDIM, (i + 1) * HDIM)
        turned = jnp.zeros((HDIM, ROWS), jnp.float32)
        for r in range(2):
            seen = (r + 1) * HALF
            block = slice(r * HALF, seen)
            decay = decay_block(run[block, :], run_row[:, :seen])
            mixing = bf(affinity[block, :seen] * decay)
            mixing_grad = product_right(rows_low[block, lanes], steps[:seen, lanes])
            pair_grad[block, :seen] += mixing_grad * decay
            part = product(rows_turned[lanes, block], mixing)
            if seen < ROWS:
                part = jnp.concatenate(
                    [part, jnp.zeros((HDIM, ROWS - seen), jnp.float32)], axis=1
                )
            turned = turned + part
        steps_grads.append(turned)
    steps_grad = jnp.concatenate(steps_grads, axis=0).T
    lanes_in = lax.broadcasted_iota(jnp.int32, (128, 128), 0)
    lanes_out = lax.broadcasted_iota(jnp.int32, (128, 128), 1)
    to_head = up(lanes_out == 2 * j + lanes_in // HDIM)

    def head_sums(columns_of):
        return jnp.dot(columns_of, to_head, precision=HIGH, preferred_element_type=jnp.float32)

    run_grad[...] += head_sums(up(rows_low) * within - up(steps) * steps_grad)
    step_grad[...] += head_sums(steps_grad * values)
    params_grad[2:3, :] += jnp.sum(head_sums(rows_grad * values), axis=0, keepdims=True)
    conv_grad = (steps_grad * step + skip * rows_grad) * values_slope
    before_grad, taps_grad = conv_back(before, taps, masks, conv_grad)
    grads[:, columns_in] = bf(before_grad)
    for k in range(KCONV):
        table_grad[k : k + 1, columns] = taps_grad[k]
    table_grad[4:5, columns] = gain_grad

    @pl.when(j == 3)
    def _():
        decay_grad = jnp.dot(
            lower((ROWS, ROWS), True), run_grad[...], precision=HIGH,
            preferred_element_type=jnp.float32,
        )
        rate = jnp.exp(params[1:2, :])
        step_total = step_grad[...] - decay_grad * rate
        slope = 1.0 / (1.0 + jnp.exp(-(rest_pre[:, 256:] + params[0:1, :])))
        lanes = lax.broadcasted_iota(jnp.int32, (1, 128), 1)
        step_total = jnp.where(lanes < 8, step_total * slope, 0.0)
        grads[:, 1280:] = bf(step_total)
        params_grad[0:1, :] = jnp.sum(step_total, axis=0, keepdims=True)
        params_grad[1:2, :] = jnp.sum(
            -decay_grad * step_ref[...] * rate, axis=0, keepdims=True
        )
        pairs = jnp.where(allowed_pairs(lengths), pair_grad[...], 0.0)
        read_grad = product(bf(pairs), wr_ref[:, :NSTATE])
        write_grad = product(bf(pairs.T), wr_ref[:, NSTATE:])
        wide = [jnp.concatenate([mask, mask], axis=1) for mask in masks]
        state_before = rest_pre[:, :256]
        state_slope = silu_parts(conv_rows(state_before, state_taps[...], wide))[1]
        state_grad, state_taps_parts = conv_back(
            state_before,
            state_taps[...],
            wide,
            jnp.concatenate([write_grad, read_grad], axis=1) * state_slope,
        )
        grads[:, 1024:1280] = bf(state_grad)
        for k in range(KCONV):
            state_taps_grad[k : k + 1, :] = state_taps_parts[k]
        for copy in first_copies:
            copy.wait()
        for out, half in ((send, 1 - place[0]), (keep, place[0])):
            at = pl.ds(pl.multiple_of(half * HALF, HALF), HALF)
            out[:, :1024] = bf(product_right(grads[at, :], weights[...]))
            out[:, 1024:] = grads[at, 1024:1280]


def mixer_backward(place, lengths, pieces, weights, table, state_taps, params, pre, inside):
    gate_pre, input_pre, rest_pre = pre
    f32, low = (jnp.float32, jnp.bfloat16)
    shapes = [
        ((HALF, 1280), low),
        ((HALF, 1280), low),
        ((ROWS, 1408), low),
        ((ROWS, 1024), low),
        ((8, 512), f32),
        ((8, 256), f32),
        ((8, 128), f32),
    ]
    operands = (*pieces, table, state_taps, params)
    return pl.pallas_call(
        mixer_backward_kernel,
        grid=(4,),
        in_specs=[scalars(), scalars()]
        + [whole(a.shape) for a in operands]
        + [by_columns(), by_columns(), whole(rest_pre.shape), by_columns()]
        + [pl.BlockSpec(memory_space=pl.ANY)] * 9,
        out_specs=[whole(s) for s, _ in shapes],
        out_shape=[jax.ShapeDtypeStruct(s, t) for s, t in shapes],
        scratch_shapes=[
            pltpu.VMEM((ROWS, 512), f32),
            pltpu.VMEM((ROWS, 128), f32),
            pltpu.VMEM((ROWS, ROWS), f32),
            pltpu.VMEM((ROWS, 128), f32),
            pltpu.VMEM((ROWS, 128), f32),
            pltpu.VMEM((128, ROWS), f32),
            pltpu.VMEM((ROWS, 256), low),
            pltpu.VMEM((KCONV - 1, ROWS, 128), f32),
            pltpu.VMEM((ROWS, ROWS), f32),
            pltpu.VMEM((ROWS, 128), f32),
            pltpu.VMEM((ROWS, 128), f32),
            pltpu.VMEM((1024, 512), low),
            pltpu.VMEM((512, 1024), low),
            pltpu.VMEM((1024, 1408), low),
            pltpu.SemaphoreType.DMA((9,)),
            pltpu.SemaphoreType.DMA((9,)),
        ],
        compiler_params=kernel_params(),
        cost_estimate=cost(1_000_000, 10_000),
        name="mixer_backward",
    )(place, lengths, *operands, gate_pre, input_pre, rest_pre, inside, *weights)


def patch_mask():
    rows = lax.broadcasted_iota(jnp.int32, (128, 128), 0)
    columns = lax.broadcasted_iota(jnp.int32, (128, 128), 1)
    return (rows >= columns) & (rows // PATCH == columns // PATCH)


def patch_probs(queries, keys, mask):
    scores = product_right(queries * jnp.bfloat16(HDIM ** (-0.5)), keys)
    scores = jnp.where(mask, scores, -1e30)
    weights = jnp.exp(scores - jnp.max(scores, axis=1, keepdims=True))
    return weights * (1.0 / jnp.sum(weights, axis=1, keepdims=True))


def split_blocks(values, keep, send):
    for k, out in ((0, keep), (1, send), (2, keep), (3, send)):
        out[k // 2] = bf(values[k * 128 : (k + 1) * 128, :])


def put_w_out(weights, w_out):
    for s in range(8):
        for q in range(4):
            at = s * 128 + q * 32
            w_out[s * 32 : (s + 1) * 32, q * 256 : (q + 1) * 256] = weights[at : at + 32, 768:]


def attend_forward_kernel(
    place, x0, x1, x2, x3, w0, w1, w2, w3, w4, w5, w6, w7, w8,
    keep, send, rows, qkv, context, w_out, weights, arrived,
):
    pieces = [p.at[:, 1920:] for p in (w0, w1, w2, w3, w4, w5, w6, w7, w8)]
    for copy in start_weights(place, pieces, weights, arrived):
        copy.wait()
    put_w_out(weights, w_out)
    for k, piece in enumerate((x0, x1, x2, x3)):
        rows[k * 128 : (k + 1) * 128, :] = piece[...]
    qkv[...] = bf(product(rows[...], weights[:, :768]))
    mask = patch_mask()
    for b in range(4):
        at = slice(b * 128, (b + 1) * 128)
        outs = []
        for h in range(4):
            q, k, v = (qkv[at, n * 256 + h * HDIM : n * 256 + (h + 1) * HDIM] for n in range(3))
            outs.append(product(bf(patch_probs(q, k, mask)), v))
        context[at, :] = bf(jnp.concatenate(outs, axis=1))
    split_blocks(product(context[...], w_out[...]), keep, send)


def attend_forward(place, pieces, weights):
    low = jnp.bfloat16
    shapes = [(2, 128, 1024), (2, 128, 1024), (ROWS, 1024), (ROWS, 768), (ROWS, 256)]
    return pl.pallas_call(
        attend_forward_kernel,
        grid=(1,),
        in_specs=[scalars()]
        + [whole(a.shape) for a in pieces]
        + [pl.BlockSpec(memory_space=pl.ANY)] * 9,
        out_specs=[whole(s) for s in shapes],
        out_shape=[jax.ShapeDtypeStruct(s, low) for s in shapes],
        compiler_params=kernel_params(),
        scratch_shapes=[
            pltpu.VMEM((256, 1024), low),
            pltpu.VMEM((1024, 1024), low),
            pltpu.SemaphoreType.DMA((9,)),
        ],
        cost_estimate=cost(1_000_000, 10_000),
        name="attend_forward",
    )(place, *pieces, *weights)


def attend_backward_kernel(
    place, g0, g1, g2, g3, qkv, w0, w1, w2, w3, w4, w5, w6, w7, w8,
    keep, send, rows, qkv_grad, w_out, weights, arrived,
):
    pieces = [p.at[:, 1920:] for p in (w0, w1, w2, w3, w4, w5, w6, w7, w8)]
    for copy in start_weights(place, pieces, weights, arrived):
        copy.wait()
    put_w_out(weights, w_out)
    for k, piece in enumerate((g0, g1, g2, g3)):
        rows[k * 128 : (k + 1) * 128, :] = piece[...]
    context_grad = product_right(rows[...], w_out[...])
    mask = patch_mask()
    for b in range(4):
        at = slice(b * 128, (b + 1) * 128)
        outs = [[], [], []]
        for h in range(4):
            q, k, v = (qkv[at, n * 256 + h * HDIM : n * 256 + (h + 1) * HDIM] for n in range(3))
            probs = patch_probs(q, k, mask)
            grad = bf(context_grad[at, h * HDIM : (h + 1) * HDIM])
            probs_grad = product_right(grad, v)
            mean = jnp.sum(probs * probs_grad, axis=1, keepdims=True)
            scores_grad = probs * (probs_grad - mean) * HDIM ** (-0.5)
            outs[0].append(product(bf(scores_grad), k))
            outs[1].append(product(bf(scores_grad.T), q))
            outs[2].append(product(bf(probs.T), grad))
        qkv_grad[at, :] = bf(jnp.concatenate(outs[0] + outs[1] + outs[2], axis=1))
    split_blocks(product_right(qkv_grad[...], weights[:, :768]), keep, send)


def attend_backward(place, pieces, qkv, weights):
    low = jnp.bfloat16
    shapes = [(2, 128, 1024), (2, 128, 1024), (ROWS, 1024), (ROWS, 768)]
    return pl.pallas_call(
        attend_backward_kernel,
        grid=(1,),
        in_specs=[scalars()]
        + [whole(a.shape) for a in (*pieces, qkv)]
        + [pl.BlockSpec(memory_space=pl.ANY)] * 9,
        out_specs=[whole(s) for s in shapes],
        out_shape=[jax.ShapeDtypeStruct(s, low) for s in shapes],
        compiler_params=pltpu.CompilerParams(vmem_limit_bytes=VMEM_BYTES),
        scratch_shapes=[
            pltpu.VMEM((256, 1024), low),
            pltpu.VMEM((1024, 1024), low),
            pltpu.SemaphoreType.DMA((9,)),
        ],
        cost_estimate=cost(1_000_000, 10_000),
        name="attend_backward",
    )(place, *pieces, qkv, *weights)


def feed_copies(place, pieces, weights, arrived, j):
    chunk = pl.multiple_of(j * 256, 256)
    copies = []
    for n, start in enumerate((chunk, pl.multiple_of(1024 + chunk, 256))):
        at = pl.ds(start, 256)
        copies += weight_copies(
            place, [p.at[:, at] for p in pieces], weights.at[:, at], arrived.at[2 * j + n]
        )
    return copies


def down_copies(place, pieces, weights, arrived):
    return weight_copies(
        place, [p.at[:, 2048:] for p in pieces], weights.at[:, 2048:], arrived.at[8]
    )


def feed_kernel(
    place, x0, x1, x2, x3, out_grad, w0, w1, w2, w3, w4, w5, w6, w7, w8,
    keep, send, out_keep, out_send, rows, hidden, gate_grad, up_grad,
    weights, total, total_out, arrived,
):
    j = pl.program_id(0)
    pieces = (w0, w1, w2, w3, w4, w5, w6, w7, w8)

    @pl.when(j == 0)
    def _():
        for copy in feed_copies(place, pieces, weights, arrived, 0):
            copy.start()
        for copy in down_copies(place, pieces, weights, arrived):
            copy.start()
        for k in range(1, 4):
            for copy in feed_copies(place, pieces, weights, arrived, k):
                copy.start()
        for k, piece in enumerate((x0, x1, x2, x3)):
            rows[k * 128 : (k + 1) * 128, :] = piece[...]
        total[...] = jnp.zeros_like(total)
        total_out[...] = jnp.zeros_like(total_out)

    for copy in feed_copies(place, pieces, weights, arrived, j):
        copy.wait()

    @pl.when(j == 0)
    def _():
        for copy in down_copies(place, pieces, weights, arrived):
            copy.wait()

    chunk = pl.multiple_of(j * 256, 256)
    w_gate = weights[:, pl.ds(chunk, 256)]
    w_up = weights[:, pl.ds(pl.multiple_of(1024 + chunk, 256), 256)]
    w_down = weights[pl.ds(chunk, 256), 2048:]
    gate, slope = silu_parts(product(rows[...], w_gate))
    lift = product(rows[...], w_up)
    units = bf(gate * lift)
    hidden[...] = units
    units_grad = product_right(out_grad[...], w_down)
    gate_low = bf(units_grad * lift * slope)
    up_low = bf(units_grad * gate)
    gate_grad[...] = gate_low
    up_grad[...] = up_low
    total[...] += product_right(gate_low, w_gate) + product_right(up_low, w_up)
    total_out[...] += product(units, w_down)

    @pl.when(j == pl.num_programs(0) - 1)
    def _():
        split_blocks(total, keep, send)
        split_blocks(total_out, out_keep, out_send)


def feed(place, pieces, out_grad, weights):
    low = jnp.bfloat16
    pair = (2, 128, 1024)
    column = pl.BlockSpec((ROWS, 256), lambda j: (0, j))
    return pl.pallas_call(
        feed_kernel,
        grid=(4,),
        in_specs=[scalars()]
        + [whole(a.shape) for a in (*pieces, out_grad)]
        + [pl.BlockSpec(memory_space=pl.ANY)] * 9,
        out_specs=[whole(pair)] * 4 + [whole((ROWS, 1024)), column, column, column],
        out_shape=[jax.ShapeDtypeStruct(pair, low)] * 4
        + [jax.ShapeDtypeStruct((ROWS, 1024), low)] * 4,
        scratch_shapes=[
            pltpu.VMEM((1024, 3072), low),
            pltpu.VMEM((ROWS, 1024), jnp.float32),
            pltpu.VMEM((ROWS, 1024), jnp.float32),
            pltpu.SemaphoreType.DMA((9, 9)),
        ],
        compiler_params=kernel_params(),
        cost_estimate=cost(1_000_000, 10_000),
        name="feed",
    )(place, *pieces, out_grad, *weights)


def put_by_target(place, values, out):
    for s in range(8):
        out[place[12 + s], :, : values.shape[1]] = values[s * 128 : (s + 1) * 128, :]


def feed_grads_kernel(place, rows, gate_grad, up_grad, hidden, out_grad, grads, turned):
    j = pl.program_id(0)

    @pl.when(j == 0)
    def _():
        turned[...] = rows[...].T

    @pl.when(j == 4)
    def _():
        turned[...] = hidden[...].T

    columns = pl.ds(pl.multiple_of((j % 2) * 512, 512), 512)
    for first, right in ((0, gate_grad), (2, up_grad), (4, out_grad)):

        @pl.when((j >= first) & (j < first + 2))
        def _():
            put_by_target(place, bf(product(turned[...], right[:, columns])), grads)


def feed_grads(place, rows, gate_grad, up_grad, hidden, out_grad):
    low = jnp.bfloat16
    return pl.pallas_call(
        feed_grads_kernel,
        grid=(6,),
        in_specs=[scalars()] + [whole((ROWS, 1024))] * 5,
        out_specs=pl.BlockSpec((8, 128, 512), lambda j: (0, 0, j)),
        out_shape=jax.ShapeDtypeStruct((8, 128, 3072), low),
        scratch_shapes=[pltpu.VMEM((1024, ROWS), low)],
        compiler_params=kernel_params(),
        cost_estimate=cost(1_000_000, 10_000),
        name="feed_grads",
    )(place, rows, gate_grad, up_grad, hidden, out_grad)


def attend_grads_kernel(place, rows, qkv_grad, context, middle_grad, grads):
    put_by_target(place, bf(product(rows[...].T, qkv_grad[...])), grads)
    out_grad = bf(product(context[...].T, middle_grad[...]))
    for s in range(8):
        for q in range(4):
            grads[place[12 + s], q * 32 : (q + 1) * 32, 768:] = out_grad[
                s * 32 : (s + 1) * 32, q * 256 : (q + 1) * 256
            ]


def attend_grads(place, rows, qkv_grad, context, middle_grad):
    operands = (rows, qkv_grad, context, middle_grad)
    return pl.pallas_call(
        attend_grads_kernel,
        grid=(1,),
        in_specs=[scalars()] + [whole(a.shape) for a in operands],
        out_specs=whole((8, 128, 1024)),
        out_shape=jax.ShapeDtypeStruct((8, 128, 1024), jnp.bfloat16),
        compiler_params=kernel_params(),
        cost_estimate=cost(1_000_000, 10_000),
        name="attend_grads",
    )(place, *operands)


def placed_kernel(turned, place, p0, p1, p2, p3, weights, rows, result):
    put_pieces(place, (p0, p1, p2, p3), rows)
    left = rows[:, :1024]
    result[...] = bf(product_right(left, weights[...]) if turned else product(left, weights[...]))


def placed_product(place, pieces, weights, turned):
    width = pieces[0].shape[1]
    low = jnp.bfloat16
    return pl.pallas_call(
        partial(placed_kernel, turned),
        in_specs=[scalars()] + [whole(a.shape) for a in (*pieces, weights)],
        out_specs=[whole((ROWS, width)), whole((ROWS, 256))],
        grid=(1,),
        out_shape=[
            jax.ShapeDtypeStruct((ROWS, width), low),
            jax.ShapeDtypeStruct((ROWS, 256), low),
        ],
        compiler_params=kernel_params(),
        cost_estimate=cost(1_000_000, 10_000),
        name="placed_product",
    )(place, *pieces, weights)


PAIR_C = [(i, i ^ 1) for i in range(4)]
PAIR_Y = [(i, i ^ 2) for i in range(4)]


def swap_c(shard):
    return lax.ppermute(shard, "mp", PAIR_C)


def swap_y(shard):
    return lax.ppermute(shard, "mp", PAIR_Y)


def swap_seq(shard, by):
    return lax.ppermute(shard, "seq", [(i, i ^ by) for i in range(8)])


RING = (0, 2, 4, 6, 7, 5, 3, 1)
UP = [(RING[i], RING[(i + 1) % 8]) for i in range(8)]
DOWN = [(b, a) for a, b in UP]
REACH = (0, -1, 1, -2, 2, -3, 3, 4, 4)


def swap_up(shard):
    return lax.ppermute(shard, "seq", UP)


def swap_down(shard):
    return lax.ppermute(shard, "seq", DOWN)


def chosen(index, values):
    places = jnp.arange(len(values), dtype=jnp.int32)
    return jnp.sum(jnp.where(index[..., None] == places, jnp.array(values, jnp.int32), 0), axis=-1)


def places_of(c, y, s):
    at = [RING.index(k) for k in range(8)]
    own = chosen(s, at)
    owners = chosen((own + jnp.array(REACH, jnp.int32) + 8) % 8, RING)
    ahead = (jnp.array(at, jnp.int32) - own + 8) % 8
    return jnp.concatenate([jnp.stack([c, y, s]), owners, ahead]).astype(jnp.int32)


class RingGather:
    def __init__(self, shard):
        self.pieces = [shard]
        self.flying = [shard, shard]

    def step(self):
        ahead, behind = self.flying
        if len(self.pieces) == 7:
            ahead, behind = (ahead[:64], behind[64:])
        self.flying = [swap_up(ahead), swap_down(behind)]

    def landed(self, value):
        value, self.flying = lax.optimization_barrier((value, self.flying))
        self.pieces = self.pieces + self.flying
        return value


class RingSum:
    def __init__(self, blocks):
        self.blocks = blocks
        self.flying = None
        self.count = 0

    def step(self):
        if self.count == 0:
            far = self.blocks[4]
            sent = [far[:64], far[64:]]
        elif self.count == 1:
            ahead, behind = (self.blocks[3], self.blocks[5])
            sent = [
                jnp.concatenate([bf(up(ahead[:64]) + up(self.flying[0])), ahead[64:]]),
                jnp.concatenate([behind[:64], bf(up(behind[64:]) + up(self.flying[1]))]),
            ]
        else:
            sent = [
                bf(up(self.blocks[k]) + up(part))
                for k, part in zip((4 - self.count, 4 + self.count), self.flying, strict=True)
            ]
        self.flying = [swap_up(sent[0]), swap_down(sent[1])]
        self.count += 1

    def landed(self, value):
        value, self.flying = lax.optimization_barrier((value, self.flying))
        return value

    def held(self, value):
        value, self.blocks, self.flying = lax.optimization_barrier(
            (value, self.blocks, self.flying)
        )
        return value

    def result(self):
        return up(self.blocks[0]) + up(self.flying[0]) + up(self.flying[1])


def pick(stacked, index):
    return lax.dynamic_index_in_dim(stacked, index, 0, keepdims=False)


def over_seq(rows):
    return lax.all_to_all(rows, "seq", 0, 0, tiled=True)


def over_all(blocks):
    return lax.all_to_all(blocks, ("seq", "mp"), 0, 0, tiled=True)


def from_all_seq(rows):
    return over_seq(jnp.broadcast_to(rows[None], (8, *rows.shape)))


def sum_rows(send, keep, y):
    total = up(keep) + up(swap_c(send))
    parts = total.reshape(2, 128, -1)
    return pick(parts, y) + up(swap_y(bf(pick(parts, 1 - y))))


def gather_rows(rows):
    far = swap_y(rows)
    return [rows, far, swap_c(rows), swap_c(far)]


def alike(parts):
    return (parts[0] + parts[2]) + (parts[1] + parts[3])


def sum_group(partial, c, y):
    halves = bf(partial).reshape(2, HALF, -1)
    return bf(sum_rows(pick(halves, 1 - c), pick(halves, c), y))


def sum_seq(rows):
    return jnp.sum(up(over_seq(rows.reshape(8, 16, -1))), axis=0)


def gather_bytes(rows):
    far = swap_y(rows)
    return [rows, swap_c(rows), far, swap_c(far)]


def sum_bytes(keep, send):
    got = up(keep) + up(swap_c(send))
    return got[0] + up(swap_y(bf(got[1])))


def placed(parts, m):
    blocks = jnp.stack(parts)
    return jnp.concatenate([pick(blocks, m ^ k) for k in range(4)], axis=0)


def to_bytes(columns):
    got = over_all(columns.reshape(32, 16, 256))
    return got.reshape(8, 4, 16, 256).transpose(2, 1, 0, 3).reshape(128, E)


def to_columns(rows):
    sent = rows.reshape(16, 4, 8, 256).transpose(2, 1, 0, 3).reshape(32, 16, 256)
    return over_all(sent).reshape(ROWS, 256)


def split_plan(
    byte_input,
    seq_lengths,
    cotangent,
    gain_global,
    patch_in,
    mixer_gate,
    mixer_input,
    mixer_state,
    mixer_step,
    conv_input,
    conv_state,
    step_bias,
    decay_log,
    skip_gain,
    gain_mixer,
    mixer_out,
    patch_out,
    gain_attend,
    attend_query,
    attend_key,
    attend_value,
    attend_out,
    gain_feed,
    feed_gate,
    feed_up,
    feed_down,
):
    s, m = (lax.axis_index("seq"), lax.axis_index("mp"))
    y, c = (m // 2, m % 2)
    place = places_of(c, y, s)
    f32 = jnp.float32

    out_halves = mixer_out.reshape(64, 2, 512).transpose(1, 0, 2).reshape(128, 512)
    out_quarters = attend_out.reshape(32, 4, 256).transpose(1, 0, 2).reshape(128, 256)
    w_mixer = RingGather(jnp.concatenate(
        [
            mixer_gate,
            mixer_input,
            mixer_state,
            mixer_step,
            jnp.zeros((128, 120), jnp.bfloat16),
            out_halves,
            attend_query,
            attend_key,
            attend_value,
            out_quarters,
        ],
        axis=1,
    ))
    w_mixer.step()
    table = jnp.concatenate([conv_input, gain_mixer[None], jnp.zeros((3, 512), f32)], axis=0)
    state_taps = jnp.concatenate([conv_state, jnp.zeros((4, 256), f32)], axis=0)
    params = jnp.pad(jnp.stack([step_bias, decay_log, skip_gain]), ((0, 5), (0, 120)))

    own_slots = lax.dynamic_slice_in_dim(byte_input.reshape(64, PATCH, E), 2 * m, 2, 1)
    columns_in = over_seq(own_slots.reshape(64, 8, 256).transpose(1, 0, 2)).reshape(ROWS, 256)
    w_patch = patch_out.reshape(128, 8, 256).transpose(1, 0, 2)
    w_feed = jnp.concatenate([feed_gate, feed_up, feed_down], axis=1)
    columns_in, place, table, state_taps, params, w_patch, w_feed = w_mixer.landed(
        (columns_in, place, table, state_taps, params, w_patch, w_feed)
    )
    w_feed = RingGather(w_feed)
    w_mixer.step()
    rows = sum_group(product(columns_in, patch_in), c, y)
    hidden = w_mixer.landed(bf(sum_seq(rows)))
    w_mixer.step()
    hidden = up(w_mixer.landed(from_all_seq(hidden).reshape(128, 1024)))
    w_mixer.step()
    w_feed.step()
    normed_parts = w_mixer.landed(gather_rows(bf(rms_scale(hidden, gain_global))))

    normed_parts, w_patch = lax.optimization_barrier((normed_parts, w_patch))
    send, keep, own_normed, *pre, inside, scaled = mixer_forward(
        place, seq_lengths, normed_parts, w_mixer.pieces, table, state_taps, params
    )
    send, w_patch = lax.optimization_barrier((send, over_seq(w_patch)))
    w_patch = w_patch.reshape(1024, 256)
    sums = w_feed.landed(sum_rows(send, keep, y))
    w_feed.step()
    unscaled, root = (sums[:, :1024], lax.rsqrt(sums[:, 1024:1025] / DI + EPS))
    merged_parts = gather_rows(bf(hidden + root * unscaled))
    merged_low, slots = placed_product(place, merged_parts, w_patch, False)
    slots = w_feed.landed(to_bytes(slots))
    w_feed.step()
    residual = up(lax.dynamic_slice_in_dim(byte_input, m * 128, 128, 0)) + slots

    attend_parts = gather_bytes(bf(rms_scale(residual, gain_attend)))
    keep, send, attend_in, qkv, context = attend_forward(place, attend_parts, w_mixer.pieces)
    send = w_feed.landed(send)
    w_feed.step()
    middle = residual + sum_bytes(keep, send)
    feed_parts = w_feed.landed(gather_bytes(bf(rms_scale(middle, gain_feed))))
    cot_blocks = cotangent.reshape(4, 128, E)
    cot_rows = pick(cot_blocks, m)
    out_low = jnp.concatenate([bf(pick(cot_blocks, m ^ k)) for k in range(4)], axis=0)
    keep, send, out_keep, out_send, feed_in, hidden_units, grad_gate, grad_up = feed(
        place, feed_parts, out_low, w_feed.pieces
    )
    grads = feed_grads(place, feed_in, grad_gate, grad_up, hidden_units, out_low)
    grad_feed_in, grads = lax.optimization_barrier((sum_bytes(keep, send), grads))
    feed_sums = RingSum(grads)
    feed_sums.step()
    grad_middle_part, gain_feed_part = rms_back(middle, gain_feed, grad_feed_in)
    grad_middle = cot_rows + grad_middle_part
    keep, send, middle_low, grad_qkv = attend_backward(
        place, gather_bytes(bf(grad_middle)), qkv, w_mixer.pieces
    )
    send = feed_sums.landed(send)
    feed_sums.step()
    grads = attend_grads(place, attend_in, grad_qkv, context, middle_low)
    grad_attend_in, grads = lax.optimization_barrier((sum_bytes(keep, send), grads))
    attend_sums = RingSum(grads)
    grad_residual_part, gain_attend_part = rms_back(residual, gain_attend, grad_attend_in)
    grad_residual = grad_middle + grad_residual_part

    slot_grad, out_send = lax.optimization_barrier(
        (to_columns(bf(grad_residual)), swap_c(out_send))
    )
    slot_grad = feed_sums.landed(slot_grad)
    feed_sums.step()
    grad_patch_out = bf(product_left(merged_low, slot_grad)).reshape(8, 128, 256)
    rows = sum_group(product_right(slot_grad, w_patch), c, y)
    out_parts = up(out_keep) + up(out_send)
    rows, out_far = lax.optimization_barrier((rows, bf(out_parts[1])))
    merged_rows, out_far = lax.optimization_barrier((sum_seq(rows), swap_y(out_far)))
    out_rows = bf(middle + out_parts[0] + up(out_far))
    merged_rows = feed_sums.landed(merged_rows)
    gains = jnp.stack([gain_feed_part, gain_attend_part])
    got = from_all_seq(
        bf(jnp.concatenate([merged_rows, gains, jnp.zeros((6, 1024), f32)], axis=0))
    )
    got, out_far, out_near = lax.optimization_barrier((got, swap_y(out_rows), swap_c(out_rows)))
    got = feed_sums.held(got)
    feed_sums.step()
    grad_merged = up(got[:, :16].reshape(128, 1024))
    gains = jnp.sum(up(got[:, 16:18]), axis=0)
    kappa = jnp.sum(grad_merged * unscaled, axis=1, keepdims=True) * root**3 / DI
    rows = jnp.concatenate([grad_merged * root, jnp.broadcast_to(kappa, (128, 128))], axis=1)
    merged_parts = gather_rows(
        bf(jnp.concatenate([rows, jnp.pad(gains, ((0, 6), (0, 128)))], axis=0))
    )
    merged_parts, grad_patch_out = attend_sums.held((merged_parts, grad_patch_out))
    attend_sums.step()
    out_both = swap_c(out_far)
    grad_patch_out = over_seq(grad_patch_out)
    gains = alike([up(part[128:130, :1024]) for part in merged_parts])
    send, keep, grads, merged_grad, table_grad, state_taps_grad, params_grad = mixer_backward(
        place,
        seq_lengths,
        merged_parts,
        w_mixer.pieces,
        table,
        state_taps,
        params,
        pre,
        inside,
    )
    send, grad_patch_out, out_both = feed_sums.landed((send, grad_patch_out, out_both))
    send = attend_sums.landed(send)
    attend_sums.step()
    feed_sums = feed_sums.result()
    byte_output = placed([out_rows, out_near, out_far, out_both], m)
    sums = sum_rows(send, keep, y)
    grad_hidden_part, gain_global_part = rms_back(hidden, gain_global, sums[:, :1024])
    rows = jnp.concatenate([grad_merged + grad_hidden_part, sums[:, 1024:]], axis=1)
    small = jnp.stack([gain_global_part, state_taps_grad[:4].reshape(1024)])
    hidden_parts = gather_rows(
        bf(jnp.concatenate([rows, jnp.pad(small, ((0, 6), (0, 256)))], axis=0))
    )
    hidden_parts = attend_sums.landed(hidden_parts)
    attend_sums.step()
    small = alike([up(part[128:130, :1024]) for part in hidden_parts])
    hidden_rows, back = placed_product(place, hidden_parts, patch_in, True)
    hidden_grad = hidden_rows[:, :1024]
    back, grad_patch_in, grad_mixer_state = lax.optimization_barrier(
        (
            to_bytes(back),
            product_left(columns_in, hidden_grad),
            product_left(own_normed, hidden_rows[:, 1024:]),
        )
    )
    grad_rows = attend_sums.landed(bf(grad_residual + back))
    attend_sums.step()
    grad_input = placed(gather_bytes(grad_rows), m)
    attend_sums = attend_sums.result()

    first_grad = product_left(own_normed, grads)
    own_scaled = lax.dynamic_slice_in_dim(scaled, s * HDIM, HDIM, 1)
    return (
        byte_output,
        grad_input,
        small[0],
        grad_patch_in,
        first_grad[:, :512],
        first_grad[:, 512:1024],
        grad_mixer_state,
        first_grad[:, 1280:1288],
        table_grad[:4],
        small[1].reshape(4, 256),
        params_grad[0, :8],
        params_grad[1, :8],
        params_grad[2, :8],
        table_grad[4],
        product_left(own_scaled, merged_grad),
        grad_patch_out.transpose(1, 0, 2).reshape(128, 2048).astype(f32),
        gains[1],
        attend_sums[:, :256],
        attend_sums[:, 256:512],
        attend_sums[:, 512:768],
        attend_sums[:, 768:].reshape(4, 32, 256).transpose(1, 0, 2).reshape(32, 1024),
        gains[0],
        feed_sums[:, :1024],
        feed_sums[:, 1024:2048],
        feed_sums[:, 2048:],
    )


def solution(mesh):
    in_specs = (
        P("seq", None),
        P(),
        P("seq", None),
        P(),
        P(("mp", "seq"), None),
        P("seq", "mp"),
        P("seq", "mp"),
        P("seq", None),
        P("seq", "mp"),
        P(None, "mp"),
        P(),
        P("mp"),
        P("mp"),
        P("mp"),
        P("mp"),
        P(("mp", "seq"), None),
        P("seq", "mp"),
        P(),
        P("seq", "mp"),
        P("seq", "mp"),
        P("seq", "mp"),
        P(("mp", "seq"), None),
        P(),
        P("seq", "mp"),
        P("seq", "mp"),
        P(("mp", "seq"), None),
    )
    out_specs = (
        P("seq", None),
        P("seq", None),
        P(),
        P(("mp", "seq"), None),
        P("seq", "mp"),
        P("seq", "mp"),
        P("seq", None),
        P("seq", "mp"),
        P(None, "mp"),
        P(),
        P("mp"),
        P("mp"),
        P("mp"),
        P("mp"),
        P(("mp", "seq"), None),
        P("seq", "mp"),
        P(),
        P("seq", "mp"),
        P("seq", "mp"),
        P("seq", "mp"),
        P(("mp", "seq"), None),
        P(),
        P("seq", "mp"),
        P("seq", "mp"),
        P(("mp", "seq"), None),
    )
    plan = split_plan if (mesh.shape["seq"], mesh.shape["mp"]) == (8, 4) else gathered_plan
    return jax.shard_map(plan, mesh=mesh, in_specs=in_specs, out_specs=out_specs, check_vma=False)
```

```python
from functools import partial

import jax
import jax.numpy as jnp
from jax import lax
from jax.experimental import pallas as pl
from jax.experimental.pallas import tpu as pltpu
from jax.sharding import PartitionSpec as P

E = 1024
HDIM = 64
DI = 2048
NSTATE = 128
KCONV = 4
PATCH = 8
TOK_DEV = 512
BLOCK = 64


EPS = 1e-05
HIGH = lax.Precision.HIGHEST


def shifted(shard, axis, by):
    length = lax.axis_size(axis)
    pairs = [(i, i + by) for i in range(length) if 0 <= i + by < length]
    return lax.ppermute(shard, axis, pairs)


def prefix(shard, axis, combine, identity):
    length, position = (lax.axis_size(axis), lax.axis_index(axis))
    everything = jax.tree.map(
        lambda part, kind: lax.all_gather(part.astype(kind), axis),
        shard,
        (jnp.bfloat16, jnp.bfloat16),
    )
    start = jax.tree.map(
        lambda part, zero: jnp.broadcast_to(jnp.asarray(zero, part.dtype), part.shape),
        shard,
        identity,
    )

    def prefix_turn(k, before):
        reached = k < position
        new = combine(
            before, jax.tree.map(lambda part, own: part[k].astype(own.dtype), everything, shard)
        )
        return jax.tree.map(lambda a, b: jnp.where(reached, a, b), new, before)

    return lax.fori_loop(0, length, prefix_turn, start)


def carried_in(shard, axis, combine, identity):
    length, position = (lax.axis_size(axis), lax.axis_index(axis))
    everything = jax.tree.map(
        lambda part, kind: lax.all_gather(part.astype(kind), axis),
        shard,
        jax.tree.map(lambda a: jnp.bfloat16 if a.dtype == jnp.float32 else a.dtype, shard),
    )
    start = jax.tree.map(
        lambda part, zero: jnp.broadcast_to(jnp.asarray(zero, part.dtype), part.shape),
        shard,
        identity,
    )

    def carried_turn(k, before):
        at = length - 1 - k
        reached = at > position
        new = combine(
            before, jax.tree.map(lambda part, own: part[at].astype(own.dtype), everything, shard)
        )
        return jax.tree.map(lambda a, b: jnp.where(reached, a, b), new, before)

    return lax.fori_loop(0, length, carried_turn, start)


def product(former, latter):
    return jnp.dot(former, latter, preferred_element_type=jnp.float32)


def product_left(former, latter):
    return lax.dot_general(
        former, latter, (((0,), (0,)), ((), ())), preferred_element_type=jnp.float32
    )


def product_right(former, latter):
    return lax.dot_general(
        former, latter, (((1,), (1,)), ((), ())), preferred_element_type=jnp.float32
    )


def over_heads(partial_sum):
    return lax.psum(partial_sum, "mp")


def gather_slots(pieces):
    return lax.all_gather(pieces.astype(jnp.bfloat16), "mp", axis=1, tiled=True).astype(
        pieces.dtype
    )


def rms_scale(values, scale_gain):
    mean_square = jnp.mean(values * values, axis=-1, keepdims=True)
    return values * lax.rsqrt(mean_square + EPS) * scale_gain


def rms_back(values, scale_gain, upstream):
    pullback = jax.vjp(rms_scale, values, scale_gain)[1]
    return pullback(upstream)


def running_bounds(lengths):
    places = jnp.arange(lengths.shape[0])
    upto = places[None, :] <= places[:-1, None]
    return jnp.sum(jnp.where(upto, lengths[None, :], 0), axis=1)


def running_sum(values):
    places = jnp.arange(values.shape[0])
    lower_part = (places[:, None] >= places[None, :]).astype(jnp.float32)
    return jnp.dot(lower_part, values, precision=HIGH, preferred_element_type=jnp.float32)


def segment_of(lengths, start_row, row_count):
    bounds = running_bounds(lengths)
    places = start_row + jnp.arange(row_count, dtype=jnp.int32)
    return jnp.sum((places[:, None] >= bounds[None, :]).astype(jnp.int32), axis=1)


def conv_silu(extended, kernel, segment_rows):
    row_count = extended.shape[0] - KCONV + 1
    segment_now = segment_rows[KCONV - 1 :]
    summed = jnp.zeros((row_count, extended.shape[1]), jnp.float32)
    for offset in range(KCONV):
        same_seq = (segment_rows[offset : offset + row_count] == segment_now)[:, None]
        summed = (
            summed
            + jnp.where(same_seq, extended[offset : offset + row_count], 0.0) * kernel[offset]
        )
    return jax.nn.silu(summed)


def block_output(
    head_values,
    write_vecs,
    read_vecs,
    step_size,
    log_rate,
    skip_term,
    state_value,
    segment_rows,
    segment_prev,
):
    length = head_values.shape[0]
    running = running_sum(-step_size * jnp.exp(log_rate))
    places = jnp.arange(length)
    allowed = (places[:, None] >= places[None, :]) & (
        segment_rows[:, None] == segment_rows[None, :]
    )
    allowed = allowed[:, :, None]
    spread = jnp.where(allowed, running[:, None, :] - running[None, :, :], 0.0)
    factors = jnp.where(allowed, jnp.exp(spread), 0.0)
    affinity = jnp.dot(read_vecs, write_vecs.T, precision=HIGH, preferred_element_type=jnp.float32)
    mixing = factors * affinity[:, :, None] * step_size[None, :, :]
    inside = jnp.einsum("tsh,shp->thp", mixing, head_values, precision=HIGH)
    carried = jnp.where((segment_rows == segment_prev)[:, None], jnp.exp(running), 0.0)
    reading = (
        jnp.einsum("tn,hpn->thp", read_vecs, state_value, precision=HIGH) * carried[:, :, None]
    )
    result = inside + reading + skip_term[None, :, None] * head_values
    return result.reshape(length, -1)


def block_summary(head_values, write_vecs, step_size, log_rate, segment_rows, segment_prev):
    running = running_sum(-step_size * jnp.exp(log_rate))
    latest = running[-1]
    in_tail = (segment_rows == segment_rows[-1])[:, None]
    weights = jnp.where(in_tail, jnp.exp(latest[None, :] - running), 0.0) * step_size
    scaled = weights[:, :, None] * head_values
    state_local = jnp.einsum("shp,sn->hpn", scaled, write_vecs, precision=HIGH)
    decay_total = jnp.where(segment_rows[-1] == segment_prev, jnp.exp(latest), 0.0)
    return (decay_total, state_local)


def combine_state(earlier, later):
    return (earlier[0] * later[0], later[0][:, None, None] * earlier[1] + later[1])


def patch_attention(queries, keys_all, values_all):
    row_count = queries.shape[0]
    head_count = queries.shape[1] // HDIM
    query_rows = queries.reshape(row_count // PATCH, PATCH, head_count, HDIM)
    key_rows = keys_all.reshape(row_count // PATCH, PATCH, head_count, HDIM)
    value_rows = values_all.reshape(row_count // PATCH, PATCH, head_count, HDIM)
    scores = jnp.einsum("bihd,bjhd->bhij", query_rows, key_rows, precision=HIGH) * HDIM ** (-0.5)
    causal = jnp.arange(PATCH)[:, None] >= jnp.arange(PATCH)[None, :]
    scores = jnp.where(causal, scores, -1e30)
    peak = jnp.max(scores, axis=-1, keepdims=True)
    probs = jnp.exp(scores - peak)
    probs = probs / jnp.sum(probs, axis=-1, keepdims=True)
    context = jnp.einsum("bhij,bjhd->bihd", probs, value_rows, precision=HIGH)
    return context.reshape(row_count, head_count * HDIM)


def add_tail(main_rows, tail_rows):
    keep_count = main_rows.shape[0] - tail_rows.shape[0]
    return jnp.concatenate([main_rows[:keep_count], main_rows[keep_count:] + tail_rows], axis=0)


def gathered_plan(
    byte_input,
    seq_lengths,
    cotangent,
    gain_global,
    patch_in,
    mixer_gate,
    mixer_input,
    mixer_state,
    mixer_step,
    conv_input,
    conv_state,
    step_bias,
    decay_log,
    skip_gain,
    gain_mixer,
    mixer_out,
    patch_out,
    gain_attend,
    attend_query,
    attend_key,
    attend_value,
    attend_out,
    gain_feed,
    feed_gate,
    feed_up,
    feed_down,
):
    group_size = lax.axis_size("mp")
    slot_width = PATCH * E // group_size
    slot_start = lax.axis_index("mp") * slot_width
    first_row = lax.axis_index("seq") * BLOCK
    segment_ext = segment_of(seq_lengths, first_row - (KCONV - 1), BLOCK + KCONV - 1)
    segment_rows = segment_ext[KCONV - 1 :]
    segment_prev = segment_of(seq_lengths, first_row - 1, 1)[0]

    def fetch_global():
        return (
            lax.all_gather(patch_in, "seq", axis=0, tiled=True),
            lax.all_gather(mixer_gate, "seq", axis=0, tiled=True),
            lax.all_gather(mixer_input, "seq", axis=0, tiled=True),
            lax.all_gather(mixer_state, "seq", axis=0, tiled=True),
            lax.all_gather(mixer_step, "seq", axis=0, tiled=True),
            lax.all_gather(mixer_out, "seq", axis=0, tiled=True),
            lax.all_gather(patch_out, "seq", axis=0, tiled=True),
        )

    def fetch_local():
        return (
            lax.all_gather(attend_query, "seq", axis=0, tiled=True),
            lax.all_gather(attend_key, "seq", axis=0, tiled=True),
            lax.all_gather(attend_value, "seq", axis=0, tiled=True),
            lax.all_gather(attend_out, "seq", axis=0, tiled=True),
            lax.all_gather(feed_gate, "seq", axis=0, tiled=True),
            lax.all_gather(feed_up, "seq", axis=0, tiled=True),
            lax.all_gather(feed_down, "seq", axis=0, tiled=True),
        )

    def conv_of(extended, kernel):
        return conv_silu(extended, kernel, segment_ext)

    def summary_of(values_in, writes_in, steps_in, rates_in):
        return block_summary(values_in, writes_in, steps_in, rates_in, segment_rows, segment_prev)

    def output_of(values_in, writes_in, reads_in, steps_in, rates_in, skips_in, state_value):
        return block_output(
            values_in,
            writes_in,
            reads_in,
            steps_in,
            rates_in,
            skips_in,
            state_value,
            segment_rows,
            segment_prev,
        )

    full_patch_in, full_gate, full_input, full_state, full_step, full_mixout, full_patchout = (
        fetch_global()
    )
    patches = byte_input.reshape(BLOCK, PATCH * E)
    local_bytes = lax.dynamic_slice_in_dim(patches, slot_start, slot_width, 1)
    hidden = over_heads(product(local_bytes, full_patch_in))
    normed = rms_scale(hidden, gain_global).astype(jnp.bfloat16)
    gate_pre = product(normed, full_gate)
    input_pre = product(normed, full_input)
    state_pre = product(normed, full_state)
    step_pre = product(normed, full_step)
    rim_rows = shifted((input_pre[BLOCK - KCONV + 1 :], state_pre[BLOCK - KCONV + 1 :]), "seq", 1)
    input_ext = jnp.concatenate([rim_rows[0], input_pre], axis=0)
    state_ext = jnp.concatenate([rim_rows[1], state_pre], axis=0)
    input_conv = conv_of(input_ext, conv_input)
    state_conv = conv_of(state_ext, conv_state)
    step_size = jax.nn.softplus(step_pre + step_bias)
    head_count = step_size.shape[1]
    head_values = input_conv.reshape(BLOCK, head_count, HDIM)
    write_vecs = state_conv[:, :NSTATE]
    read_vecs = state_conv[:, NSTATE:]
    decay_total, state_local = summary_of(head_values, write_vecs, step_size, decay_log)
    identity = (jnp.ones_like(decay_total), jnp.zeros_like(state_local))
    state_in = prefix((decay_total, state_local), "seq", combine_state, identity)[1]
    mixer_rows = output_of(
        head_values, write_vecs, read_vecs, step_size, decay_log, skip_gain, state_in
    )
    gate_sigm = jax.nn.sigmoid(gate_pre)
    gate_silu = gate_pre * gate_sigm
    gated = mixer_rows * gate_silu
    mean_square = over_heads(jnp.sum(gated * gated, axis=-1, keepdims=True)) / DI
    root_inverse = lax.rsqrt(mean_square + EPS)
    mixed = (gated * root_inverse * gain_mixer).astype(jnp.bfloat16)
    merged = hidden + over_heads(product(mixed, full_mixout))
    merged_low = merged.astype(jnp.bfloat16)
    slot_values = gather_slots(product(merged_low, full_patchout)).reshape(TOK_DEV, E)
    residual = byte_input.astype(jnp.float32) + slot_values
    full_query, full_key, full_value, full_attout, full_feedgate, full_up, full_down = fetch_local()
    attend_in = rms_scale(residual, gain_attend).astype(jnp.bfloat16)
    queries = product(attend_in, full_query)
    keys_all = product(attend_in, full_key)
    values_all = product(attend_in, full_value)
    context = patch_attention(queries, keys_all, values_all).astype(jnp.bfloat16)
    middle = residual + over_heads(product(context, full_attout))
    feed_in = rms_scale(middle, gain_feed).astype(jnp.bfloat16)
    gate_value = product(feed_in, full_feedgate)
    up_value = product(feed_in, full_up)
    gate_sig = jax.nn.sigmoid(gate_value)
    hidden_units = (gate_value * gate_sig * up_value).astype(jnp.bfloat16)
    byte_output = middle + over_heads(product(hidden_units, full_down))
    full_query, full_key, full_value, full_attout, full_feedgate, full_up, full_down = fetch_local()
    out_low = cotangent.astype(jnp.bfloat16)
    grad_feed_down = product_left(hidden_units, out_low)
    grad_units = product_right(out_low, full_down)
    grad_gate_value = (
        grad_units * up_value * gate_sig * (1.0 + gate_value * (1.0 - gate_sig))
    ).astype(jnp.bfloat16)
    grad_up_value = (grad_units * gate_value * gate_sig).astype(jnp.bfloat16)
    grad_feed_gate = product_left(feed_in, grad_gate_value)
    grad_feed_up = product_left(feed_in, grad_up_value)
    grad_feed_in = over_heads(
        product_right(grad_gate_value, full_feedgate) + product_right(grad_up_value, full_up)
    )
    grad_middle_part, grad_gain_feed = rms_back(middle, gain_feed, grad_feed_in)
    grad_middle = cotangent + grad_middle_part
    middle_low = grad_middle.astype(jnp.bfloat16)
    grad_attend_out = product_left(context, middle_low)
    grad_context = product_right(middle_low, full_attout)
    attention_pull = jax.vjp(patch_attention, queries, keys_all, values_all)[1]
    grad_query_raw, grad_key_raw, grad_value_raw = attention_pull(grad_context)
    grad_query_rows = grad_query_raw.astype(jnp.bfloat16)
    grad_key_rows = grad_key_raw.astype(jnp.bfloat16)
    grad_value_rows = grad_value_raw.astype(jnp.bfloat16)
    grad_attend_query = product_left(attend_in, grad_query_rows)
    grad_attend_key = product_left(attend_in, grad_key_rows)
    grad_attend_value = product_left(attend_in, grad_value_rows)
    grad_attend_in = over_heads(
        product_right(grad_query_rows, full_query)
        + product_right(grad_key_rows, full_key)
        + product_right(grad_value_rows, full_value)
    )
    grad_residual_part, grad_gain_attend = rms_back(residual, gain_attend, grad_attend_in)
    grad_residual = grad_middle + grad_residual_part
    local_sums = (
        lax.psum_scatter(grad_attend_query, "seq", scatter_dimension=0, tiled=True),
        lax.psum_scatter(grad_attend_key, "seq", scatter_dimension=0, tiled=True),
        lax.psum_scatter(grad_attend_value, "seq", scatter_dimension=0, tiled=True),
        lax.psum_scatter(grad_attend_out, "seq", scatter_dimension=0, tiled=True),
        lax.psum_scatter(grad_feed_gate, "seq", scatter_dimension=0, tiled=True),
        lax.psum_scatter(grad_feed_up, "seq", scatter_dimension=0, tiled=True),
        lax.psum_scatter(grad_feed_down, "seq", scatter_dimension=0, tiled=True),
    )
    full_patch_in, full_gate, full_input, full_state, full_step, full_mixout, full_patchout = (
        fetch_global()
    )
    residual_patches = grad_residual.reshape(BLOCK, PATCH * E)
    slot_grad = lax.dynamic_slice_in_dim(residual_patches, slot_start, slot_width, 1).astype(
        jnp.bfloat16
    )
    grad_patch_out = product_left(merged_low, slot_grad)
    grad_merged = over_heads(product_right(slot_grad, full_patchout))
    merged_grad_low = grad_merged.astype(jnp.bfloat16)
    grad_mixer_out = product_left(mixed, merged_grad_low)
    grad_mixed = product_right(merged_grad_low, full_mixout)
    grad_gain_mixer = jnp.sum(grad_mixed * gated * root_inverse, axis=0)
    scaled_grad = grad_mixed * gain_mixer
    inner_dot = over_heads(jnp.sum(scaled_grad * gated, axis=-1, keepdims=True))
    grad_gated = scaled_grad * root_inverse - gated * inner_dot * root_inverse**3 / DI
    grad_mixer_rows = grad_gated * gate_silu
    grad_gate_pre = grad_gated * mixer_rows * gate_sigm * (1.0 + gate_pre * (1.0 - gate_sigm))
    output_pull = jax.vjp(
        output_of, head_values, write_vecs, read_vecs, step_size, decay_log, skip_gain, state_in
    )[1]
    (
        grad_values_a,
        grad_writes_a,
        grad_reads,
        grad_steps_a,
        grad_rates_a,
        grad_skip_gain,
        grad_state_in,
    ) = output_pull(grad_mixer_rows)
    state_end = carried_in((decay_total, grad_state_in), "seq", combine_state, identity)[1]
    summary_pull = jax.vjp(summary_of, head_values, write_vecs, step_size, decay_log)[1]
    grad_values_b, grad_writes_b, grad_steps_b, grad_rates_b = summary_pull(
        (jnp.sum(state_end * state_in, axis=(1, 2)), state_end)
    )
    grad_input_conv = (grad_values_a + grad_values_b).reshape(BLOCK, -1)
    grad_state_conv = over_heads(
        jnp.concatenate([grad_writes_a + grad_writes_b, grad_reads], axis=1)
    )
    grad_step_pre = (grad_steps_a + grad_steps_b) * jax.nn.sigmoid(step_pre + step_bias)
    grad_step_bias = jnp.sum(grad_step_pre, axis=0)
    grad_decay_log = grad_rates_a + grad_rates_b
    grad_input_ext, grad_conv_input = jax.vjp(conv_of, input_ext, conv_input)[1](grad_input_conv)
    grad_state_ext, grad_conv_state = jax.vjp(conv_of, state_ext, conv_state)[1](grad_state_conv)
    rim_back = shifted((grad_input_ext[: KCONV - 1], grad_state_ext[: KCONV - 1]), "seq", -1)
    grad_input_low = add_tail(grad_input_ext[KCONV - 1 :], rim_back[0]).astype(jnp.bfloat16)
    grad_state_low = add_tail(grad_state_ext[KCONV - 1 :], rim_back[1]).astype(jnp.bfloat16)
    grad_gate_low = grad_gate_pre.astype(jnp.bfloat16)
    grad_step_low = grad_step_pre.astype(jnp.bfloat16)
    grad_mixer_gate = product_left(normed, grad_gate_low)
    grad_mixer_input = product_left(normed, grad_input_low)
    grad_mixer_state = product_left(normed, grad_state_low)
    grad_mixer_step = product_left(normed, grad_step_low)
    head_part = over_heads(
        product_right(grad_gate_low, full_gate)
        + product_right(grad_input_low, full_input)
        + product_right(grad_step_low, full_step)
    )
    grad_normed = head_part + product_right(grad_state_low, full_state)
    grad_hidden_part, grad_gain_global = rms_back(hidden, gain_global, grad_normed)
    hidden_grad_low = (grad_merged + grad_hidden_part).astype(jnp.bfloat16)
    grad_patch_in = product_left(local_bytes, hidden_grad_low)
    grad_byte_part = gather_slots(product_right(hidden_grad_low, full_patch_in)).reshape(TOK_DEV, E)
    grad_input = (grad_residual + grad_byte_part).astype(jnp.bfloat16)
    global_sums = (
        lax.psum_scatter(grad_patch_in, "seq", scatter_dimension=0, tiled=True),
        lax.psum_scatter(grad_mixer_gate, "seq", scatter_dimension=0, tiled=True),
        lax.psum_scatter(grad_mixer_input, "seq", scatter_dimension=0, tiled=True),
        lax.psum_scatter(grad_mixer_state, "seq", scatter_dimension=0, tiled=True),
        lax.psum_scatter(grad_mixer_step, "seq", scatter_dimension=0, tiled=True),
        lax.psum_scatter(grad_mixer_out, "seq", scatter_dimension=0, tiled=True),
        lax.psum_scatter(grad_patch_out, "seq", scatter_dimension=0, tiled=True),
    )
    small_sums = lax.psum(
        (
            grad_gain_global,
            grad_conv_input,
            grad_conv_state,
            grad_step_bias,
            grad_decay_log,
            grad_skip_gain,
            grad_gain_mixer,
            grad_gain_attend,
            grad_gain_feed,
        ),
        "seq",
    )
    return (
        byte_output.astype(jnp.bfloat16),
        grad_input,
        small_sums[0],
        global_sums[0],
        global_sums[1],
        global_sums[2],
        global_sums[3],
        global_sums[4],
        small_sums[1],
        small_sums[2],
        small_sums[3],
        small_sums[4],
        small_sums[5],
        small_sums[6],
        global_sums[5],
        global_sums[6],
        small_sums[7],
        local_sums[0],
        local_sums[1],
        local_sums[2],
        local_sums[3],
        small_sums[8],
        local_sums[4],
        local_sums[5],
        local_sums[6],
    )


ROWS = 512
HALF = 256
HEADS_STEP = 8
WIDTH = HEADS_STEP * HDIM
STEPS = 8 // HEADS_STEP
VMEM_BYTES = 56 * 1024 * 1024


def bf(values):
    return values.astype(jnp.bfloat16)


def up(values):
    return values.astype(jnp.float32)


def whole(shape):
    return pl.BlockSpec(shape, lambda *_: (0,) * len(shape))


def scalars():
    return pl.BlockSpec(memory_space=pltpu.SMEM)


def kernel_params(limit=VMEM_BYTES):
    return pltpu.CompilerParams(vmem_limit_bytes=limit, dimension_semantics=("arbitrary",))


def cost(flops, size):
    return pl.CostEstimate(flops=flops, bytes_accessed=size, transcendentals=0)


def block_index(place, k):
    c, y = (place[0], place[1])
    c = 1 - c if k >= 2 else c
    y = 1 - y if k % 2 else y
    return c * 2 + y


def put_pieces(place, pieces, out_ref, rows=128):
    for k, piece in enumerate(pieces):
        at = pl.multiple_of(block_index(place, k) * rows, rows)
        out_ref[pl.ds(at, rows), :] = piece[:rows, :]


def lane_of(values, lane):
    lanes = lax.broadcasted_iota(jnp.int32, values.shape, 1)
    return jnp.sum(jnp.where(lanes == lane, values, 0.0), axis=1, keepdims=True)


def segments(lengths, shift, shape, axis):
    rows = lax.broadcasted_iota(jnp.int32, shape, axis) - shift
    total = jnp.zeros(shape, jnp.int32)
    bound = 0
    for k in range(lengths.shape[0] - 1):
        bound = bound + lengths[k]
        total = total + (rows >= bound).astype(jnp.int32)
    return total


def tap_masks(lengths):
    here = segments(lengths, 0, (ROWS, 1), 0)
    rows = lax.broadcasted_iota(jnp.int32, (ROWS, 1), 0)
    return [
        up((rows >= j) & (segments(lengths, j, (ROWS, 1), 0) == here))
        for j in range(1, KCONV)
    ]


def conv_rows(values, taps, masks):
    total = values * taps[KCONV - 1 : KCONV, :]
    for j in range(1, KCONV):
        earlier = pltpu.roll(values, j, 0) * masks[j - 1]
        total = total + earlier * taps[KCONV - 1 - j : KCONV - j, :]
    return total


def conv_back(values, taps, masks, grads):
    rows_grad = grads * taps[KCONV - 1 : KCONV, :]
    taps_grad = [None] * KCONV
    taps_grad[KCONV - 1] = jnp.sum(grads * values, axis=0, keepdims=True)
    for j in range(1, KCONV):
        masked = grads * masks[j - 1]
        rows_grad = rows_grad + pltpu.roll(masked, ROWS - j, 0) * taps[
            KCONV - 1 - j : KCONV - j, :
        ]
        taps_grad[KCONV - 1 - j] = jnp.sum(
            masked * pltpu.roll(values, j, 0), axis=0, keepdims=True
        )
    return rows_grad, taps_grad


def silu_parts(values):
    gate = 1.0 / (1.0 + jnp.exp(-values))
    return values * gate, gate * (1.0 + values * (1.0 - gate))


def softplus(values):
    return jnp.maximum(values, 0.0) + jnp.log1p(jnp.exp(-jnp.abs(values)))


def three_parts(values):
    first = bf(values)
    rest = values - up(first)
    second = bf(rest)
    return first, second, bf(rest - up(second))


def sums_left(ones, values):
    first, second, third = (product(ones, part) for part in three_parts(values))
    return (third + second) + first


def sums_right(values, ones):
    first, second, third = (product(part, ones) for part in three_parts(values))
    return (third + second) + first


def lower(shape, flip=False):
    rows = lax.broadcasted_iota(jnp.int32, shape, 0)
    columns = lax.broadcasted_iota(jnp.int32, shape, 1)
    return bf(up(rows <= columns) if flip else up(rows >= columns))


def allowed_pairs(lengths):
    rows = lax.broadcasted_iota(jnp.int32, (ROWS, ROWS), 0)
    columns = lax.broadcasted_iota(jnp.int32, (ROWS, ROWS), 1)
    same = segments(lengths, 0, (ROWS, 1), 0) == segments(lengths, 0, (1, ROWS), 1)
    return (rows >= columns) & same


def decay_block(run, run_row):
    return jnp.exp(jnp.minimum(run - run_row, 0.0))


def head_columns(j, i, table):
    return lane_of(table, HEADS_STEP * j + i)


def by_head(parts):
    lanes = lax.broadcasted_iota(jnp.int32, (1, WIDTH), 1)
    value = parts[-1]
    for i in range(len(parts) - 2, -1, -1):
        value = jnp.where(lanes < (i + 1) * HDIM, parts[i], value)
    return value


def wide(mask):
    return jnp.concatenate([mask] * (WIDTH // 128), axis=1)


def shared_setup(
    j, lengths, pre_ref, state_taps, params, affinity, step_ref, run_ref, run_t, wr_ref, mask_ref
):
    @pl.when(j == 0)
    def _():
        step = softplus(pre_ref[:, 256:] + params[0:1, :])
        step_ref[...] = step
        running = sums_left(lower((ROWS, ROWS)), -step * jnp.exp(params[1:2, :]))
        run_ref[...] = running
        run_t[...] = running.T
        masks = [jnp.broadcast_to(mask, (ROWS, 128)) for mask in tap_masks(lengths)]
        for k in range(KCONV - 1):
            mask_ref[k] = masks[k]
        masks = [jnp.concatenate([mask, mask], axis=1) for mask in masks]
        state = silu_parts(conv_rows(pre_ref[:, :256], state_taps[...], masks))[0]
        wr_ref[...] = bf(state)
        pairs = product_right(bf(state[:, NSTATE:]), bf(state[:, :NSTATE]))
        affinity[...] = jnp.where(allowed_pairs(lengths), pairs, 0.0)


def weight_copies(place, pieces, weights, arrived):
    copies = []
    for v, piece in enumerate(pieces):
        at = pl.multiple_of(place[3 + v] * 128 + (64 if v == 8 else 0), 64)
        target = weights.at[pl.ds(at, piece.shape[0]), :]
        copies.append(pltpu.make_async_copy(piece, target, arrived.at[v]))
    return copies


def start_weights(place, pieces, weights, arrived):
    copies = weight_copies(place, pieces, weights, arrived)
    for copy in copies:
        copy.start()
    return copies


def put_mix_out(parts, mix_out):
    for s in range(8):
        rows = slice(s * HDIM, (s + 1) * HDIM)
        mix_out[rows, :512] = parts[s * 128 : s * 128 + 64, :]
        mix_out[rows, 512:] = parts[s * 128 + 64 : (s + 1) * 128, :]


def mixer_forward_kernel(
    place, lengths, p0, p1, p2, p3, table, state_taps, params, w0, w1, w2, w3, w4, w5, w6, w7, w8,
    send, keep, own_normed, gate_pre, input_pre, rest_pre, inside, scaled,
    normed, pre, all_scaled, affinity, step_ref, run_ref, run_t, wr_ref, mask_ref, squares,
    mix_out, weights, arrived, rest_sent,
):
    j = pl.program_id(0)
    rest_copy = pltpu.make_async_copy(pre.at[:, 1024:], rest_pre, rest_sent)

    @pl.when(j == 0)
    def _():
        pieces = (w0, w1, w2, w3, w4, w5, w6, w7, w8)
        copies = start_weights(place, [p.at[:, :1920] for p in pieces], weights, arrived)
        put_pieces(place, (p0, p1, p2, p3), normed)
        own = pl.ds(pl.multiple_of(place[2] * 128, 128), 128)
        own_normed[...] = normed[:, own]
        squares[...] = jnp.zeros_like(squares)
        for copy in copies:
            copy.wait()
        pre[...] = product(normed[...], weights[:, :1408])
        put_mix_out(weights.at[:, 1408:], mix_out)
        rest_copy.start()

    shared_setup(
        j, lengths, pre.at[:, 1024:], state_taps, params, affinity, step_ref, run_ref, run_t,
        wr_ref, mask_ref,
    )
    columns = pl.ds(pl.multiple_of(j * WIDTH, WIDTH), WIDTH)
    masks = [wide(mask_ref[k]) for k in range(KCONV - 1)]
    before = pre[:, pl.ds(pl.multiple_of(512 + j * WIDTH, WIDTH), WIDTH)]
    input_pre[...] = before
    values = silu_parts(conv_rows(before, table[:, columns], masks))[0]
    step = by_head([head_columns(j, i, step_ref[...]) for i in range(HEADS_STEP)])
    steps = bf(values * step)
    inner = []
    for r in range(2):
        seen = (r + 1) * HALF
        pairs = affinity[r * HALF : seen, :seen]
        parts = []
        for i in range(HEADS_STEP):
            run = head_columns(j, i, run_ref[r * HALF : seen, :])
            run_row = run_t[pl.ds(HEADS_STEP * j + i, 1), :seen]
            mixing = bf(pairs * decay_block(run, run_row))
            parts.append(product(mixing, steps[:seen, i * HDIM : (i + 1) * HDIM]))
        inner.append(jnp.concatenate(parts, axis=1))
    inner = jnp.concatenate(inner, axis=0)
    inside[...] = inner
    skip = by_head([head_columns(j, i, params[2:3, :]) for i in range(HEADS_STEP)])
    gate = pre[:, columns]
    gate_pre[...] = gate
    gated = (inner + skip * values) * silu_parts(gate)[0]
    low = bf(gated * table[4:5, columns])
    all_scaled[:, columns] = low
    scaled[...] = low
    squares[...] += jnp.broadcast_to(jnp.sum(gated * gated, axis=1, keepdims=True), (ROWS, 128))

    @pl.when(j == STEPS - 1)
    def _():
        for out, half in ((send, 1 - place[0]), (keep, place[0])):
            at = pl.ds(pl.multiple_of(half * HALF, HALF), HALF)
            out[:, :1024] = bf(product(all_scaled[at, :], mix_out[...]))
            out[:, 1024:] = bf(squares[at, :])
        rest_copy.wait()


def by_columns():
    return pl.BlockSpec((ROWS, WIDTH), lambda j: (0, j))


def mixer_forward(place, lengths, pieces, weights, table, state_taps, params):
    f32, low = (jnp.float32, jnp.bfloat16)
    shapes = [
        ((HALF, 1152), low, whole((HALF, 1152))),
        ((HALF, 1152), low, whole((HALF, 1152))),
        ((ROWS, 128), low, whole((ROWS, 128))),
        ((ROWS, 512), f32, by_columns()),
        ((ROWS, 512), f32, by_columns()),
        ((ROWS, 384), f32, pl.BlockSpec(memory_space=pl.ANY)),
        ((ROWS, 512), f32, by_columns()),
        ((ROWS, 512), low, by_columns()),
    ]
    return pl.pallas_call(
        mixer_forward_kernel,
        grid=(STEPS,),
        in_specs=[scalars(), scalars()]
        + [whole(a.shape) for a in (*pieces, table, state_taps, params)]
        + [pl.BlockSpec(memory_space=pl.ANY)] * 9,
        out_specs=[spec for _, _, spec in shapes],
        out_shape=[jax.ShapeDtypeStruct(s, t) for s, t, _ in shapes],
        scratch_shapes=[
            pltpu.VMEM((ROWS, 1024), low),
            pltpu.VMEM((ROWS, 1408), f32),
            pltpu.VMEM((ROWS, 512), low),
            pltpu.VMEM((ROWS, ROWS), f32),
            pltpu.VMEM((ROWS, 128), f32),
            pltpu.VMEM((ROWS, 128), f32),
            pltpu.VMEM((128, ROWS), f32),
            pltpu.VMEM((ROWS, 256), low),
            pltpu.VMEM((KCONV - 1, ROWS, 128), f32),
            pltpu.VMEM((ROWS, 128), f32),
            pltpu.VMEM((512, 1024), low),
            pltpu.VMEM((1024, 1920), low),
            pltpu.SemaphoreType.DMA((9,)),
            pltpu.SemaphoreType.DMA,
        ],
        compiler_params=kernel_params(),
        cost_estimate=cost(1_000_000, 10_000),
        name="mixer_forward",
    )(place, lengths, *pieces, table, state_taps, params, *weights)


def mixer_backward_kernel(
    place, lengths, g0, g1, g2, g3, table, state_taps, params, gate_pre, input_pre, rest_pre, inside,
    w0, w1, w2, w3, w4, w5, w6, w7, w8,
    send, keep, grads, merged, table_grad, state_taps_grad, params_grad,
    grad_mixed, kappa, affinity, step_ref, run_ref, run_t, wr_ref, mask_ref, pair_grad, run_grad,
    step_grad, out_parts, mix_out, weights, out_arrived, arrived,
):
    j = pl.program_id(0)
    pieces = (w0, w1, w2, w3, w4, w5, w6, w7, w8)
    first_copies = weight_copies(place, [p.at[:, :1408] for p in pieces], weights, arrived)

    @pl.when(j == 0)
    def _():
        copies = weight_copies(place, [p.at[:, 1408:1920] for p in pieces], out_parts, out_arrived)
        for copy in copies + first_copies:
            copy.start()
        for copy in copies:
            copy.wait()

    shared_setup(
        j, lengths, rest_pre, state_taps, params, affinity, step_ref, run_ref, run_t, wr_ref, mask_ref
    )

    @pl.when(j == 0)
    def _():
        for k, piece in enumerate((g0, g1, g2, g3)):
            at = pl.ds(pl.multiple_of(block_index(place, k) * 128, 128), 128)
            merged[at, :] = piece[:128, :1024]
            kappa[at, :] = up(piece[:128, 1024:])
        put_mix_out(out_parts, mix_out)
        grad_mixed[...] = product_right(merged[...], mix_out[...])
        pair_grad[...] = jnp.zeros_like(pair_grad)
        run_grad[...] = jnp.zeros_like(run_grad)
        step_grad[...] = jnp.zeros_like(step_grad)
        params_grad[...] = jnp.zeros_like(params_grad)
        table_grad[...] = jnp.zeros_like(table_grad)
        state_taps_grad[...] = jnp.zeros_like(state_taps_grad)

    columns = pl.ds(pl.multiple_of(j * WIDTH, WIDTH), WIDTH)
    columns_in = pl.ds(pl.multiple_of(512 + j * WIDTH, WIDTH), WIDTH)
    masks = [wide(mask_ref[k]) for k in range(KCONV - 1)]
    taps = table[:, columns]
    before = input_pre[...]
    values, values_slope = silu_parts(conv_rows(before, taps, masks))
    step = by_head([head_columns(j, i, step_ref[...]) for i in range(HEADS_STEP)])
    skip = by_head([head_columns(j, i, params[2:3, :]) for i in range(HEADS_STEP)])
    steps = bf(values * step)
    gate, gate_slope = silu_parts(gate_pre[...])
    within = inside[...]
    rows = within + skip * values
    gated = rows * gate
    mixed_grad = grad_mixed[:, columns]
    gain_grad = jnp.sum(mixed_grad * gated, axis=0, keepdims=True)
    gated_grad = mixed_grad * table[4:5, columns] - gated * wide(kappa[...])
    grads[:, columns] = bf(gated_grad * rows * gate_slope)
    rows_grad = gated_grad * gate
    rows_low = bf(rows_grad)
    rows_turned = rows_low.T
    steps_grads = []
    for i in range(HEADS_STEP):
        run = head_columns(j, i, run_ref[...])
        run_row = run_t[pl.ds(HEADS_STEP * j + i, 1), :]
        lanes = slice(i * HDIM, (i + 1) * HDIM)
        turned = jnp.zeros((HDIM, ROWS), jnp.float32)
        for r in range(2):
            seen = (r + 1) * HALF
            block = slice(r * HALF, seen)
            decay = decay_block(run[block, :], run_row[:, :seen])
            mixing = bf(affinity[block, :seen] * decay)
            mixing_grad = product_right(rows_low[block, lanes], steps[:seen, lanes])
            pair_grad[block, :seen] += mixing_grad * decay
            part = product(rows_turned[lanes, block], mixing)
            if seen < ROWS:
                part = jnp.concatenate(
                    [part, jnp.zeros((HDIM, ROWS - seen), jnp.float32)], axis=1
                )
            turned = turned + part
        steps_grads.append(turned)
    steps_grad = jnp.concatenate(steps_grads, axis=0).T
    lanes_in = lax.broadcasted_iota(jnp.int32, (WIDTH, 128), 0)
    lanes_out = lax.broadcasted_iota(jnp.int32, (WIDTH, 128), 1)
    to_head = bf(up(lanes_out == HEADS_STEP * j + lanes_in // HDIM))
    run_grad[...] += sums_right(up(rows_low) * within - up(steps) * steps_grad, to_head)
    step_grad[...] += sums_right(steps_grad * values, to_head)
    skip_sums = jnp.sum(rows_grad * values, axis=0, keepdims=True)
    params_grad[2:3, :] += sums_right(jnp.broadcast_to(skip_sums, (8, WIDTH)), to_head)[:1, :]
    conv_grad = (steps_grad * step + skip * rows_grad) * values_slope
    before_grad, taps_grad = conv_back(before, taps, masks, conv_grad)
    grads[:, columns_in] = bf(before_grad)
    for k in range(KCONV):
        table_grad[k : k + 1, columns] = taps_grad[k]
    table_grad[4:5, columns] = gain_grad

    @pl.when(j == STEPS - 1)
    def _():
        decay_grad = sums_left(lower((ROWS, ROWS), True), run_grad[...])
        rate = jnp.exp(params[1:2, :])
        step_total = step_grad[...] - decay_grad * rate
        slope = 1.0 / (1.0 + jnp.exp(-(rest_pre[:, 256:] + params[0:1, :])))
        lanes = lax.broadcasted_iota(jnp.int32, (1, 128), 1)
        step_total = jnp.where(lanes < 8, step_total * slope, 0.0)
        grads[:, 1280:] = bf(step_total)
        params_grad[0:1, :] = jnp.sum(step_total, axis=0, keepdims=True)
        params_grad[1:2, :] = jnp.sum(
            -decay_grad * step_ref[...] * rate, axis=0, keepdims=True
        )
        pairs = jnp.where(allowed_pairs(lengths), pair_grad[...], 0.0)
        read_grad = product(bf(pairs), wr_ref[:, :NSTATE])
        write_grad = product(bf(pairs.T), wr_ref[:, NSTATE:])
        state_masks = [
            jnp.concatenate([mask_ref[k], mask_ref[k]], axis=1) for k in range(KCONV - 1)
        ]
        state_before = rest_pre[:, :256]
        state_slope = silu_parts(conv_rows(state_before, state_taps[...], state_masks))[1]
        state_grad, state_taps_parts = conv_back(
            state_before,
            state_taps[...],
            state_masks,
            jnp.concatenate([write_grad, read_grad], axis=1) * state_slope,
        )
        grads[:, 1024:1280] = bf(state_grad)
        for k in range(KCONV):
            state_taps_grad[k : k + 1, :] = state_taps_parts[k]
        for copy in first_copies:
            copy.wait()
        for out, half in ((send, 1 - place[0]), (keep, place[0])):
            at = pl.ds(pl.multiple_of(half * HALF, HALF), HALF)
            out[:, :1024] = bf(product_right(grads[at, :], weights[...]))
            out[:, 1024:] = grads[at, 1024:1280]


def mixer_backward(place, lengths, pieces, weights, table, state_taps, params, pre, inside):
    gate_pre, input_pre, rest_pre = pre
    f32, low = (jnp.float32, jnp.bfloat16)
    shapes = [
        ((HALF, 1280), low),
        ((HALF, 1280), low),
        ((ROWS, 1408), low),
        ((ROWS, 1024), low),
        ((8, 512), f32),
        ((8, 256), f32),
        ((8, 128), f32),
    ]
    operands = (*pieces, table, state_taps, params)
    return pl.pallas_call(
        mixer_backward_kernel,
        grid=(STEPS,),
        in_specs=[scalars(), scalars()]
        + [whole(a.shape) for a in operands]
        + [by_columns(), by_columns(), whole(rest_pre.shape), by_columns()]
        + [pl.BlockSpec(memory_space=pl.ANY)] * 9,
        out_specs=[whole(s) for s, _ in shapes],
        out_shape=[jax.ShapeDtypeStruct(s, t) for s, t in shapes],
        scratch_shapes=[
            pltpu.VMEM((ROWS, 512), f32),
            pltpu.VMEM((ROWS, 128), f32),
            pltpu.VMEM((ROWS, ROWS), f32),
            pltpu.VMEM((ROWS, 128), f32),
            pltpu.VMEM((ROWS, 128), f32),
            pltpu.VMEM((128, ROWS), f32),
            pltpu.VMEM((ROWS, 256), low),
            pltpu.VMEM((KCONV - 1, ROWS, 128), f32),
            pltpu.VMEM((ROWS, ROWS), f32),
            pltpu.VMEM((ROWS, 128), f32),
            pltpu.VMEM((ROWS, 128), f32),
            pltpu.VMEM((1024, 512), low),
            pltpu.VMEM((512, 1024), low),
            pltpu.VMEM((1024, 1408), low),
            pltpu.SemaphoreType.DMA((9,)),
            pltpu.SemaphoreType.DMA((9,)),
        ],
        compiler_params=kernel_params(),
        cost_estimate=cost(1_000_000, 10_000),
        name="mixer_backward",
    )(place, lengths, *operands, gate_pre, input_pre, rest_pre, inside, *weights)


GROUP = 2


def patch_mask():
    rows = lax.broadcasted_iota(jnp.int32, (128, 128), 0)
    columns = lax.broadcasted_iota(jnp.int32, (128, 128), 1)
    return (rows >= columns) & (rows // PATCH == columns // PATCH)


def unit(values, n, i):
    start = n * 256 + (i % 4) * HDIM
    return values[(i // 4) * 128 : (i // 4 + 1) * 128, start : start + HDIM]


def stacked(parts):
    return jnp.stack(parts, axis=0)


def patch_probs(qkv, units, mask):
    scale = jnp.bfloat16(HDIM ** (-0.5))
    scores = stacked([product_right(unit(qkv, 0, i) * scale, unit(qkv, 1, i)) for i in units])
    scores = jnp.where(mask[None], scores, -1e30)
    weights = jnp.exp(scores - jnp.max(scores, axis=2, keepdims=True))
    return weights * (1.0 / jnp.sum(weights, axis=2, keepdims=True))


def split_blocks(values, keep, send):
    for k, out in ((0, keep), (1, send), (2, keep), (3, send)):
        out[k // 2] = bf(values[k * 128 : (k + 1) * 128, :])


def put_w_out(weights, w_out):
    for s in range(8):
        for q in range(4):
            at = s * 128 + q * 32
            w_out[s * 32 : (s + 1) * 32, q * 256 : (q + 1) * 256] = weights[at : at + 32, 768:]


def attend_forward_kernel(
    place, x0, x1, x2, x3, w0, w1, w2, w3, w4, w5, w6, w7, w8,
    keep, send, rows, qkv, context, w_out, weights, arrived,
):
    pieces = [p.at[:, 1920:] for p in (w0, w1, w2, w3, w4, w5, w6, w7, w8)]
    for copy in start_weights(place, pieces, weights, arrived):
        copy.wait()
    put_w_out(weights, w_out)
    for k, piece in enumerate((x0, x1, x2, x3)):
        rows[k * 128 : (k + 1) * 128, :] = piece[...]
    qkv[...] = bf(product(rows[...], weights[:, :768]))
    mask = patch_mask()
    for b in range(4 // GROUP):
        units = range(b * GROUP * 4, (b + 1) * GROUP * 4)
        probs = bf(patch_probs(qkv, units, mask))
        for n, i in enumerate(units):
            context[(i // 4) * 128 : (i // 4 + 1) * 128, (i % 4) * HDIM : (i % 4 + 1) * HDIM] = bf(
                product(probs[n], unit(qkv, 2, i))
            )
    split_blocks(product(context[...], w_out[...]), keep, send)


def attend_forward(place, pieces, weights):
    low = jnp.bfloat16
    shapes = [(2, 128, 1024), (2, 128, 1024), (ROWS, 1024), (ROWS, 768), (ROWS, 256)]
    return pl.pallas_call(
        attend_forward_kernel,
        grid=(1,),
        in_specs=[scalars()]
        + [whole(a.shape) for a in pieces]
        + [pl.BlockSpec(memory_space=pl.ANY)] * 9,
        out_specs=[whole(s) for s in shapes],
        out_shape=[jax.ShapeDtypeStruct(s, low) for s in shapes],
        compiler_params=kernel_params(),
        scratch_shapes=[
            pltpu.VMEM((256, 1024), low),
            pltpu.VMEM((1024, 1024), low),
            pltpu.SemaphoreType.DMA((9,)),
        ],
        cost_estimate=cost(1_000_000, 10_000),
        name="attend_forward",
    )(place, *pieces, *weights)


def attend_backward_kernel(
    place, g0, g1, g2, g3, qkv, w0, w1, w2, w3, w4, w5, w6, w7, w8,
    keep, send, rows, qkv_grad, w_out, weights, arrived,
):
    pieces = [p.at[:, 1920:] for p in (w0, w1, w2, w3, w4, w5, w6, w7, w8)]
    for copy in start_weights(place, pieces, weights, arrived):
        copy.wait()
    put_w_out(weights, w_out)
    for k, piece in enumerate((g0, g1, g2, g3)):
        rows[k * 128 : (k + 1) * 128, :] = piece[...]
    context_grad = product_right(rows[...], w_out[...])
    mask = patch_mask()
    for b in range(1):
        units = range(16 * b, 16 * (b + 1))
        probs = patch_probs(qkv, units, mask)
        grads = [bf(unit(context_grad, 0, i)) for i in units]
        probs_grad = stacked(
            [product_right(g, unit(qkv, 2, i)) for g, i in zip(grads, units, strict=True)]
        )
        mean = jnp.sum(probs * probs_grad, axis=2, keepdims=True)
        scores_grad = probs * (probs_grad - mean) * HDIM ** (-0.5)
        for n, i in enumerate(units):
            rows_at = slice((i // 4) * 128, (i // 4 + 1) * 128)
            for k, part in enumerate(
                (
                    product(bf(scores_grad[n]), unit(qkv, 1, i)),
                    product(bf(scores_grad[n].T), unit(qkv, 0, i)),
                    product(bf(probs[n].T), grads[n]),
                )
            ):
                start = k * 256 + (i % 4) * HDIM
                qkv_grad[rows_at, start : start + HDIM] = bf(part)
    split_blocks(product_right(qkv_grad[...], weights[:, :768]), keep, send)


def attend_backward(place, pieces, qkv, weights):
    low = jnp.bfloat16
    shapes = [(2, 128, 1024), (2, 128, 1024), (ROWS, 1024), (ROWS, 768)]
    return pl.pallas_call(
        attend_backward_kernel,
        grid=(1,),
        in_specs=[scalars()]
        + [whole(a.shape) for a in (*pieces, qkv)]
        + [pl.BlockSpec(memory_space=pl.ANY)] * 9,
        out_specs=[whole(s) for s in shapes],
        out_shape=[jax.ShapeDtypeStruct(s, low) for s in shapes],
        compiler_params=pltpu.CompilerParams(vmem_limit_bytes=VMEM_BYTES),
        scratch_shapes=[
            pltpu.VMEM((256, 1024), low),
            pltpu.VMEM((1024, 1024), low),
            pltpu.SemaphoreType.DMA((9,)),
        ],
        cost_estimate=cost(1_000_000, 10_000),
        name="attend_backward",
    )(place, *pieces, qkv, *weights)


def feed_copies(place, pieces, weights, arrived, j):
    chunk = pl.multiple_of(j * 512, 512)
    copies = []
    for n, start in enumerate((chunk, pl.multiple_of(1024 + chunk, 512))):
        at = pl.ds(start, 512)
        copies += weight_copies(
            place, [p.at[:, at] for p in pieces], weights.at[:, at], arrived.at[2 * j + n]
        )
    return copies


def down_copies(place, pieces, weights, arrived):
    return weight_copies(
        place, [p.at[:, 2048:] for p in pieces], weights.at[:, 2048:], arrived.at[4]
    )


def feed_kernel(
    place, x0, x1, x2, x3, out_grad, w0, w1, w2, w3, w4, w5, w6, w7, w8,
    keep, send, out_keep, out_send, rows, hidden, gate_grad, up_grad,
    weights, total, total_out, arrived,
):
    j = pl.program_id(0)
    pieces = (w0, w1, w2, w3, w4, w5, w6, w7, w8)

    @pl.when(j == 0)
    def _():
        for copy in feed_copies(place, pieces, weights, arrived, 0):
            copy.start()
        for copy in down_copies(place, pieces, weights, arrived):
            copy.start()
        for k in range(1, 2):
            for copy in feed_copies(place, pieces, weights, arrived, k):
                copy.start()
        for k, piece in enumerate((x0, x1, x2, x3)):
            rows[k * 128 : (k + 1) * 128, :] = piece[...]
        total[...] = jnp.zeros_like(total)
        total_out[...] = jnp.zeros_like(total_out)

    for copy in feed_copies(place, pieces, weights, arrived, j):
        copy.wait()

    @pl.when(j == 0)
    def _():
        for copy in down_copies(place, pieces, weights, arrived):
            copy.wait()

    chunk = pl.multiple_of(j * 512, 512)
    w_gate = weights[:, pl.ds(chunk, 512)]
    w_up = weights[:, pl.ds(pl.multiple_of(1024 + chunk, 512), 512)]
    w_down = weights[pl.ds(chunk, 512), 2048:]
    gate, slope = silu_parts(product(rows[...], w_gate))
    lift = product(rows[...], w_up)
    units = bf(gate * lift)
    hidden[...] = units
    units_grad = product_right(out_grad[...], w_down)
    gate_low = bf(units_grad * lift * slope)
    up_low = bf(units_grad * gate)
    gate_grad[...] = gate_low
    up_grad[...] = up_low
    total[...] += product_right(gate_low, w_gate) + product_right(up_low, w_up)
    total_out[...] += product(units, w_down)

    @pl.when(j == pl.num_programs(0) - 1)
    def _():
        split_blocks(total, keep, send)
        split_blocks(total_out, out_keep, out_send)


def feed(place, pieces, out_grad, weights):
    low = jnp.bfloat16
    pair = (2, 128, 1024)
    column = pl.BlockSpec((ROWS, 512), lambda j: (0, j))
    return pl.pallas_call(
        feed_kernel,
        grid=(2,),
        in_specs=[scalars()]
        + [whole(a.shape) for a in (*pieces, out_grad)]
        + [pl.BlockSpec(memory_space=pl.ANY)] * 9,
        out_specs=[whole(pair)] * 4 + [whole((ROWS, 1024)), column, column, column],
        out_shape=[jax.ShapeDtypeStruct(pair, low)] * 4
        + [jax.ShapeDtypeStruct((ROWS, 1024), low)] * 4,
        scratch_shapes=[
            pltpu.VMEM((1024, 3072), low),
            pltpu.VMEM((ROWS, 1024), jnp.float32),
            pltpu.VMEM((ROWS, 1024), jnp.float32),
            pltpu.SemaphoreType.DMA((5, 9)),
        ],
        compiler_params=kernel_params(),
        cost_estimate=cost(1_000_000, 10_000),
        name="feed",
    )(place, *pieces, out_grad, *weights)


def put_by_target(place, values, out):
    for s in range(8):
        out[place[12 + s], :, : values.shape[1]] = values[s * 128 : (s + 1) * 128, :]


def feed_grads_kernel(place, rows, gate_grad, up_grad, hidden, out_grad, grads, turned):
    j = pl.program_id(0)

    @pl.when(j == 0)
    def _():
        turned[...] = rows[...].T

    @pl.when(j == 4)
    def _():
        turned[...] = hidden[...].T

    columns = pl.ds(pl.multiple_of((j % 2) * 512, 512), 512)
    for first, right in ((0, gate_grad), (2, up_grad), (4, out_grad)):

        @pl.when((j >= first) & (j < first + 2))
        def _():
            put_by_target(place, bf(product(turned[...], right[:, columns])), grads)


def feed_grads(place, rows, gate_grad, up_grad, hidden, out_grad):
    low = jnp.bfloat16
    return pl.pallas_call(
        feed_grads_kernel,
        grid=(6,),
        in_specs=[scalars()] + [whole((ROWS, 1024))] * 5,
        out_specs=pl.BlockSpec((8, 128, 512), lambda j: (0, 0, j)),
        out_shape=jax.ShapeDtypeStruct((8, 128, 3072), low),
        scratch_shapes=[pltpu.VMEM((1024, ROWS), low)],
        compiler_params=kernel_params(),
        cost_estimate=cost(1_000_000, 10_000),
        name="feed_grads",
    )(place, rows, gate_grad, up_grad, hidden, out_grad)


def attend_grads_kernel(place, rows, qkv_grad, context, middle_grad, grads):
    put_by_target(place, bf(product(rows[...].T, qkv_grad[...])), grads)
    out_grad = bf(product(context[...].T, middle_grad[...]))
    for s in range(8):
        for q in range(4):
            grads[place[12 + s], q * 32 : (q + 1) * 32, 768:] = out_grad[
                s * 32 : (s + 1) * 32, q * 256 : (q + 1) * 256
            ]


def attend_grads(place, rows, qkv_grad, context, middle_grad):
    operands = (rows, qkv_grad, context, middle_grad)
    return pl.pallas_call(
        attend_grads_kernel,
        grid=(1,),
        in_specs=[scalars()] + [whole(a.shape) for a in operands],
        out_specs=whole((8, 128, 1024)),
        out_shape=jax.ShapeDtypeStruct((8, 128, 1024), jnp.bfloat16),
        compiler_params=kernel_params(),
        cost_estimate=cost(1_000_000, 10_000),
        name="attend_grads",
    )(place, *operands)


def placed_kernel(turned, place, p0, p1, p2, p3, weights, rows, result):
    put_pieces(place, (p0, p1, p2, p3), rows)
    left = rows[:, :1024]
    result[...] = bf(product_right(left, weights[...]) if turned else product(left, weights[...]))


def placed_product(place, pieces, weights, turned):
    width = pieces[0].shape[1]
    low = jnp.bfloat16
    return pl.pallas_call(
        partial(placed_kernel, turned),
        in_specs=[scalars()] + [whole(a.shape) for a in (*pieces, weights)],
        out_specs=[whole((ROWS, width)), whole((ROWS, 256))],
        grid=(1,),
        out_shape=[
            jax.ShapeDtypeStruct((ROWS, width), low),
            jax.ShapeDtypeStruct((ROWS, 256), low),
        ],
        compiler_params=kernel_params(),
        cost_estimate=cost(1_000_000, 10_000),
        name="placed_product",
    )(place, *pieces, weights)


PAIR_C = [(i, i ^ 1) for i in range(4)]
PAIR_Y = [(i, i ^ 2) for i in range(4)]


def swap_c(shard):
    return lax.ppermute(shard, "mp", PAIR_C)


def swap_y(shard):
    return lax.ppermute(shard, "mp", PAIR_Y)


def swap_seq(shard, by):
    return lax.ppermute(shard, "seq", [(i, i ^ by) for i in range(8)])


RING = (0, 2, 4, 6, 7, 5, 3, 1)
UP = [(RING[i], RING[(i + 1) % 8]) for i in range(8)]
DOWN = [(b, a) for a, b in UP]
REACH = (0, -1, 1, -2, 2, -3, 3, 4, 4)


def swap_up(shard):
    return lax.ppermute(shard, "seq", UP)


def swap_down(shard):
    return lax.ppermute(shard, "seq", DOWN)


def chosen(index, values):
    places = jnp.arange(len(values), dtype=jnp.int32)
    return jnp.sum(jnp.where(index[..., None] == places, jnp.array(values, jnp.int32), 0), axis=-1)


def places_of(c, y, s):
    at = [RING.index(k) for k in range(8)]
    own = chosen(s, at)
    owners = chosen((own + jnp.array(REACH, jnp.int32) + 8) % 8, RING)
    ahead = (jnp.array(at, jnp.int32) - own + 8) % 8
    return jnp.concatenate([jnp.stack([c, y, s]), owners, ahead]).astype(jnp.int32)


class RingGather:
    def __init__(self, shard):
        self.pieces = [shard]
        self.flying = [shard, shard]

    def step(self):
        ahead, behind = self.flying
        if len(self.pieces) == 7:
            ahead, behind = (ahead[:64], behind[64:])
        self.flying = [swap_up(ahead), swap_down(behind)]

    def landed(self, value):
        value, self.flying = lax.optimization_barrier((value, self.flying))
        self.pieces = self.pieces + self.flying
        return value


    def held(self, value):
        value, shard = lax.optimization_barrier((value, self.pieces[0]))
        self.pieces, self.flying = ([shard], [shard, shard])
        return value


class RingSum:
    def __init__(self, blocks):
        self.blocks = blocks
        self.flying = None
        self.count = 0

    def step(self):
        if self.count == 0:
            far = self.blocks[4]
            sent = [far[:64], far[64:]]
        elif self.count == 1:
            ahead, behind = (self.blocks[3], self.blocks[5])
            sent = [
                jnp.concatenate([bf(up(ahead[:64]) + up(self.flying[0])), ahead[64:]]),
                jnp.concatenate([behind[:64], bf(up(behind[64:]) + up(self.flying[1]))]),
            ]
        else:
            sent = [
                bf(up(self.blocks[k]) + up(part))
                for k, part in zip((4 - self.count, 4 + self.count), self.flying, strict=True)
            ]
        self.flying = [swap_up(sent[0]), swap_down(sent[1])]
        self.count += 1

    def landed(self, value):
        value, self.flying = lax.optimization_barrier((value, self.flying))
        return value

    def held(self, value):
        value, self.blocks, self.flying = lax.optimization_barrier(
            (value, self.blocks, self.flying)
        )
        return value

    def result(self):
        return up(self.blocks[0]) + up(self.flying[0]) + up(self.flying[1])


def pick(stacked, index):
    return lax.dynamic_index_in_dim(stacked, index, 0, keepdims=False)


def over_seq(rows):
    return lax.all_to_all(rows, "seq", 0, 0, tiled=True)


def over_all(blocks):
    return lax.all_to_all(blocks, ("seq", "mp"), 0, 0, tiled=True)


def from_all_seq(rows):
    return over_seq(jnp.broadcast_to(rows[None], (8, *rows.shape)))


def sum_rows(send, keep, y):
    total = up(keep) + up(swap_c(send))
    parts = total.reshape(2, 128, -1)
    return pick(parts, y) + up(swap_y(bf(pick(parts, 1 - y))))


def gather_rows(rows):
    far = swap_y(rows)
    return [rows, far, swap_c(rows), swap_c(far)]


def alike(parts):
    return (parts[0] + parts[2]) + (parts[1] + parts[3])


def sum_group(partial, c, y):
    halves = bf(partial).reshape(2, HALF, -1)
    return bf(sum_rows(pick(halves, 1 - c), pick(halves, c), y))


def sum_seq(rows):
    return jnp.sum(up(over_seq(rows.reshape(8, 16, -1))), axis=0)


def gather_bytes(rows):
    far = swap_y(rows)
    return [rows, swap_c(rows), far, swap_c(far)]


def sum_bytes(keep, send):
    got = up(keep) + up(swap_c(send))
    return got[0] + up(swap_y(bf(got[1])))


def placed(parts, m):
    blocks = jnp.stack(parts)
    return jnp.concatenate([pick(blocks, m ^ k) for k in range(4)], axis=0)


def to_bytes(columns):
    got = over_all(columns.reshape(32, 16, 256))
    return got.reshape(8, 4, 16, 256).transpose(2, 1, 0, 3).reshape(128, E)


def to_columns(rows):
    sent = rows.reshape(16, 4, 8, 256).transpose(2, 1, 0, 3).reshape(32, 16, 256)
    return over_all(sent).reshape(ROWS, 256)


def split_plan(
    byte_input,
    seq_lengths,
    cotangent,
    gain_global,
    patch_in,
    mixer_gate,
    mixer_input,
    mixer_state,
    mixer_step,
    conv_input,
    conv_state,
    step_bias,
    decay_log,
    skip_gain,
    gain_mixer,
    mixer_out,
    patch_out,
    gain_attend,
    attend_query,
    attend_key,
    attend_value,
    attend_out,
    gain_feed,
    feed_gate,
    feed_up,
    feed_down,
):
    s, m = (lax.axis_index("seq"), lax.axis_index("mp"))
    y, c = (m // 2, m % 2)
    place = places_of(c, y, s)
    f32 = jnp.float32

    out_halves = mixer_out.reshape(64, 2, 512).transpose(1, 0, 2).reshape(128, 512)
    out_quarters = attend_out.reshape(32, 4, 256).transpose(1, 0, 2).reshape(128, 256)
    w_mixer = RingGather(jnp.concatenate(
        [
            mixer_gate,
            mixer_input,
            mixer_state,
            mixer_step,
            jnp.zeros((128, 120), jnp.bfloat16),
            out_halves,
            attend_query,
            attend_key,
            attend_value,
            out_quarters,
        ],
        axis=1,
    ))
    w_mixer.step()
    table = jnp.concatenate([conv_input, gain_mixer[None], jnp.zeros((3, 512), f32)], axis=0)
    state_taps = jnp.concatenate([conv_state, jnp.zeros((4, 256), f32)], axis=0)
    params = jnp.pad(jnp.stack([step_bias, decay_log, skip_gain]), ((0, 5), (0, 120)))

    own_slots = lax.dynamic_slice_in_dim(byte_input.reshape(64, PATCH, E), 2 * m, 2, 1)
    columns_in = over_seq(own_slots.reshape(64, 8, 256).transpose(1, 0, 2)).reshape(ROWS, 256)
    w_patch = patch_out.reshape(128, 8, 256).transpose(1, 0, 2)
    w_feed = jnp.concatenate([feed_gate, feed_up, feed_down], axis=1)
    columns_in, place, table, state_taps, params, w_patch, w_feed = w_mixer.landed(
        (columns_in, place, table, state_taps, params, w_patch, w_feed)
    )
    w_feed = RingGather(w_feed)
    w_mixer.step()
    rows = sum_group(product(columns_in, patch_in), c, y)
    hidden = w_mixer.landed(bf(sum_seq(rows)))
    w_mixer.step()
    hidden = up(w_mixer.landed(from_all_seq(hidden).reshape(128, 1024)))
    w_mixer.step()
    normed_parts = w_mixer.landed(gather_rows(bf(rms_scale(hidden, gain_global))))
    normed_parts = w_feed.held(normed_parts)
    w_feed.step()

    normed_parts, w_patch = lax.optimization_barrier((normed_parts, w_patch))
    send, keep, own_normed, *pre, inside, scaled = mixer_forward(
        place, seq_lengths, normed_parts, w_mixer.pieces, table, state_taps, params
    )
    send, w_patch = lax.optimization_barrier((send, over_seq(w_patch)))
    w_patch = w_patch.reshape(1024, 256)
    sums = w_feed.landed(sum_rows(send, keep, y))
    w_feed.step()
    unscaled, root = (sums[:, :1024], lax.rsqrt(sums[:, 1024:1025] / DI + EPS))
    merged_parts = gather_rows(bf(hidden + root * unscaled))
    merged_low, slots = placed_product(place, merged_parts, w_patch, False)
    cot_blocks = cotangent.reshape(4, 128, E)
    out_low = jnp.concatenate([bf(pick(cot_blocks, m ^ k)) for k in range(4)], axis=0)
    slots, out_low = w_feed.landed((to_bytes(slots), out_low))
    w_feed.step()
    residual = up(lax.dynamic_slice_in_dim(byte_input, m * 128, 128, 0)) + slots

    attend_parts = gather_bytes(bf(rms_scale(residual, gain_attend)))
    keep, send, attend_in, qkv, context = attend_forward(place, attend_parts, w_mixer.pieces)
    send = w_feed.landed(send)
    w_feed.step()
    middle = residual + sum_bytes(keep, send)
    feed_parts = w_feed.landed(gather_bytes(bf(rms_scale(middle, gain_feed))))
    cot_rows = pick(cot_blocks, m)
    keep, send, out_keep, out_send, feed_in, hidden_units, grad_gate, grad_up = feed(
        place, feed_parts, out_low, w_feed.pieces
    )
    grads = feed_grads(place, feed_in, grad_gate, grad_up, hidden_units, out_low)
    grad_feed_in, grads = lax.optimization_barrier((sum_bytes(keep, send), grads))
    feed_sums = RingSum(grads)
    feed_sums.step()
    grad_middle_part, gain_feed_part = rms_back(middle, gain_feed, grad_feed_in)
    grad_middle = cot_rows + grad_middle_part
    keep, send, middle_low, grad_qkv = attend_backward(
        place, gather_bytes(bf(grad_middle)), qkv, w_mixer.pieces
    )
    send = feed_sums.landed(send)
    feed_sums.step()
    grads = attend_grads(place, attend_in, grad_qkv, context, middle_low)
    grad_attend_in, grads = lax.optimization_barrier((sum_bytes(keep, send), grads))
    attend_sums = RingSum(grads)
    grad_residual_part, gain_attend_part = rms_back(residual, gain_attend, grad_attend_in)
    grad_residual = grad_middle + grad_residual_part

    slot_grad, out_send = lax.optimization_barrier(
        (to_columns(bf(grad_residual)), swap_c(out_send))
    )
    slot_grad = feed_sums.landed(slot_grad)
    feed_sums.step()
    grad_patch_out = bf(product_left(merged_low, slot_grad)).reshape(8, 128, 256)
    rows = sum_group(product_right(slot_grad, w_patch), c, y)
    out_parts = up(out_keep) + up(out_send)
    rows, out_far = lax.optimization_barrier((rows, bf(out_parts[1])))
    merged_rows, out_far = lax.optimization_barrier((sum_seq(rows), swap_y(out_far)))
    out_rows = bf(middle + out_parts[0] + up(out_far))
    merged_rows = feed_sums.landed(merged_rows)
    gains = jnp.stack([gain_feed_part, gain_attend_part])
    got = from_all_seq(
        bf(jnp.concatenate([merged_rows, gains, jnp.zeros((6, 1024), f32)], axis=0))
    )
    got, out_far, out_near = lax.optimization_barrier((got, swap_y(out_rows), swap_c(out_rows)))
    got = feed_sums.held(got)
    feed_sums.step()
    grad_merged = up(got[:, :16].reshape(128, 1024))
    gains = jnp.sum(up(got[:, 16:18]), axis=0)
    kappa = jnp.sum(grad_merged * unscaled, axis=1, keepdims=True) * root**3 / DI
    rows = jnp.concatenate([grad_merged * root, jnp.broadcast_to(kappa, (128, 128))], axis=1)
    merged_parts = gather_rows(
        bf(jnp.concatenate([rows, jnp.pad(gains, ((0, 6), (0, 128)))], axis=0))
    )
    merged_parts, grad_patch_out = attend_sums.held((merged_parts, grad_patch_out))
    attend_sums.step()
    out_both = swap_c(out_far)
    grad_patch_out = over_seq(grad_patch_out)
    gains = alike([up(part[128:130, :1024]) for part in merged_parts])
    send, keep, grads, merged_grad, table_grad, state_taps_grad, params_grad = mixer_backward(
        place,
        seq_lengths,
        merged_parts,
        w_mixer.pieces,
        table,
        state_taps,
        params,
        pre,
        inside,
    )
    send, grad_patch_out, out_both = feed_sums.landed((send, grad_patch_out, out_both))
    send = attend_sums.landed(send)
    attend_sums.step()
    feed_sums = feed_sums.result()
    byte_output = placed([out_rows, out_near, out_far, out_both], m)
    sums = sum_rows(send, keep, y)
    grad_hidden_part, gain_global_part = rms_back(hidden, gain_global, sums[:, :1024])
    rows = jnp.concatenate([grad_merged + grad_hidden_part, sums[:, 1024:]], axis=1)
    small = jnp.stack([gain_global_part, state_taps_grad[:4].reshape(1024)])
    hidden_parts = gather_rows(
        bf(jnp.concatenate([rows, jnp.pad(small, ((0, 6), (0, 256)))], axis=0))
    )
    hidden_parts = attend_sums.landed(hidden_parts)
    attend_sums.step()
    small = alike([up(part[128:130, :1024]) for part in hidden_parts])
    hidden_rows, back = placed_product(place, hidden_parts, patch_in, True)
    hidden_grad = hidden_rows[:, :1024]
    back, grad_patch_in, grad_mixer_state = lax.optimization_barrier(
        (
            to_bytes(back),
            product_left(columns_in, hidden_grad),
            product_left(own_normed, hidden_rows[:, 1024:]),
        )
    )
    grad_rows = attend_sums.landed(bf(grad_residual + back))
    attend_sums.step()
    grad_input = placed(gather_bytes(grad_rows), m)
    attend_sums = attend_sums.result()

    first_grad = product_left(own_normed, grads)
    own_scaled = lax.dynamic_slice_in_dim(scaled, s * HDIM, HDIM, 1)
    return (
        byte_output,
        grad_input,
        small[0],
        grad_patch_in,
        first_grad[:, :512],
        first_grad[:, 512:1024],
        grad_mixer_state,
        first_grad[:, 1280:1288],
        table_grad[:4],
        small[1].reshape(4, 256),
        params_grad[0, :8],
        params_grad[1, :8],
        params_grad[2, :8],
        table_grad[4],
        product_left(own_scaled, merged_grad),
        grad_patch_out.transpose(1, 0, 2).reshape(128, 2048).astype(f32),
        gains[1],
        attend_sums[:, :256],
        attend_sums[:, 256:512],
        attend_sums[:, 512:768],
        attend_sums[:, 768:].reshape(4, 32, 256).transpose(1, 0, 2).reshape(32, 1024),
        gains[0],
        feed_sums[:, :1024],
        feed_sums[:, 1024:2048],
        feed_sums[:, 2048:],
    )


def solution(mesh):
    in_specs = (
        P("seq", None),
        P(),
        P("seq", None),
        P(),
        P(("mp", "seq"), None),
        P("seq", "mp"),
        P("seq", "mp"),
        P("seq", None),
        P("seq", "mp"),
        P(None, "mp"),
        P(),
        P("mp"),
        P("mp"),
        P("mp"),
        P("mp"),
        P(("mp", "seq"), None),
        P("seq", "mp"),
        P(),
        P("seq", "mp"),
        P("seq", "mp"),
        P("seq", "mp"),
        P(("mp", "seq"), None),
        P(),
        P("seq", "mp"),
        P("seq", "mp"),
        P(("mp", "seq"), None),
    )
    out_specs = (
        P("seq", None),
        P("seq", None),
        P(),
        P(("mp", "seq"), None),
        P("seq", "mp"),
        P("seq", "mp"),
        P("seq", None),
        P("seq", "mp"),
        P(None, "mp"),
        P(),
        P("mp"),
        P("mp"),
        P("mp"),
        P("mp"),
        P(("mp", "seq"), None),
        P("seq", "mp"),
        P(),
        P("seq", "mp"),
        P("seq", "mp"),
        P("seq", "mp"),
        P(("mp", "seq"), None),
        P(),
        P("seq", "mp"),
        P("seq", "mp"),
        P(("mp", "seq"), None),
    )
    plan = split_plan if (mesh.shape["seq"], mesh.shape["mp"]) == (8, 4) else gathered_plan
    return jax.shard_map(plan, mesh=mesh, in_specs=in_specs, out_specs=out_specs, check_vma=False)
```

```python
from functools import partial

import jax
import jax.numpy as jnp
from jax import lax
from jax.experimental import pallas as pl
from jax.experimental.pallas import tpu as pltpu
from jax.sharding import PartitionSpec as P

E = 1024
HDIM = 64
DI = 2048
NSTATE = 128
KCONV = 4
PATCH = 8
TOK_DEV = 512
BLOCK = 64


EPS = 1e-05
HIGH = lax.Precision.HIGHEST


def shifted(shard, axis, by):
    length = lax.axis_size(axis)
    pairs = [(i, i + by) for i in range(length) if 0 <= i + by < length]
    return lax.ppermute(shard, axis, pairs)


def prefix(shard, axis, combine, identity):
    length, position = (lax.axis_size(axis), lax.axis_index(axis))
    everything = jax.tree.map(
        lambda part, kind: lax.all_gather(part.astype(kind), axis),
        shard,
        (jnp.bfloat16, jnp.bfloat16),
    )
    start = jax.tree.map(
        lambda part, zero: jnp.broadcast_to(jnp.asarray(zero, part.dtype), part.shape),
        shard,
        identity,
    )

    def prefix_turn(k, before):
        reached = k < position
        new = combine(
            before, jax.tree.map(lambda part, own: part[k].astype(own.dtype), everything, shard)
        )
        return jax.tree.map(lambda a, b: jnp.where(reached, a, b), new, before)

    return lax.fori_loop(0, length, prefix_turn, start)


def carried_in(shard, axis, combine, identity):
    length, position = (lax.axis_size(axis), lax.axis_index(axis))
    everything = jax.tree.map(
        lambda part, kind: lax.all_gather(part.astype(kind), axis),
        shard,
        jax.tree.map(lambda a: jnp.bfloat16 if a.dtype == jnp.float32 else a.dtype, shard),
    )
    start = jax.tree.map(
        lambda part, zero: jnp.broadcast_to(jnp.asarray(zero, part.dtype), part.shape),
        shard,
        identity,
    )

    def carried_turn(k, before):
        at = length - 1 - k
        reached = at > position
        new = combine(
            before, jax.tree.map(lambda part, own: part[at].astype(own.dtype), everything, shard)
        )
        return jax.tree.map(lambda a, b: jnp.where(reached, a, b), new, before)

    return lax.fori_loop(0, length, carried_turn, start)


def product(former, latter):
    return jnp.dot(former, latter, preferred_element_type=jnp.float32)


def product_left(former, latter):
    return lax.dot_general(
        former, latter, (((0,), (0,)), ((), ())), preferred_element_type=jnp.float32
    )


def product_right(former, latter):
    return lax.dot_general(
        former, latter, (((1,), (1,)), ((), ())), preferred_element_type=jnp.float32
    )


def over_heads(partial_sum):
    return lax.psum(partial_sum, "mp")


def gather_slots(pieces):
    return lax.all_gather(pieces.astype(jnp.bfloat16), "mp", axis=1, tiled=True).astype(
        pieces.dtype
    )


def rms_scale(values, scale_gain):
    mean_square = jnp.mean(values * values, axis=-1, keepdims=True)
    return values * lax.rsqrt(mean_square + EPS) * scale_gain


def rms_back(values, scale_gain, upstream):
    pullback = jax.vjp(rms_scale, values, scale_gain)[1]
    return pullback(upstream)


def running_bounds(lengths):
    places = jnp.arange(lengths.shape[0])
    upto = places[None, :] <= places[:-1, None]
    return jnp.sum(jnp.where(upto, lengths[None, :], 0), axis=1)


def running_sum(values):
    places = jnp.arange(values.shape[0])
    lower_part = (places[:, None] >= places[None, :]).astype(jnp.float32)
    return jnp.dot(lower_part, values, precision=HIGH, preferred_element_type=jnp.float32)


def segment_of(lengths, start_row, row_count):
    bounds = running_bounds(lengths)
    places = start_row + jnp.arange(row_count, dtype=jnp.int32)
    return jnp.sum((places[:, None] >= bounds[None, :]).astype(jnp.int32), axis=1)


def conv_silu(extended, kernel, segment_rows):
    row_count = extended.shape[0] - KCONV + 1
    segment_now = segment_rows[KCONV - 1 :]
    summed = jnp.zeros((row_count, extended.shape[1]), jnp.float32)
    for offset in range(KCONV):
        same_seq = (segment_rows[offset : offset + row_count] == segment_now)[:, None]
        summed = (
            summed
            + jnp.where(same_seq, extended[offset : offset + row_count], 0.0) * kernel[offset]
        )
    return jax.nn.silu(summed)


def block_output(
    head_values,
    write_vecs,
    read_vecs,
    step_size,
    log_rate,
    skip_term,
    state_value,
    segment_rows,
    segment_prev,
):
    length = head_values.shape[0]
    running = running_sum(-step_size * jnp.exp(log_rate))
    places = jnp.arange(length)
    allowed = (places[:, None] >= places[None, :]) & (
        segment_rows[:, None] == segment_rows[None, :]
    )
    allowed = allowed[:, :, None]
    spread = jnp.where(allowed, running[:, None, :] - running[None, :, :], 0.0)
    factors = jnp.where(allowed, jnp.exp(spread), 0.0)
    affinity = jnp.dot(read_vecs, write_vecs.T, precision=HIGH, preferred_element_type=jnp.float32)
    mixing = factors * affinity[:, :, None] * step_size[None, :, :]
    inside = jnp.einsum("tsh,shp->thp", mixing, head_values, precision=HIGH)
    carried = jnp.where((segment_rows == segment_prev)[:, None], jnp.exp(running), 0.0)
    reading = (
        jnp.einsum("tn,hpn->thp", read_vecs, state_value, precision=HIGH) * carried[:, :, None]
    )
    result = inside + reading + skip_term[None, :, None] * head_values
    return result.reshape(length, -1)


def block_summary(head_values, write_vecs, step_size, log_rate, segment_rows, segment_prev):
    running = running_sum(-step_size * jnp.exp(log_rate))
    latest = running[-1]
    in_tail = (segment_rows == segment_rows[-1])[:, None]
    weights = jnp.where(in_tail, jnp.exp(latest[None, :] - running), 0.0) * step_size
    scaled = weights[:, :, None] * head_values
    state_local = jnp.einsum("shp,sn->hpn", scaled, write_vecs, precision=HIGH)
    decay_total = jnp.where(segment_rows[-1] == segment_prev, jnp.exp(latest), 0.0)
    return (decay_total, state_local)


def combine_state(earlier, later):
    return (earlier[0] * later[0], later[0][:, None, None] * earlier[1] + later[1])


def patch_attention(queries, keys_all, values_all):
    row_count = queries.shape[0]
    head_count = queries.shape[1] // HDIM
    query_rows = queries.reshape(row_count // PATCH, PATCH, head_count, HDIM)
    key_rows = keys_all.reshape(row_count // PATCH, PATCH, head_count, HDIM)
    value_rows = values_all.reshape(row_count // PATCH, PATCH, head_count, HDIM)
    scores = jnp.einsum("bihd,bjhd->bhij", query_rows, key_rows, precision=HIGH) * HDIM ** (-0.5)
    causal = jnp.arange(PATCH)[:, None] >= jnp.arange(PATCH)[None, :]
    scores = jnp.where(causal, scores, -1e30)
    peak = jnp.max(scores, axis=-1, keepdims=True)
    probs = jnp.exp(scores - peak)
    probs = probs / jnp.sum(probs, axis=-1, keepdims=True)
    context = jnp.einsum("bhij,bjhd->bihd", probs, value_rows, precision=HIGH)
    return context.reshape(row_count, head_count * HDIM)


def add_tail(main_rows, tail_rows):
    keep_count = main_rows.shape[0] - tail_rows.shape[0]
    return jnp.concatenate([main_rows[:keep_count], main_rows[keep_count:] + tail_rows], axis=0)


def gathered_plan(
    byte_input,
    seq_lengths,
    cotangent,
    gain_global,
    patch_in,
    mixer_gate,
    mixer_input,
    mixer_state,
    mixer_step,
    conv_input,
    conv_state,
    step_bias,
    decay_log,
    skip_gain,
    gain_mixer,
    mixer_out,
    patch_out,
    gain_attend,
    attend_query,
    attend_key,
    attend_value,
    attend_out,
    gain_feed,
    feed_gate,
    feed_up,
    feed_down,
):
    group_size = lax.axis_size("mp")
    slot_width = PATCH * E // group_size
    slot_start = lax.axis_index("mp") * slot_width
    first_row = lax.axis_index("seq") * BLOCK
    segment_ext = segment_of(seq_lengths, first_row - (KCONV - 1), BLOCK + KCONV - 1)
    segment_rows = segment_ext[KCONV - 1 :]
    segment_prev = segment_of(seq_lengths, first_row - 1, 1)[0]

    def fetch_global():
        return (
            lax.all_gather(patch_in, "seq", axis=0, tiled=True),
            lax.all_gather(mixer_gate, "seq", axis=0, tiled=True),
            lax.all_gather(mixer_input, "seq", axis=0, tiled=True),
            lax.all_gather(mixer_state, "seq", axis=0, tiled=True),
            lax.all_gather(mixer_step, "seq", axis=0, tiled=True),
            lax.all_gather(mixer_out, "seq", axis=0, tiled=True),
            lax.all_gather(patch_out, "seq", axis=0, tiled=True),
        )

    def fetch_local():
        return (
            lax.all_gather(attend_query, "seq", axis=0, tiled=True),
            lax.all_gather(attend_key, "seq", axis=0, tiled=True),
            lax.all_gather(attend_value, "seq", axis=0, tiled=True),
            lax.all_gather(attend_out, "seq", axis=0, tiled=True),
            lax.all_gather(feed_gate, "seq", axis=0, tiled=True),
            lax.all_gather(feed_up, "seq", axis=0, tiled=True),
            lax.all_gather(feed_down, "seq", axis=0, tiled=True),
        )

    def conv_of(extended, kernel):
        return conv_silu(extended, kernel, segment_ext)

    def summary_of(values_in, writes_in, steps_in, rates_in):
        return block_summary(values_in, writes_in, steps_in, rates_in, segment_rows, segment_prev)

    def output_of(values_in, writes_in, reads_in, steps_in, rates_in, skips_in, state_value):
        return block_output(
            values_in,
            writes_in,
            reads_in,
            steps_in,
            rates_in,
            skips_in,
            state_value,
            segment_rows,
            segment_prev,
        )

    full_patch_in, full_gate, full_input, full_state, full_step, full_mixout, full_patchout = (
        fetch_global()
    )
    patches = byte_input.reshape(BLOCK, PATCH * E)
    local_bytes = lax.dynamic_slice_in_dim(patches, slot_start, slot_width, 1)
    hidden = over_heads(product(local_bytes, full_patch_in))
    normed = rms_scale(hidden, gain_global).astype(jnp.bfloat16)
    gate_pre = product(normed, full_gate)
    input_pre = product(normed, full_input)
    state_pre = product(normed, full_state)
    step_pre = product(normed, full_step)
    rim_rows = shifted((input_pre[BLOCK - KCONV + 1 :], state_pre[BLOCK - KCONV + 1 :]), "seq", 1)
    input_ext = jnp.concatenate([rim_rows[0], input_pre], axis=0)
    state_ext = jnp.concatenate([rim_rows[1], state_pre], axis=0)
    input_conv = conv_of(input_ext, conv_input)
    state_conv = conv_of(state_ext, conv_state)
    step_size = jax.nn.softplus(step_pre + step_bias)
    head_count = step_size.shape[1]
    head_values = input_conv.reshape(BLOCK, head_count, HDIM)
    write_vecs = state_conv[:, :NSTATE]
    read_vecs = state_conv[:, NSTATE:]
    decay_total, state_local = summary_of(head_values, write_vecs, step_size, decay_log)
    identity = (jnp.ones_like(decay_total), jnp.zeros_like(state_local))
    state_in = prefix((decay_total, state_local), "seq", combine_state, identity)[1]
    mixer_rows = output_of(
        head_values, write_vecs, read_vecs, step_size, decay_log, skip_gain, state_in
    )
    gate_sigm = jax.nn.sigmoid(gate_pre)
    gate_silu = gate_pre * gate_sigm
    gated = mixer_rows * gate_silu
    mean_square = over_heads(jnp.sum(gated * gated, axis=-1, keepdims=True)) / DI
    root_inverse = lax.rsqrt(mean_square + EPS)
    mixed = (gated * root_inverse * gain_mixer).astype(jnp.bfloat16)
    merged = hidden + over_heads(product(mixed, full_mixout))
    merged_low = merged.astype(jnp.bfloat16)
    slot_values = gather_slots(product(merged_low, full_patchout)).reshape(TOK_DEV, E)
    residual = byte_input.astype(jnp.float32) + slot_values
    full_query, full_key, full_value, full_attout, full_feedgate, full_up, full_down = fetch_local()
    attend_in = rms_scale(residual, gain_attend).astype(jnp.bfloat16)
    queries = product(attend_in, full_query)
    keys_all = product(attend_in, full_key)
    values_all = product(attend_in, full_value)
    context = patch_attention(queries, keys_all, values_all).astype(jnp.bfloat16)
    middle = residual + over_heads(product(context, full_attout))
    feed_in = rms_scale(middle, gain_feed).astype(jnp.bfloat16)
    gate_value = product(feed_in, full_feedgate)
    up_value = product(feed_in, full_up)
    gate_sig = jax.nn.sigmoid(gate_value)
    hidden_units = (gate_value * gate_sig * up_value).astype(jnp.bfloat16)
    byte_output = middle + over_heads(product(hidden_units, full_down))
    full_query, full_key, full_value, full_attout, full_feedgate, full_up, full_down = fetch_local()
    out_low = cotangent.astype(jnp.bfloat16)
    grad_feed_down = product_left(hidden_units, out_low)
    grad_units = product_right(out_low, full_down)
    grad_gate_value = (
        grad_units * up_value * gate_sig * (1.0 + gate_value * (1.0 - gate_sig))
    ).astype(jnp.bfloat16)
    grad_up_value = (grad_units * gate_value * gate_sig).astype(jnp.bfloat16)
    grad_feed_gate = product_left(feed_in, grad_gate_value)
    grad_feed_up = product_left(feed_in, grad_up_value)
    grad_feed_in = over_heads(
        product_right(grad_gate_value, full_feedgate) + product_right(grad_up_value, full_up)
    )
    grad_middle_part, grad_gain_feed = rms_back(middle, gain_feed, grad_feed_in)
    grad_middle = cotangent + grad_middle_part
    middle_low = grad_middle.astype(jnp.bfloat16)
    grad_attend_out = product_left(context, middle_low)
    grad_context = product_right(middle_low, full_attout)
    attention_pull = jax.vjp(patch_attention, queries, keys_all, values_all)[1]
    grad_query_raw, grad_key_raw, grad_value_raw = attention_pull(grad_context)
    grad_query_rows = grad_query_raw.astype(jnp.bfloat16)
    grad_key_rows = grad_key_raw.astype(jnp.bfloat16)
    grad_value_rows = grad_value_raw.astype(jnp.bfloat16)
    grad_attend_query = product_left(attend_in, grad_query_rows)
    grad_attend_key = product_left(attend_in, grad_key_rows)
    grad_attend_value = product_left(attend_in, grad_value_rows)
    grad_attend_in = over_heads(
        product_right(grad_query_rows, full_query)
        + product_right(grad_key_rows, full_key)
        + product_right(grad_value_rows, full_value)
    )
    grad_residual_part, grad_gain_attend = rms_back(residual, gain_attend, grad_attend_in)
    grad_residual = grad_middle + grad_residual_part
    local_sums = (
        lax.psum_scatter(grad_attend_query, "seq", scatter_dimension=0, tiled=True),
        lax.psum_scatter(grad_attend_key, "seq", scatter_dimension=0, tiled=True),
        lax.psum_scatter(grad_attend_value, "seq", scatter_dimension=0, tiled=True),
        lax.psum_scatter(grad_attend_out, "seq", scatter_dimension=0, tiled=True),
        lax.psum_scatter(grad_feed_gate, "seq", scatter_dimension=0, tiled=True),
        lax.psum_scatter(grad_feed_up, "seq", scatter_dimension=0, tiled=True),
        lax.psum_scatter(grad_feed_down, "seq", scatter_dimension=0, tiled=True),
    )
    full_patch_in, full_gate, full_input, full_state, full_step, full_mixout, full_patchout = (
        fetch_global()
    )
    residual_patches = grad_residual.reshape(BLOCK, PATCH * E)
    slot_grad = lax.dynamic_slice_in_dim(residual_patches, slot_start, slot_width, 1).astype(
        jnp.bfloat16
    )
    grad_patch_out = product_left(merged_low, slot_grad)
    grad_merged = over_heads(product_right(slot_grad, full_patchout))
    merged_grad_low = grad_merged.astype(jnp.bfloat16)
    grad_mixer_out = product_left(mixed, merged_grad_low)
    grad_mixed = product_right(merged_grad_low, full_mixout)
    grad_gain_mixer = jnp.sum(grad_mixed * gated * root_inverse, axis=0)
    scaled_grad = grad_mixed * gain_mixer
    inner_dot = over_heads(jnp.sum(scaled_grad * gated, axis=-1, keepdims=True))
    grad_gated = scaled_grad * root_inverse - gated * inner_dot * root_inverse**3 / DI
    grad_mixer_rows = grad_gated * gate_silu
    grad_gate_pre = grad_gated * mixer_rows * gate_sigm * (1.0 + gate_pre * (1.0 - gate_sigm))
    output_pull = jax.vjp(
        output_of, head_values, write_vecs, read_vecs, step_size, decay_log, skip_gain, state_in
    )[1]
    (
        grad_values_a,
        grad_writes_a,
        grad_reads,
        grad_steps_a,
        grad_rates_a,
        grad_skip_gain,
        grad_state_in,
    ) = output_pull(grad_mixer_rows)
    state_end = carried_in((decay_total, grad_state_in), "seq", combine_state, identity)[1]
    summary_pull = jax.vjp(summary_of, head_values, write_vecs, step_size, decay_log)[1]
    grad_values_b, grad_writes_b, grad_steps_b, grad_rates_b = summary_pull(
        (jnp.sum(state_end * state_in, axis=(1, 2)), state_end)
    )
    grad_input_conv = (grad_values_a + grad_values_b).reshape(BLOCK, -1)
    grad_state_conv = over_heads(
        jnp.concatenate([grad_writes_a + grad_writes_b, grad_reads], axis=1)
    )
    grad_step_pre = (grad_steps_a + grad_steps_b) * jax.nn.sigmoid(step_pre + step_bias)
    grad_step_bias = jnp.sum(grad_step_pre, axis=0)
    grad_decay_log = grad_rates_a + grad_rates_b
    grad_input_ext, grad_conv_input = jax.vjp(conv_of, input_ext, conv_input)[1](grad_input_conv)
    grad_state_ext, grad_conv_state = jax.vjp(conv_of, state_ext, conv_state)[1](grad_state_conv)
    rim_back = shifted((grad_input_ext[: KCONV - 1], grad_state_ext[: KCONV - 1]), "seq", -1)
    grad_input_low = add_tail(grad_input_ext[KCONV - 1 :], rim_back[0]).astype(jnp.bfloat16)
    grad_state_low = add_tail(grad_state_ext[KCONV - 1 :], rim_back[1]).astype(jnp.bfloat16)
    grad_gate_low = grad_gate_pre.astype(jnp.bfloat16)
    grad_step_low = grad_step_pre.astype(jnp.bfloat16)
    grad_mixer_gate = product_left(normed, grad_gate_low)
    grad_mixer_input = product_left(normed, grad_input_low)
    grad_mixer_state = product_left(normed, grad_state_low)
    grad_mixer_step = product_left(normed, grad_step_low)
    head_part = over_heads(
        product_right(grad_gate_low, full_gate)
        + product_right(grad_input_low, full_input)
        + product_right(grad_step_low, full_step)
    )
    grad_normed = head_part + product_right(grad_state_low, full_state)
    grad_hidden_part, grad_gain_global = rms_back(hidden, gain_global, grad_normed)
    hidden_grad_low = (grad_merged + grad_hidden_part).astype(jnp.bfloat16)
    grad_patch_in = product_left(local_bytes, hidden_grad_low)
    grad_byte_part = gather_slots(product_right(hidden_grad_low, full_patch_in)).reshape(TOK_DEV, E)
    grad_input = (grad_residual + grad_byte_part).astype(jnp.bfloat16)
    global_sums = (
        lax.psum_scatter(grad_patch_in, "seq", scatter_dimension=0, tiled=True),
        lax.psum_scatter(grad_mixer_gate, "seq", scatter_dimension=0, tiled=True),
        lax.psum_scatter(grad_mixer_input, "seq", scatter_dimension=0, tiled=True),
        lax.psum_scatter(grad_mixer_state, "seq", scatter_dimension=0, tiled=True),
        lax.psum_scatter(grad_mixer_step, "seq", scatter_dimension=0, tiled=True),
        lax.psum_scatter(grad_mixer_out, "seq", scatter_dimension=0, tiled=True),
        lax.psum_scatter(grad_patch_out, "seq", scatter_dimension=0, tiled=True),
    )
    small_sums = lax.psum(
        (
            grad_gain_global,
            grad_conv_input,
            grad_conv_state,
            grad_step_bias,
            grad_decay_log,
            grad_skip_gain,
            grad_gain_mixer,
            grad_gain_attend,
            grad_gain_feed,
        ),
        "seq",
    )
    return (
        byte_output.astype(jnp.bfloat16),
        grad_input,
        small_sums[0],
        global_sums[0],
        global_sums[1],
        global_sums[2],
        global_sums[3],
        global_sums[4],
        small_sums[1],
        small_sums[2],
        small_sums[3],
        small_sums[4],
        small_sums[5],
        small_sums[6],
        global_sums[5],
        global_sums[6],
        small_sums[7],
        local_sums[0],
        local_sums[1],
        local_sums[2],
        local_sums[3],
        small_sums[8],
        local_sums[4],
        local_sums[5],
        local_sums[6],
    )


ROWS = 512
HALF = 256
HEADS_STEP = 8
WIDTH = HEADS_STEP * HDIM
STEPS = 8 // HEADS_STEP
VMEM_BYTES = 56 * 1024 * 1024


def bf(values):
    return values.astype(jnp.bfloat16)


def up(values):
    return values.astype(jnp.float32)


def whole(shape):
    return pl.BlockSpec(shape, lambda *_: (0,) * len(shape))


def scalars():
    return pl.BlockSpec(memory_space=pltpu.SMEM)


def kernel_params(limit=VMEM_BYTES):
    return pltpu.CompilerParams(vmem_limit_bytes=limit, dimension_semantics=("arbitrary",))


def cost(flops, size):
    return pl.CostEstimate(flops=flops, bytes_accessed=size, transcendentals=0)


def block_index(place, k):
    c, y = (place[0], place[1])
    c = 1 - c if k >= 2 else c
    y = 1 - y if k % 2 else y
    return c * 2 + y


def put_pieces(place, pieces, out_ref, rows=128):
    for k, piece in enumerate(pieces):
        at = pl.multiple_of(block_index(place, k) * rows, rows)
        out_ref[pl.ds(at, rows), :] = piece[:rows, :]


def lane_of(values, lane):
    lanes = lax.broadcasted_iota(jnp.int32, values.shape, 1)
    return jnp.sum(jnp.where(lanes == lane, values, 0.0), axis=1, keepdims=True)


def segments(lengths, shift, shape, axis):
    rows = lax.broadcasted_iota(jnp.int32, shape, axis) - shift
    total = jnp.zeros(shape, jnp.int32)
    bound = 0
    for k in range(lengths.shape[0] - 1):
        bound = bound + lengths[k]
        total = total + (rows >= bound).astype(jnp.int32)
    return total


def tap_masks(lengths):
    here = segments(lengths, 0, (ROWS, 1), 0)
    rows = lax.broadcasted_iota(jnp.int32, (ROWS, 1), 0)
    return [
        up((rows >= j) & (segments(lengths, j, (ROWS, 1), 0) == here))
        for j in range(1, KCONV)
    ]


def conv_rows(values, taps, masks):
    total = values * taps[KCONV - 1 : KCONV, :]
    for j in range(1, KCONV):
        earlier = pltpu.roll(values, j, 0) * masks[j - 1]
        total = total + earlier * taps[KCONV - 1 - j : KCONV - j, :]
    return total


def conv_back(values, taps, masks, grads):
    rows_grad = grads * taps[KCONV - 1 : KCONV, :]
    taps_grad = [None] * KCONV
    taps_grad[KCONV - 1] = jnp.sum(grads * values, axis=0, keepdims=True)
    for j in range(1, KCONV):
        masked = grads * masks[j - 1]
        rows_grad = rows_grad + pltpu.roll(masked, ROWS - j, 0) * taps[
            KCONV - 1 - j : KCONV - j, :
        ]
        taps_grad[KCONV - 1 - j] = jnp.sum(
            masked * pltpu.roll(values, j, 0), axis=0, keepdims=True
        )
    return rows_grad, taps_grad


def silu_parts(values):
    gate = 1.0 / (1.0 + jnp.exp(-values))
    return values * gate, gate * (1.0 + values * (1.0 - gate))


def softplus(values):
    return jnp.maximum(values, 0.0) + jnp.log1p(jnp.exp(-jnp.abs(values)))


def three_parts(values):
    first = bf(values)
    rest = values - up(first)
    second = bf(rest)
    return first, second, bf(rest - up(second))


def sums_left(ones, values):
    first, second, third = (product(ones, part) for part in three_parts(values))
    return (third + second) + first


def sums_right(values, ones):
    first, second, third = (product(part, ones) for part in three_parts(values))
    return (third + second) + first


def lower(shape, flip=False):
    rows = lax.broadcasted_iota(jnp.int32, shape, 0)
    columns = lax.broadcasted_iota(jnp.int32, shape, 1)
    return bf(up(rows <= columns) if flip else up(rows >= columns))


def allowed_pairs(lengths):
    rows = lax.broadcasted_iota(jnp.int32, (ROWS, ROWS), 0)
    columns = lax.broadcasted_iota(jnp.int32, (ROWS, ROWS), 1)
    same = segments(lengths, 0, (ROWS, 1), 0) == segments(lengths, 0, (1, ROWS), 1)
    return (rows >= columns) & same


def decay_block(run, run_row):
    return jnp.exp(jnp.minimum(run - run_row, 0.0))


def head_columns(j, i, table):
    return lane_of(table, HEADS_STEP * j + i)


def by_head(parts):
    lanes = lax.broadcasted_iota(jnp.int32, (1, WIDTH), 1)
    value = parts[-1]
    for i in range(len(parts) - 2, -1, -1):
        value = jnp.where(lanes < (i + 1) * HDIM, parts[i], value)
    return value


def wide(mask):
    return jnp.concatenate([mask] * (WIDTH // 128), axis=1)


def shared_setup(
    j, lengths, pre_ref, state_taps, params, affinity, step_ref, run_ref, run_t, wr_ref, mask_ref
):
    @pl.when(j == 0)
    def _():
        step = softplus(pre_ref[:, 256:] + params[0:1, :])
        step_ref[...] = step
        running = sums_left(lower((ROWS, ROWS)), -step * jnp.exp(params[1:2, :]))
        run_ref[...] = running
        run_t[...] = running.T
        masks = [jnp.broadcast_to(mask, (ROWS, 128)) for mask in tap_masks(lengths)]
        for k in range(KCONV - 1):
            mask_ref[k] = masks[k]
        masks = [jnp.concatenate([mask, mask], axis=1) for mask in masks]
        state = silu_parts(conv_rows(pre_ref[:, :256], state_taps[...], masks))[0]
        wr_ref[...] = bf(state)
        pairs = product_right(bf(state[:, NSTATE:]), bf(state[:, :NSTATE]))
        affinity[...] = jnp.where(allowed_pairs(lengths), pairs, 0.0)


def weight_copies(place, pieces, weights, arrived):
    copies = []
    for v, piece in enumerate(pieces):
        at = pl.multiple_of(place[3 + v] * 128 + (64 if v == 8 else 0), 64)
        target = weights.at[pl.ds(at, piece.shape[0]), :]
        copies.append(pltpu.make_async_copy(piece, target, arrived.at[v]))
    return copies


def start_weights(place, pieces, weights, arrived):
    copies = weight_copies(place, pieces, weights, arrived)
    for copy in copies:
        copy.start()
    return copies


def put_mix_out(parts, mix_out):
    for s in range(8):
        rows = slice(s * HDIM, (s + 1) * HDIM)
        mix_out[rows, :512] = parts[s * 128 : s * 128 + 64, :]
        mix_out[rows, 512:] = parts[s * 128 + 64 : (s + 1) * 128, :]


def mixer_forward_kernel(
    place, lengths, p0, p1, p2, p3, table, state_taps, params, w0, w1, w2, w3, w4, w5, w6, w7, w8,
    send, keep, own_normed, gate_pre, input_pre, rest_pre, inside, scaled,
    normed, pre, all_scaled, affinity, step_ref, run_ref, run_t, wr_ref, mask_ref, squares,
    mix_out, weights, arrived, rest_sent,
):
    j = pl.program_id(0)
    rest_copy = pltpu.make_async_copy(pre.at[:, 1024:], rest_pre, rest_sent)

    @pl.when(j == 0)
    def _():
        pieces = (w0, w1, w2, w3, w4, w5, w6, w7, w8)
        copies = start_weights(place, [p.at[:, :1920] for p in pieces], weights, arrived)
        put_pieces(place, (p0, p1, p2, p3), normed)
        own = pl.ds(pl.multiple_of(place[2] * 128, 128), 128)
        own_normed[...] = normed[:, own]
        squares[...] = jnp.zeros_like(squares)
        for copy in copies:
            copy.wait()
        pre[...] = product(normed[...], weights[:, :1408])
        put_mix_out(weights.at[:, 1408:], mix_out)
        rest_copy.start()

    shared_setup(
        j, lengths, pre.at[:, 1024:], state_taps, params, affinity, step_ref, run_ref, run_t,
        wr_ref, mask_ref,
    )
    columns = pl.ds(pl.multiple_of(j * WIDTH, WIDTH), WIDTH)
    masks = [wide(mask_ref[k]) for k in range(KCONV - 1)]
    before = pre[:, pl.ds(pl.multiple_of(512 + j * WIDTH, WIDTH), WIDTH)]
    input_pre[...] = before
    values = silu_parts(conv_rows(before, table[:, columns], masks))[0]
    step = by_head([head_columns(j, i, step_ref[...]) for i in range(HEADS_STEP)])
    steps = bf(values * step)
    inner = []
    for r in range(2):
        seen = (r + 1) * HALF
        pairs = affinity[r * HALF : seen, :seen]
        parts = []
        for i in range(HEADS_STEP):
            run = head_columns(j, i, run_ref[r * HALF : seen, :])
            run_row = run_t[pl.ds(HEADS_STEP * j + i, 1), :seen]
            mixing = bf(pairs * decay_block(run, run_row))
            parts.append(product(mixing, steps[:seen, i * HDIM : (i + 1) * HDIM]))
        inner.append(jnp.concatenate(parts, axis=1))
    inner = jnp.concatenate(inner, axis=0)
    inside[...] = inner
    skip = by_head([head_columns(j, i, params[2:3, :]) for i in range(HEADS_STEP)])
    gate = pre[:, columns]
    gate_pre[...] = gate
    gated = (inner + skip * values) * silu_parts(gate)[0]
    low = bf(gated * table[4:5, columns])
    all_scaled[:, columns] = low
    scaled[...] = low
    squares[...] += jnp.broadcast_to(jnp.sum(gated * gated, axis=1, keepdims=True), (ROWS, 128))

    @pl.when(j == STEPS - 1)
    def _():
        for out, half in ((send, 1 - place[0]), (keep, place[0])):
            at = pl.ds(pl.multiple_of(half * HALF, HALF), HALF)
            out[:, :1024] = bf(product(all_scaled[at, :], mix_out[...]))
            out[:, 1024:] = bf(squares[at, :])
        rest_copy.wait()


def by_columns():
    return pl.BlockSpec((ROWS, WIDTH), lambda j: (0, j))


def mixer_forward(place, lengths, pieces, weights, table, state_taps, params):
    f32, low = (jnp.float32, jnp.bfloat16)
    shapes = [
        ((HALF, 1152), low, whole((HALF, 1152))),
        ((HALF, 1152), low, whole((HALF, 1152))),
        ((ROWS, 128), low, whole((ROWS, 128))),
        ((ROWS, 512), f32, by_columns()),
        ((ROWS, 512), f32, by_columns()),
        ((ROWS, 384), f32, pl.BlockSpec(memory_space=pl.ANY)),
        ((ROWS, 512), f32, by_columns()),
        ((ROWS, 512), low, by_columns()),
    ]
    return pl.pallas_call(
        mixer_forward_kernel,
        grid=(STEPS,),
        in_specs=[scalars(), scalars()]
        + [whole(a.shape) for a in (*pieces, table, state_taps, params)]
        + [pl.BlockSpec(memory_space=pl.ANY)] * 9,
        out_specs=[spec for _, _, spec in shapes],
        out_shape=[jax.ShapeDtypeStruct(s, t) for s, t, _ in shapes],
        scratch_shapes=[
            pltpu.VMEM((ROWS, 1024), low),
            pltpu.VMEM((ROWS, 1408), f32),
            pltpu.VMEM((ROWS, 512), low),
            pltpu.VMEM((ROWS, ROWS), f32),
            pltpu.VMEM((ROWS, 128), f32),
            pltpu.VMEM((ROWS, 128), f32),
            pltpu.VMEM((128, ROWS), f32),
            pltpu.VMEM((ROWS, 256), low),
            pltpu.VMEM((KCONV - 1, ROWS, 128), f32),
            pltpu.VMEM((ROWS, 128), f32),
            pltpu.VMEM((512, 1024), low),
            pltpu.VMEM((1024, 1920), low),
            pltpu.SemaphoreType.DMA((9,)),
            pltpu.SemaphoreType.DMA,
        ],
        compiler_params=kernel_params(),
        cost_estimate=cost(1_000_000, 10_000),
        name="mixer_forward",
    )(place, lengths, *pieces, table, state_taps, params, *weights)


def mixer_backward_kernel(
    place, lengths, g0, g1, g2, g3, table, state_taps, params, gate_pre, input_pre, rest_pre, inside,
    w0, w1, w2, w3, w4, w5, w6, w7, w8,
    send, keep, grads, merged, table_grad, state_taps_grad, params_grad,
    grad_mixed, kappa, affinity, step_ref, run_ref, run_t, wr_ref, mask_ref, pair_grad, run_grad,
    step_grad, out_parts, mix_out, weights, out_arrived, arrived,
):
    j = pl.program_id(0)
    pieces = (w0, w1, w2, w3, w4, w5, w6, w7, w8)
    first_copies = weight_copies(place, [p.at[:, :1408] for p in pieces], weights, arrived)

    @pl.when(j == 0)
    def _():
        copies = weight_copies(place, [p.at[:, 1408:1920] for p in pieces], out_parts, out_arrived)
        for copy in copies + first_copies:
            copy.start()
        for copy in copies:
            copy.wait()

    shared_setup(
        j, lengths, rest_pre, state_taps, params, affinity, step_ref, run_ref, run_t, wr_ref, mask_ref
    )

    @pl.when(j == 0)
    def _():
        for k, piece in enumerate((g0, g1, g2, g3)):
            at = pl.ds(pl.multiple_of(block_index(place, k) * 128, 128), 128)
            merged[at, :] = piece[:128, :1024]
            kappa[at, :] = up(piece[:128, 1024:])
        put_mix_out(out_parts, mix_out)
        grad_mixed[...] = product_right(merged[...], mix_out[...])
        pair_grad[...] = jnp.zeros_like(pair_grad)
        run_grad[...] = jnp.zeros_like(run_grad)
        step_grad[...] = jnp.zeros_like(step_grad)
        params_grad[...] = jnp.zeros_like(params_grad)
        table_grad[...] = jnp.zeros_like(table_grad)
        state_taps_grad[...] = jnp.zeros_like(state_taps_grad)

    columns = pl.ds(pl.multiple_of(j * WIDTH, WIDTH), WIDTH)
    columns_in = pl.ds(pl.multiple_of(512 + j * WIDTH, WIDTH), WIDTH)
    masks = [wide(mask_ref[k]) for k in range(KCONV - 1)]
    taps = table[:, columns]
    before = input_pre[...]
    values, values_slope = silu_parts(conv_rows(before, taps, masks))
    step = by_head([head_columns(j, i, step_ref[...]) for i in range(HEADS_STEP)])
    skip = by_head([head_columns(j, i, params[2:3, :]) for i in range(HEADS_STEP)])
    steps = bf(values * step)
    gate, gate_slope = silu_parts(gate_pre[...])
    within = inside[...]
    rows = within + skip * values
    gated = rows * gate
    mixed_grad = grad_mixed[:, columns]
    gain_grad = jnp.sum(mixed_grad * gated, axis=0, keepdims=True)
    gated_grad = mixed_grad * table[4:5, columns] - gated * wide(kappa[...])
    grads[:, columns] = bf(gated_grad * rows * gate_slope)
    rows_grad = gated_grad * gate
    rows_low = bf(rows_grad)
    rows_turned = rows_low.T
    steps_grads = []
    for i in range(HEADS_STEP):
        run = head_columns(j, i, run_ref[...])
        run_row = run_t[pl.ds(HEADS_STEP * j + i, 1), :]
        lanes = slice(i * HDIM, (i + 1) * HDIM)
        turned = jnp.zeros((HDIM, ROWS), jnp.float32)
        for r in range(2):
            seen = (r + 1) * HALF
            block = slice(r * HALF, seen)
            decay = decay_block(run[block, :], run_row[:, :seen])
            mixing = bf(affinity[block, :seen] * decay)
            mixing_grad = product_right(rows_low[block, lanes], steps[:seen, lanes])
            pair_grad[block, :seen] += mixing_grad * decay
            part = product(rows_turned[lanes, block], mixing)
            if seen < ROWS:
                part = jnp.concatenate(
                    [part, jnp.zeros((HDIM, ROWS - seen), jnp.float32)], axis=1
                )
            turned = turned + part
        steps_grads.append(turned)
    steps_grad = jnp.concatenate(steps_grads, axis=0).T
    lanes_in = lax.broadcasted_iota(jnp.int32, (WIDTH, 128), 0)
    lanes_out = lax.broadcasted_iota(jnp.int32, (WIDTH, 128), 1)
    to_head = bf(up(lanes_out == HEADS_STEP * j + lanes_in // HDIM))
    run_grad[...] += sums_right(up(rows_low) * within - up(steps) * steps_grad, to_head)
    step_grad[...] += sums_right(steps_grad * values, to_head)
    skip_sums = jnp.sum(rows_grad * values, axis=0, keepdims=True)
    params_grad[2:3, :] += sums_right(jnp.broadcast_to(skip_sums, (8, WIDTH)), to_head)[:1, :]
    conv_grad = (steps_grad * step + skip * rows_grad) * values_slope
    before_grad, taps_grad = conv_back(before, taps, masks, conv_grad)
    grads[:, columns_in] = bf(before_grad)
    for k in range(KCONV):
        table_grad[k : k + 1, columns] = taps_grad[k]
    table_grad[4:5, columns] = gain_grad

    @pl.when(j == STEPS - 1)
    def _():
        decay_grad = sums_left(lower((ROWS, ROWS), True), run_grad[...])
        rate = jnp.exp(params[1:2, :])
        step_total = step_grad[...] - decay_grad * rate
        slope = 1.0 / (1.0 + jnp.exp(-(rest_pre[:, 256:] + params[0:1, :])))
        lanes = lax.broadcasted_iota(jnp.int32, (1, 128), 1)
        step_total = jnp.where(lanes < 8, step_total * slope, 0.0)
        grads[:, 1280:] = bf(step_total)
        params_grad[0:1, :] = jnp.sum(step_total, axis=0, keepdims=True)
        params_grad[1:2, :] = jnp.sum(
            -decay_grad * step_ref[...] * rate, axis=0, keepdims=True
        )
        pairs = jnp.where(allowed_pairs(lengths), pair_grad[...], 0.0)
        read_grad = product(bf(pairs), wr_ref[:, :NSTATE])
        write_grad = product(bf(pairs.T), wr_ref[:, NSTATE:])
        state_masks = [
            jnp.concatenate([mask_ref[k], mask_ref[k]], axis=1) for k in range(KCONV - 1)
        ]
        state_before = rest_pre[:, :256]
        state_slope = silu_parts(conv_rows(state_before, state_taps[...], state_masks))[1]
        state_grad, state_taps_parts = conv_back(
            state_before,
            state_taps[...],
            state_masks,
            jnp.concatenate([write_grad, read_grad], axis=1) * state_slope,
        )
        grads[:, 1024:1280] = bf(state_grad)
        for k in range(KCONV):
            state_taps_grad[k : k + 1, :] = state_taps_parts[k]
        for copy in first_copies:
            copy.wait()
        for out, half in ((send, 1 - place[0]), (keep, place[0])):
            at = pl.ds(pl.multiple_of(half * HALF, HALF), HALF)
            out[:, :1024] = bf(product_right(grads[at, :], weights[...]))
            out[:, 1024:] = grads[at, 1024:1280]


def mixer_backward(place, lengths, pieces, weights, table, state_taps, params, pre, inside):
    gate_pre, input_pre, rest_pre = pre
    f32, low = (jnp.float32, jnp.bfloat16)
    shapes = [
        ((HALF, 1280), low),
        ((HALF, 1280), low),
        ((ROWS, 1408), low),
        ((ROWS, 1024), low),
        ((8, 512), f32),
        ((8, 256), f32),
        ((8, 128), f32),
    ]
    operands = (*pieces, table, state_taps, params)
    return pl.pallas_call(
        mixer_backward_kernel,
        grid=(STEPS,),
        in_specs=[scalars(), scalars()]
        + [whole(a.shape) for a in operands]
        + [by_columns(), by_columns(), whole(rest_pre.shape), by_columns()]
        + [pl.BlockSpec(memory_space=pl.ANY)] * 9,
        out_specs=[whole(s) for s, _ in shapes],
        out_shape=[jax.ShapeDtypeStruct(s, t) for s, t in shapes],
        scratch_shapes=[
            pltpu.VMEM((ROWS, 512), f32),
            pltpu.VMEM((ROWS, 128), f32),
            pltpu.VMEM((ROWS, ROWS), f32),
            pltpu.VMEM((ROWS, 128), f32),
            pltpu.VMEM((ROWS, 128), f32),
            pltpu.VMEM((128, ROWS), f32),
            pltpu.VMEM((ROWS, 256), low),
            pltpu.VMEM((KCONV - 1, ROWS, 128), f32),
            pltpu.VMEM((ROWS, ROWS), f32),
            pltpu.VMEM((ROWS, 128), f32),
            pltpu.VMEM((ROWS, 128), f32),
            pltpu.VMEM((1024, 512), low),
            pltpu.VMEM((512, 1024), low),
            pltpu.VMEM((1024, 1408), low),
            pltpu.SemaphoreType.DMA((9,)),
            pltpu.SemaphoreType.DMA((9,)),
        ],
        compiler_params=kernel_params(),
        cost_estimate=cost(1_000_000, 10_000),
        name="mixer_backward",
    )(place, lengths, *operands, gate_pre, input_pre, rest_pre, inside, *weights)


GROUP = 2


def patch_mask():
    rows = lax.broadcasted_iota(jnp.int32, (128, 128), 0)
    columns = lax.broadcasted_iota(jnp.int32, (128, 128), 1)
    return (rows >= columns) & (rows // PATCH == columns // PATCH)


def unit(values, n, i):
    start = n * 256 + (i % 4) * HDIM
    return values[(i // 4) * 128 : (i // 4 + 1) * 128, start : start + HDIM]


def stacked(parts):
    return jnp.stack(parts, axis=0)


def patch_probs(qkv, units, mask):
    scale = jnp.bfloat16(HDIM ** (-0.5))
    scores = stacked([product_right(unit(qkv, 0, i) * scale, unit(qkv, 1, i)) for i in units])
    scores = jnp.where(mask[None], scores, -1e30)
    weights = jnp.exp(scores - jnp.max(scores, axis=2, keepdims=True))
    return weights * (1.0 / jnp.sum(weights, axis=2, keepdims=True))


def split_blocks(values, keep, send):
    for k, out in ((0, keep), (1, send), (2, keep), (3, send)):
        out[k // 2] = bf(values[k * 128 : (k + 1) * 128, :])


def put_w_out(weights, w_out):
    for s in range(8):
        for q in range(4):
            at = s * 128 + q * 32
            w_out[s * 32 : (s + 1) * 32, q * 256 : (q + 1) * 256] = weights[at : at + 32, 768:]


def attend_forward_kernel(
    place, x0, x1, x2, x3, w0, w1, w2, w3, w4, w5, w6, w7, w8,
    keep, send, rows, qkv, context, w_out, weights, arrived,
):
    pieces = [p.at[:, 1920:] for p in (w0, w1, w2, w3, w4, w5, w6, w7, w8)]
    for copy in start_weights(place, pieces, weights, arrived):
        copy.wait()
    put_w_out(weights, w_out)
    for k, piece in enumerate((x0, x1, x2, x3)):
        rows[k * 128 : (k + 1) * 128, :] = piece[...]
    qkv[...] = bf(product(rows[...], weights[:, :768]))
    mask = patch_mask()
    for b in range(4 // GROUP):
        units = range(b * GROUP * 4, (b + 1) * GROUP * 4)
        probs = bf(patch_probs(qkv, units, mask))
        for n, i in enumerate(units):
            context[(i // 4) * 128 : (i // 4 + 1) * 128, (i % 4) * HDIM : (i % 4 + 1) * HDIM] = bf(
                product(probs[n], unit(qkv, 2, i))
            )
    split_blocks(product(context[...], w_out[...]), keep, send)


def attend_forward(place, pieces, weights):
    low = jnp.bfloat16
    shapes = [(2, 128, 1024), (2, 128, 1024), (ROWS, 1024), (ROWS, 768), (ROWS, 256)]
    return pl.pallas_call(
        attend_forward_kernel,
        grid=(1,),
        in_specs=[scalars()]
        + [whole(a.shape) for a in pieces]
        + [pl.BlockSpec(memory_space=pl.ANY)] * 9,
        out_specs=[whole(s) for s in shapes],
        out_shape=[jax.ShapeDtypeStruct(s, low) for s in shapes],
        compiler_params=kernel_params(),
        scratch_shapes=[
            pltpu.VMEM((256, 1024), low),
            pltpu.VMEM((1024, 1024), low),
            pltpu.SemaphoreType.DMA((9,)),
        ],
        cost_estimate=cost(1_000_000, 10_000),
        name="attend_forward",
    )(place, *pieces, *weights)


def attend_backward_kernel(
    place, g0, g1, g2, g3, qkv, w0, w1, w2, w3, w4, w5, w6, w7, w8,
    keep, send, rows, qkv_grad, w_out, weights, arrived,
):
    pieces = [p.at[:, 1920:] for p in (w0, w1, w2, w3, w4, w5, w6, w7, w8)]
    for copy in start_weights(place, pieces, weights, arrived):
        copy.wait()
    put_w_out(weights, w_out)
    for k, piece in enumerate((g0, g1, g2, g3)):
        rows[k * 128 : (k + 1) * 128, :] = piece[...]
    context_grad = product_right(rows[...], w_out[...])
    mask = patch_mask()
    for b in range(1):
        units = range(16 * b, 16 * (b + 1))
        probs = patch_probs(qkv, units, mask)
        grads = [bf(unit(context_grad, 0, i)) for i in units]
        probs_grad = stacked(
            [product_right(g, unit(qkv, 2, i)) for g, i in zip(grads, units, strict=True)]
        )
        mean = jnp.sum(probs * probs_grad, axis=2, keepdims=True)
        scores_grad = probs * (probs_grad - mean) * HDIM ** (-0.5)
        for n, i in enumerate(units):
            rows_at = slice((i // 4) * 128, (i // 4 + 1) * 128)
            for k, part in enumerate(
                (
                    product(bf(scores_grad[n]), unit(qkv, 1, i)),
                    product(bf(scores_grad[n].T), unit(qkv, 0, i)),
                    product(bf(probs[n].T), grads[n]),
                )
            ):
                start = k * 256 + (i % 4) * HDIM
                qkv_grad[rows_at, start : start + HDIM] = bf(part)
    split_blocks(product_right(qkv_grad[...], weights[:, :768]), keep, send)


def attend_backward(place, pieces, qkv, weights):
    low = jnp.bfloat16
    shapes = [(2, 128, 1024), (2, 128, 1024), (ROWS, 1024), (ROWS, 768)]
    return pl.pallas_call(
        attend_backward_kernel,
        grid=(1,),
        in_specs=[scalars()]
        + [whole(a.shape) for a in (*pieces, qkv)]
        + [pl.BlockSpec(memory_space=pl.ANY)] * 9,
        out_specs=[whole(s) for s in shapes],
        out_shape=[jax.ShapeDtypeStruct(s, low) for s in shapes],
        compiler_params=pltpu.CompilerParams(vmem_limit_bytes=VMEM_BYTES),
        scratch_shapes=[
            pltpu.VMEM((256, 1024), low),
            pltpu.VMEM((1024, 1024), low),
            pltpu.SemaphoreType.DMA((9,)),
        ],
        cost_estimate=cost(1_000_000, 10_000),
        name="attend_backward",
    )(place, *pieces, qkv, *weights)


def feed_copies(place, pieces, weights, arrived, j):
    chunk = pl.multiple_of(j * 512, 512)
    copies = []
    for n, start in enumerate((chunk, pl.multiple_of(1024 + chunk, 512))):
        at = pl.ds(start, 512)
        copies += weight_copies(
            place, [p.at[:, at] for p in pieces], weights.at[:, at], arrived.at[2 * j + n]
        )
    return copies


def down_copies(place, pieces, weights, arrived):
    return weight_copies(
        place, [p.at[:, 2048:] for p in pieces], weights.at[:, 2048:], arrived.at[4]
    )


def feed_kernel(
    place, x0, x1, x2, x3, out_grad, w0, w1, w2, w3, w4, w5, w6, w7, w8,
    keep, send, out_keep, out_send, rows, hidden, gate_grad, up_grad,
    weights, total, total_out, arrived,
):
    j = pl.program_id(0)
    pieces = (w0, w1, w2, w3, w4, w5, w6, w7, w8)

    @pl.when(j == 0)
    def _():
        for copy in feed_copies(place, pieces, weights, arrived, 0):
            copy.start()
        for copy in down_copies(place, pieces, weights, arrived):
            copy.start()
        for k in range(1, 2):
            for copy in feed_copies(place, pieces, weights, arrived, k):
                copy.start()
        for k, piece in enumerate((x0, x1, x2, x3)):
            rows[k * 128 : (k + 1) * 128, :] = piece[...]
        total[...] = jnp.zeros_like(total)
        total_out[...] = jnp.zeros_like(total_out)

    for copy in feed_copies(place, pieces, weights, arrived, j):
        copy.wait()

    @pl.when(j == 0)
    def _():
        for copy in down_copies(place, pieces, weights, arrived):
            copy.wait()

    chunk = pl.multiple_of(j * 512, 512)
    w_gate = weights[:, pl.ds(chunk, 512)]
    w_up = weights[:, pl.ds(pl.multiple_of(1024 + chunk, 512), 512)]
    w_down = weights[pl.ds(chunk, 512), 2048:]
    gate, slope = silu_parts(product(rows[...], w_gate))
    lift = product(rows[...], w_up)
    units = bf(gate * lift)
    hidden[...] = units
    units_grad = product_right(out_grad[...], w_down)
    gate_low = bf(units_grad * lift * slope)
    up_low = bf(units_grad * gate)
    gate_grad[...] = gate_low
    up_grad[...] = up_low
    total[...] += product_right(gate_low, w_gate) + product_right(up_low, w_up)
    total_out[...] += product(units, w_down)

    @pl.when(j == pl.num_programs(0) - 1)
    def _():
        split_blocks(total, keep, send)
        split_blocks(total_out, out_keep, out_send)


def feed(place, pieces, out_grad, weights):
    low = jnp.bfloat16
    pair = (2, 128, 1024)
    column = pl.BlockSpec((ROWS, 512), lambda j: (0, j))
    return pl.pallas_call(
        feed_kernel,
        grid=(2,),
        in_specs=[scalars()]
        + [whole(a.shape) for a in (*pieces, out_grad)]
        + [pl.BlockSpec(memory_space=pl.ANY)] * 9,
        out_specs=[whole(pair)] * 4 + [whole((ROWS, 1024)), column, column, column],
        out_shape=[jax.ShapeDtypeStruct(pair, low)] * 4
        + [jax.ShapeDtypeStruct((ROWS, 1024), low)] * 4,
        scratch_shapes=[
            pltpu.VMEM((1024, 3072), low),
            pltpu.VMEM((ROWS, 1024), jnp.float32),
            pltpu.VMEM((ROWS, 1024), jnp.float32),
            pltpu.SemaphoreType.DMA((5, 9)),
        ],
        compiler_params=kernel_params(),
        cost_estimate=cost(1_000_000, 10_000),
        name="feed",
    )(place, *pieces, out_grad, *weights)


def put_by_target(place, values, out):
    for s in range(8):
        out[place[12 + s], :, : values.shape[1]] = values[s * 128 : (s + 1) * 128, :]


def feed_grads_kernel(place, rows, gate_grad, up_grad, hidden, out_grad, grads, turned):
    j = pl.program_id(0)

    @pl.when(j == 0)
    def _():
        turned[...] = rows[...].T

    @pl.when(j == 2)
    def _():
        turned[...] = hidden[...].T

    for first, right in enumerate((gate_grad, up_grad, out_grad)):

        @pl.when(j == first)
        def _():
            put_by_target(place, bf(product(turned[...], right[...])), grads)


def feed_grads(place, rows, gate_grad, up_grad, hidden, out_grad):
    low = jnp.bfloat16
    return pl.pallas_call(
        feed_grads_kernel,
        grid=(3,),
        in_specs=[scalars()] + [whole((ROWS, 1024))] * 5,
        out_specs=pl.BlockSpec((8, 128, 1024), lambda j: (0, 0, j)),
        out_shape=jax.ShapeDtypeStruct((8, 128, 3072), low),
        scratch_shapes=[pltpu.VMEM((1024, ROWS), low)],
        compiler_params=kernel_params(),
        cost_estimate=cost(1_000_000, 10_000),
        name="feed_grads",
    )(place, rows, gate_grad, up_grad, hidden, out_grad)


def attend_grads_kernel(place, rows, qkv_grad, context, middle_grad, grads):
    put_by_target(place, bf(product(rows[...].T, qkv_grad[...])), grads)
    out_grad = bf(product(context[...].T, middle_grad[...]))
    for s in range(8):
        for q in range(4):
            grads[place[12 + s], q * 32 : (q + 1) * 32, 768:] = out_grad[
                s * 32 : (s + 1) * 32, q * 256 : (q + 1) * 256
            ]


def attend_grads(place, rows, qkv_grad, context, middle_grad):
    operands = (rows, qkv_grad, context, middle_grad)
    return pl.pallas_call(
        attend_grads_kernel,
        grid=(1,),
        in_specs=[scalars()] + [whole(a.shape) for a in operands],
        out_specs=whole((8, 128, 1024)),
        out_shape=jax.ShapeDtypeStruct((8, 128, 1024), jnp.bfloat16),
        compiler_params=kernel_params(),
        cost_estimate=cost(1_000_000, 10_000),
        name="attend_grads",
    )(place, *operands)


def placed_kernel(turned, place, p0, p1, p2, p3, weights, rows, result):
    put_pieces(place, (p0, p1, p2, p3), rows)
    left = rows[:, :1024]
    result[...] = bf(product_right(left, weights[...]) if turned else product(left, weights[...]))


def placed_product(place, pieces, weights, turned):
    width = pieces[0].shape[1]
    low = jnp.bfloat16
    return pl.pallas_call(
        partial(placed_kernel, turned),
        in_specs=[scalars()] + [whole(a.shape) for a in (*pieces, weights)],
        out_specs=[whole((ROWS, width)), whole((ROWS, 256))],
        grid=(1,),
        out_shape=[
            jax.ShapeDtypeStruct((ROWS, width), low),
            jax.ShapeDtypeStruct((ROWS, 256), low),
        ],
        compiler_params=kernel_params(),
        cost_estimate=cost(1_000_000, 10_000),
        name="placed_product",
    )(place, *pieces, weights)


PAIR_C = [(i, i ^ 1) for i in range(4)]
PAIR_Y = [(i, i ^ 2) for i in range(4)]


def swap_c(shard):
    return lax.ppermute(shard, "mp", PAIR_C)


def swap_y(shard):
    return lax.ppermute(shard, "mp", PAIR_Y)


def swap_seq(shard, by):
    return lax.ppermute(shard, "seq", [(i, i ^ by) for i in range(8)])


RING = (0, 2, 4, 6, 7, 5, 3, 1)
UP = [(RING[i], RING[(i + 1) % 8]) for i in range(8)]
DOWN = [(b, a) for a, b in UP]
REACH = (0, -1, 1, -2, 2, -3, 3, 4, 4)


def swap_up(shard):
    return lax.ppermute(shard, "seq", UP)


def swap_down(shard):
    return lax.ppermute(shard, "seq", DOWN)


def chosen(index, values):
    places = jnp.arange(len(values), dtype=jnp.int32)
    return jnp.sum(jnp.where(index[..., None] == places, jnp.array(values, jnp.int32), 0), axis=-1)


def places_of(c, y, s):
    at = [RING.index(k) for k in range(8)]
    own = chosen(s, at)
    owners = chosen((own + jnp.array(REACH, jnp.int32) + 8) % 8, RING)
    ahead = (jnp.array(at, jnp.int32) - own + 8) % 8
    return jnp.concatenate([jnp.stack([c, y, s]), owners, ahead]).astype(jnp.int32)


class RingGather:
    def __init__(self, shard):
        self.pieces = [shard]
        self.flying = [shard, shard]

    def step(self):
        ahead, behind = self.flying
        if len(self.pieces) == 7:
            ahead, behind = (ahead[:64], behind[64:])
        self.flying = [swap_up(ahead), swap_down(behind)]

    def landed(self, value):
        value, self.flying = lax.optimization_barrier((value, self.flying))
        self.pieces = self.pieces + self.flying
        return value


    def held(self, value):
        value, shard = lax.optimization_barrier((value, self.pieces[0]))
        self.pieces, self.flying = ([shard], [shard, shard])
        return value


class RingSum:
    def __init__(self, blocks):
        self.blocks = blocks
        self.flying = None
        self.count = 0

    def step(self):
        if self.count == 0:
            far = self.blocks[4]
            sent = [far[:64], far[64:]]
        elif self.count == 1:
            ahead, behind = (self.blocks[3], self.blocks[5])
            sent = [
                jnp.concatenate([bf(up(ahead[:64]) + up(self.flying[0])), ahead[64:]]),
                jnp.concatenate([behind[:64], bf(up(behind[64:]) + up(self.flying[1]))]),
            ]
        else:
            sent = [
                bf(up(self.blocks[k]) + up(part))
                for k, part in zip((4 - self.count, 4 + self.count), self.flying, strict=True)
            ]
        self.flying = [swap_up(sent[0]), swap_down(sent[1])]
        self.count += 1

    def landed(self, value):
        value, self.flying = lax.optimization_barrier((value, self.flying))
        return value

    def held(self, value):
        value, self.blocks, self.flying = lax.optimization_barrier(
            (value, self.blocks, self.flying)
        )
        return value

    def result(self):
        return up(self.blocks[0]) + up(self.flying[0]) + up(self.flying[1])


def pick(stacked, index):
    return lax.dynamic_index_in_dim(stacked, index, 0, keepdims=False)


def over_seq(rows):
    return lax.all_to_all(rows, "seq", 0, 0, tiled=True)


def over_all(blocks):
    return lax.all_to_all(blocks, ("seq", "mp"), 0, 0, tiled=True)


def from_all_seq(rows):
    return over_seq(jnp.broadcast_to(rows[None], (8, *rows.shape)))


def sum_rows(send, keep, y):
    total = up(keep) + up(swap_c(send))
    parts = total.reshape(2, 128, -1)
    return pick(parts, y) + up(swap_y(bf(pick(parts, 1 - y))))


def gather_rows(rows):
    far = swap_y(rows)
    return [rows, far, swap_c(rows), swap_c(far)]


def alike(parts):
    return (parts[0] + parts[2]) + (parts[1] + parts[3])


def sum_group(partial, c, y):
    halves = bf(partial).reshape(2, HALF, -1)
    return bf(sum_rows(pick(halves, 1 - c), pick(halves, c), y))


def sum_seq(rows):
    return jnp.sum(up(over_seq(rows.reshape(8, 16, -1))), axis=0)


def gather_bytes(rows):
    far = swap_y(rows)
    return [rows, swap_c(rows), far, swap_c(far)]


def sum_bytes(keep, send):
    got = up(keep) + up(swap_c(send))
    return got[0] + up(swap_y(bf(got[1])))


def placed(parts, m):
    blocks = jnp.stack(parts)
    return jnp.concatenate([pick(blocks, m ^ k) for k in range(4)], axis=0)


def to_bytes(columns):
    got = over_all(columns.reshape(32, 16, 256))
    return got.reshape(8, 4, 16, 256).transpose(2, 1, 0, 3).reshape(128, E)


def to_columns(rows):
    sent = rows.reshape(16, 4, 8, 256).transpose(2, 1, 0, 3).reshape(32, 16, 256)
    return over_all(sent).reshape(ROWS, 256)


def split_plan(
    byte_input,
    seq_lengths,
    cotangent,
    gain_global,
    patch_in,
    mixer_gate,
    mixer_input,
    mixer_state,
    mixer_step,
    conv_input,
    conv_state,
    step_bias,
    decay_log,
    skip_gain,
    gain_mixer,
    mixer_out,
    patch_out,
    gain_attend,
    attend_query,
    attend_key,
    attend_value,
    attend_out,
    gain_feed,
    feed_gate,
    feed_up,
    feed_down,
):
    s, m = (lax.axis_index("seq"), lax.axis_index("mp"))
    y, c = (m // 2, m % 2)
    place = places_of(c, y, s)
    f32 = jnp.float32

    out_halves = mixer_out.reshape(64, 2, 512).transpose(1, 0, 2).reshape(128, 512)
    out_quarters = attend_out.reshape(32, 4, 256).transpose(1, 0, 2).reshape(128, 256)
    w_mixer = RingGather(jnp.concatenate(
        [
            mixer_gate,
            mixer_input,
            mixer_state,
            mixer_step,
            jnp.zeros((128, 120), jnp.bfloat16),
            out_halves,
            attend_query,
            attend_key,
            attend_value,
            out_quarters,
        ],
        axis=1,
    ))
    table = jnp.concatenate([conv_input, gain_mixer[None], jnp.zeros((3, 512), f32)], axis=0)
    state_taps = jnp.concatenate([conv_state, jnp.zeros((4, 256), f32)], axis=0)
    params = jnp.pad(jnp.stack([step_bias, decay_log, skip_gain]), ((0, 5), (0, 120)))

    own_slots = lax.dynamic_slice_in_dim(byte_input.reshape(64, PATCH, E), 2 * m, 2, 1)
    sent = w_mixer.held(own_slots.reshape(64, 8, 256).transpose(1, 0, 2))
    columns_in = over_seq(sent).reshape(ROWS, 256)
    w_mixer.step()
    w_patch = patch_out.reshape(128, 8, 256).transpose(1, 0, 2)
    w_feed = jnp.concatenate([feed_gate, feed_up, feed_down], axis=1)
    columns_in, place, table, state_taps, params, w_patch, w_feed = w_mixer.landed(
        (columns_in, place, table, state_taps, params, w_patch, w_feed)
    )
    w_feed = RingGather(w_feed)
    w_mixer.step()
    rows = sum_group(product(columns_in, patch_in), c, y)
    hidden = w_mixer.landed(bf(sum_seq(rows)))
    w_mixer.step()
    hidden = up(w_mixer.landed(from_all_seq(hidden).reshape(128, 1024)))
    w_mixer.step()
    normed_parts = w_mixer.landed(gather_rows(bf(rms_scale(hidden, gain_global))))
    normed_parts = w_feed.held(normed_parts)
    w_feed.step()

    normed_parts, w_patch = lax.optimization_barrier((normed_parts, w_patch))
    send, keep, own_normed, *pre, inside, scaled = mixer_forward(
        place, seq_lengths, normed_parts, w_mixer.pieces, table, state_taps, params
    )
    send, w_patch = lax.optimization_barrier((send, over_seq(w_patch)))
    w_patch = w_patch.reshape(1024, 256)
    sums = w_feed.landed(sum_rows(send, keep, y))
    w_feed.step()
    unscaled, root = (sums[:, :1024], lax.rsqrt(sums[:, 1024:1025] / DI + EPS))
    merged_parts = gather_rows(bf(hidden + root * unscaled))
    merged_low, slots = placed_product(place, merged_parts, w_patch, False)
    cot_blocks = cotangent.reshape(4, 128, E)
    out_low = jnp.concatenate([bf(pick(cot_blocks, m ^ k)) for k in range(4)], axis=0)
    slots, out_low = w_feed.landed((to_bytes(slots), out_low))
    w_feed.step()
    residual = up(lax.dynamic_slice_in_dim(byte_input, m * 128, 128, 0)) + slots

    attend_parts = gather_bytes(bf(rms_scale(residual, gain_attend)))
    keep, send, attend_in, qkv, context = attend_forward(place, attend_parts, w_mixer.pieces)
    send = w_feed.landed(send)
    w_feed.step()
    middle = residual + sum_bytes(keep, send)
    feed_parts = w_feed.landed(gather_bytes(bf(rms_scale(middle, gain_feed))))
    cot_rows = pick(cot_blocks, m)
    keep, send, out_keep, out_send, feed_in, hidden_units, grad_gate, grad_up = feed(
        place, feed_parts, out_low, w_feed.pieces
    )
    grads = feed_grads(place, feed_in, grad_gate, grad_up, hidden_units, out_low)
    grad_feed_in, grads = lax.optimization_barrier((sum_bytes(keep, send), grads))
    feed_sums = RingSum(grads)
    feed_sums.step()
    grad_middle_part, gain_feed_part = rms_back(middle, gain_feed, grad_feed_in)
    grad_middle = cot_rows + grad_middle_part
    keep, send, middle_low, grad_qkv = attend_backward(
        place, gather_bytes(bf(grad_middle)), qkv, w_mixer.pieces
    )
    send = feed_sums.landed(send)
    feed_sums.step()
    grads = attend_grads(place, attend_in, grad_qkv, context, middle_low)
    grad_attend_in, grads = lax.optimization_barrier((sum_bytes(keep, send), grads))
    attend_sums = RingSum(grads)
    grad_residual_part, gain_attend_part = rms_back(residual, gain_attend, grad_attend_in)
    grad_residual = grad_middle + grad_residual_part

    slot_grad, out_send = lax.optimization_barrier(
        (to_columns(bf(grad_residual)), swap_c(out_send))
    )
    slot_grad = feed_sums.landed(slot_grad)
    feed_sums.step()
    grad_patch_out = bf(product_left(merged_low, slot_grad)).reshape(8, 128, 256)
    rows = sum_group(product_right(slot_grad, w_patch), c, y)
    out_parts = up(out_keep) + up(out_send)
    rows, out_far = lax.optimization_barrier((rows, bf(out_parts[1])))
    merged_rows, out_far = lax.optimization_barrier((sum_seq(rows), swap_y(out_far)))
    out_rows = bf(middle + out_parts[0] + up(out_far))
    merged_rows = feed_sums.landed(merged_rows)
    gains = jnp.stack([gain_feed_part, gain_attend_part])
    got = from_all_seq(
        bf(jnp.concatenate([merged_rows, gains, jnp.zeros((6, 1024), f32)], axis=0))
    )
    got, out_far, out_near = lax.optimization_barrier((got, swap_y(out_rows), swap_c(out_rows)))
    got = feed_sums.held(got)
    feed_sums.step()
    grad_merged = up(got[:, :16].reshape(128, 1024))
    gains = jnp.sum(up(got[:, 16:18]), axis=0)
    kappa = jnp.sum(grad_merged * unscaled, axis=1, keepdims=True) * root**3 / DI
    rows = jnp.concatenate([grad_merged * root, jnp.broadcast_to(kappa, (128, 128))], axis=1)
    merged_parts = gather_rows(
        bf(jnp.concatenate([rows, jnp.pad(gains, ((0, 6), (0, 128)))], axis=0))
    )
    merged_parts, grad_patch_out = attend_sums.held((merged_parts, grad_patch_out))
    attend_sums.step()
    out_both = swap_c(out_far)
    grad_patch_out = over_seq(grad_patch_out)
    gains = alike([up(part[128:130, :1024]) for part in merged_parts])
    send, keep, grads, merged_grad, table_grad, state_taps_grad, params_grad = mixer_backward(
        place,
        seq_lengths,
        merged_parts,
        w_mixer.pieces,
        table,
        state_taps,
        params,
        pre,
        inside,
    )
    send, grad_patch_out, out_both = feed_sums.landed((send, grad_patch_out, out_both))
    send = attend_sums.landed(send)
    attend_sums.step()
    feed_sums = feed_sums.result()
    byte_output = placed([out_rows, out_near, out_far, out_both], m)
    sums = sum_rows(send, keep, y)
    grad_hidden_part, gain_global_part = rms_back(hidden, gain_global, sums[:, :1024])
    rows = jnp.concatenate([grad_merged + grad_hidden_part, sums[:, 1024:]], axis=1)
    small = jnp.stack([gain_global_part, state_taps_grad[:4].reshape(1024)])
    hidden_parts = gather_rows(
        bf(jnp.concatenate([rows, jnp.pad(small, ((0, 6), (0, 256)))], axis=0))
    )
    hidden_parts = attend_sums.landed(hidden_parts)
    attend_sums.step()
    small = alike([up(part[128:130, :1024]) for part in hidden_parts])
    hidden_rows, back = placed_product(place, hidden_parts, patch_in, True)
    hidden_grad = hidden_rows[:, :1024]
    back, grad_patch_in, grad_mixer_state = lax.optimization_barrier(
        (
            to_bytes(back),
            product_left(columns_in, hidden_grad),
            product_left(own_normed, hidden_rows[:, 1024:]),
        )
    )
    grad_rows = attend_sums.landed(bf(grad_residual + back))
    attend_sums.step()
    grad_input = placed(gather_bytes(grad_rows), m)
    attend_sums = attend_sums.result()

    first_grad = product_left(own_normed, grads)
    own_scaled = lax.dynamic_slice_in_dim(scaled, s * HDIM, HDIM, 1)
    return (
        byte_output,
        grad_input,
        small[0],
        grad_patch_in,
        first_grad[:, :512],
        first_grad[:, 512:1024],
        grad_mixer_state,
        first_grad[:, 1280:1288],
        table_grad[:4],
        small[1].reshape(4, 256),
        params_grad[0, :8],
        params_grad[1, :8],
        params_grad[2, :8],
        table_grad[4],
        product_left(own_scaled, merged_grad),
        grad_patch_out.transpose(1, 0, 2).reshape(128, 2048).astype(f32),
        gains[1],
        attend_sums[:, :256],
        attend_sums[:, 256:512],
        attend_sums[:, 512:768],
        attend_sums[:, 768:].reshape(4, 32, 256).transpose(1, 0, 2).reshape(32, 1024),
        gains[0],
        feed_sums[:, :1024],
        feed_sums[:, 1024:2048],
        feed_sums[:, 2048:],
    )


def solution(mesh):
    in_specs = (
        P("seq", None),
        P(),
        P("seq", None),
        P(),
        P(("mp", "seq"), None),
        P("seq", "mp"),
        P("seq", "mp"),
        P("seq", None),
        P("seq", "mp"),
        P(None, "mp"),
        P(),
        P("mp"),
        P("mp"),
        P("mp"),
        P("mp"),
        P(("mp", "seq"), None),
        P("seq", "mp"),
        P(),
        P("seq", "mp"),
        P("seq", "mp"),
        P("seq", "mp"),
        P(("mp", "seq"), None),
        P(),
        P("seq", "mp"),
        P("seq", "mp"),
        P(("mp", "seq"), None),
    )
    out_specs = (
        P("seq", None),
        P("seq", None),
        P(),
        P(("mp", "seq"), None),
        P("seq", "mp"),
        P("seq", "mp"),
        P("seq", None),
        P("seq", "mp"),
        P(None, "mp"),
        P(),
        P("mp"),
        P("mp"),
        P("mp"),
        P("mp"),
        P(("mp", "seq"), None),
        P("seq", "mp"),
        P(),
        P("seq", "mp"),
        P("seq", "mp"),
        P("seq", "mp"),
        P(("mp", "seq"), None),
        P(),
        P("seq", "mp"),
        P("seq", "mp"),
        P(("mp", "seq"), None),
    )
    plan = split_plan if (mesh.shape["seq"], mesh.shape["mp"]) == (8, 4) else gathered_plan
    return jax.shard_map(plan, mesh=mesh, in_specs=in_specs, out_specs=out_specs, check_vma=False)
```
